32 devices in a mesh: ctx: 8 (over y, x, core), head: 4 (over z).
Axes of the slice: x: 2, y: 2, z: 4, core: 2. Of those that a mesh axis runs over, the one named last changes fastest.
Arguments:
- queries: bfloat16 [4096, 4096], P('ctx', 'head'), may hold values from -6 to 6
- key_rows: bfloat16 [4096, 4096], P('ctx', 'head'), may hold values from -6 to 6
- value_rows: bfloat16 [4096, 4096], P('ctx', 'head'), may hold values from -6 to 6
- doc_lengths: int32 [4], replicated, may hold values from 1 to 2048, 4096 in all
- out_weight: bfloat16 [4096, 4096], P('head'), may hold values from -0.09375 to 0.09375
- out_grad: bfloat16 [4096, 4096], P('ctx', 'head'), may hold values from -6 to 6
Outputs:
- mixed: bfloat16 [4096, 4096], P('ctx', 'head')
- query_grad: bfloat16 [4096, 4096], P('ctx', 'head')
- key_grad: bfloat16 [4096, 4096], P('ctx', 'head')
- value_grad: bfloat16 [4096, 4096], P('ctx', 'head')
The draws below stay inside these ranges and needn't reach their ends.
Inputs may be any that keep to these rules, and one draw needn't show every extreme that they name: `doc_lengths`: the lengths of the 4 documents packed in order from position 0; they sum to 4096 and the longest is exactly 2048.
All inputs are finite; a program needn't handle non-finite values.
Results may differ from the reference program's by a relative error of at most 0.015.
Values may be sent and summed in bfloat16 or wider, within the bound.
No kernel may reach another device: no remote copies, remote signals or barrier semaphores. Data moves between devices by JAX's collectives and lax.ppermute only.
A program may use at most 128 MiB of HBM per device.

```python
import math
import jax
import jax.numpy as jnp
import numpy as np
from jax import lax

D = 4096
HEADS = 32
DH = 128
TOK_DEV = 512
DOCS = 4
SEQ = 4096
LONGEST = 2048
FEATURES = 4096
N_CTX = 8
N_HEAD = 4


def block_scale(rng, extent, pieces, low, largest):
    factor_of = 1.0
    for position, parts in pieces:
        steps = jax.random.uniform(jax.random.fold_in(jax.random.fold_in(rng, 6), position), (parts,), jnp.float32, low / len(pieces), largest / len(pieces))
        factor_of = factor_of * jnp.repeat(jnp.exp(steps), extent[position] // parts).reshape((-1,) + (1,) * (len(extent) - 1 - position))
    return factor_of


def split_up(amount, total, limit, slope):
    portions = [(1 << 20) // math.isqrt(standing ** slope) + 1 for standing in range(2, amount + 1)]
    spare, counts = total - limit - (amount - 1), [1] * (amount - 1)
    while spare > 0:
        candidates = [i for i in range(amount - 1) if counts[i] < limit]
        mass, left = sum([portions[i] for i in candidates]), spare
        for i in candidates:
            extra = min(limit - counts[i], max(1, left * portions[i] // mass), spare)
            counts[i] = counts[i] + extra
            spare = spare - extra
    return np.array([limit] + counts)


def uneven_parts(stream_key, count, total, bound, lean):
    if count == 2:
        one = jax.random.randint(stream_key, (), max(1, total - bound), min(bound, total - 1) + 1)
        return jnp.stack([one, total - one])
    sizes = jnp.asarray(split_up(count, total, bound, lean), jnp.int32)
    couples = (count - 1) // 2
    source_of, taker = sizes[1:1 + 2 * couples:2], sizes[2:2 + 2 * couples:2]
    margin = jnp.minimum(source_of - 1, bound - taker)
    moved = jax.random.randint(jax.random.fold_in(stream_key, 1), (couples,), 0, 1 << 20) % (margin + 1)
    sizes = sizes.at[1:1 + 2 * couples:2].set(source_of - moved).at[2:2 + 2 * couples:2].set(taker + moved)
    return sizes[jax.random.permutation(jax.random.fold_in(stream_key, 2), count)]


def normal_values(stream_key, extent, scale, most, cuts=(), held_as=jnp.bfloat16):
    drawn = jax.random.normal(stream_key, extent, jnp.float32) * scale
    if len(cuts) > 0:
        drawn = block_scale(stream_key, extent, cuts, -0.22, 0.18) * drawn
    return jnp.clip(drawn, min=-most, max=most).astype(held_as)


def setup_inputs(seed: int = 0) -> dict:
    seeds = jax.random.split(jax.random.key(seed), 7)
    return {
        "queries": normal_values(seeds[0], (SEQ, FEATURES), 1.0, 6.0, ((0, 8), (1, 4))),
        "key_rows": normal_values(seeds[1], (SEQ, FEATURES), 1.0, 6.0, ((0, 8), (1, 4))),
        "value_rows": normal_values(seeds[2], (SEQ, FEATURES), 1.0, 6.0, ((0, 8), (1, 4))),
        "doc_lengths": uneven_parts(seeds[3], DOCS, SEQ, LONGEST, 2).astype(jnp.int32),
        "out_weight": normal_values(seeds[4], (FEATURES, D), FEATURES ** -0.5, 0.09375, ((0, 4),)),
        "out_grad": normal_values(seeds[5], (SEQ, D), 1.0, 6.0, ((0, 8), (1, 4))),
    }


epsilon = 1e-06

def doc_numbers(doc_lengths, positions):
    opening = jnp.cumsum(doc_lengths) - doc_lengths
    return lax.optimization_barrier(jnp.sum((opening[None, :] <= positions[:, None]).astype(jnp.int32), axis=1)) - 1

def split_heads(matrix):
    return matrix.reshape(N_CTX, TOK_DEV, HEADS, DH)

def reference(queries, key_rows, value_rows, doc_lengths, out_weight, out_grad):
    positions = jnp.arange(SEQ, dtype=jnp.int32)
    doc_all = doc_numbers(doc_lengths, positions).reshape(N_CTX, TOK_DEV)
    doc_last = doc_all[:, -1]
    doc_before = jnp.concatenate([jnp.full((1,), -1, jnp.int32), doc_last[:-1]])
    carry_in = (doc_all == doc_before[:, None]).astype(jnp.float32)
    carry_out = (doc_all == doc_last[:, None]).astype(jnp.float32)
    resets = 1.0 - carry_in[:, -1]
    query_blk = split_heads(queries)
    key_blk = split_heads(key_rows)
    value_blk = split_heads(value_rows)
    grad_blk = out_grad.reshape(N_CTX, TOK_DEV, D)
    lower_tri = jnp.arange(TOK_DEV)[None, :] <= jnp.arange(TOK_DEV)[:, None]
    group_width = FEATURES // N_HEAD

    def masks(doc_ids):
        return lower_tri & (doc_ids[None, :] == doc_ids[:, None])

    def local_state(inputs_blk):
        key_here, value_here, keep_out = inputs_blk
        kept = key_here * keep_out.astype(jnp.bfloat16)[:, None, None]
        return jnp.einsum('shd,she->hde', kept.astype(jnp.float32), value_here.astype(jnp.float32))
    local_sums = lax.map(local_state, (key_blk, value_blk, carry_out))

    def chain_step(state_now, inputs_blk):
        reset_flag, local_sum = inputs_blk
        return (local_sum + (1.0 - reset_flag) * state_now, state_now)
    zero_state = jnp.zeros((HEADS, DH, DH), jnp.float32)
    _, entering = lax.scan(chain_step, zero_state, (resets, local_sums))

    def masked_scores(query_here, key_here, doc_ids):
        scores = jnp.einsum('thd,shd->hts', query_here.astype(jnp.float32), key_here.astype(jnp.float32))
        return jnp.where(masks(doc_ids)[None], scores, 0.0).astype(jnp.bfloat16)

    def forward_block(inputs_blk):
        query_here, key_here, value_here, doc_ids, keep_in, enter_state, grad_here = inputs_blk
        score_mask = masked_scores(query_here, key_here, doc_ids)
        intra_part = jnp.einsum('hts,shd->thd', score_mask.astype(jnp.float32), value_here.astype(jnp.float32))
        entering_b = enter_state.astype(jnp.bfloat16)
        inter_part = jnp.einsum('thd,hde->the', query_here.astype(jnp.float32), entering_b.astype(jnp.float32))
        attended = intra_part + inter_part * keep_in[:, None, None]
        root_mean = jnp.sqrt(lax.optimization_barrier(jnp.mean(attended * attended, axis=-1, keepdims=True)) + epsilon)
        normed = attended / root_mean
        normed_b = normed.astype(jnp.bfloat16).reshape(TOK_DEV, FEATURES)
        mixed_here = jnp.zeros((TOK_DEV, D), jnp.float32)
        for member in range(N_HEAD):
            lower = member * group_width
            partial_out = jnp.dot(normed_b[:, lower:lower + group_width], out_weight[lower:lower + group_width], preferred_element_type=jnp.float32)
            rounded = lax.optimization_barrier(partial_out.astype(jnp.bfloat16))
            mixed_here = mixed_here + rounded.astype(jnp.float32)
        normed_grad = jnp.dot(grad_here, out_weight.T, preferred_element_type=jnp.float32).reshape(TOK_DEV, HEADS, DH)
        projection = lax.optimization_barrier(jnp.mean(normed_grad * normed, axis=-1, keepdims=True))
        attended_grad = ((normed_grad - normed * projection) / root_mean).astype(jnp.bfloat16)
        kept_queries = query_here * keep_in.astype(jnp.bfloat16)[:, None, None]
        local_grad = jnp.einsum('thd,the->hde', kept_queries.astype(jnp.float32), attended_grad.astype(jnp.float32))
        return (mixed_here.astype(jnp.bfloat16), attended_grad, local_grad)
    mixed, attended_grads, local_grads = lax.map(forward_block, (query_blk, key_blk, value_blk, doc_all, carry_in, entering, grad_blk))
    _, leaving = lax.scan(chain_step, zero_state, (resets, local_grads), reverse=True)

    def grad_block(inputs_blk):
        query_here, key_here, value_here, doc_ids, keep_in, keep_out, enter_state, leave_state, attended_grad = inputs_blk
        score_mask = masked_scores(query_here, key_here, doc_ids)
        raw_grad = jnp.einsum('the,she->hts', attended_grad.astype(jnp.float32), value_here.astype(jnp.float32))
        grad_scores = jnp.where(masks(doc_ids)[None], raw_grad, 0.0).astype(jnp.bfloat16)
        entering_b = enter_state.astype(jnp.bfloat16).astype(jnp.float32)
        leaving_b = leave_state.astype(jnp.bfloat16).astype(jnp.float32)
        query_grad = jnp.einsum('hts,shd->thd', grad_scores.astype(jnp.float32), key_here.astype(jnp.float32))
        query_grad = query_grad + keep_in[:, None, None] * jnp.einsum('the,hde->thd', attended_grad.astype(jnp.float32), entering_b)
        key_grad = jnp.einsum('hts,thd->shd', grad_scores.astype(jnp.float32), query_here.astype(jnp.float32))
        key_grad = key_grad + keep_out[:, None, None] * jnp.einsum('she,hde->shd', value_here.astype(jnp.float32), leaving_b)
        value_grad = jnp.einsum('hts,the->she', score_mask.astype(jnp.float32), attended_grad.astype(jnp.float32))
        value_grad = value_grad + keep_out[:, None, None] * jnp.einsum('shd,hde->she', key_here.astype(jnp.float32), leaving_b)
        return (query_grad.astype(jnp.bfloat16), key_grad.astype(jnp.bfloat16), value_grad.astype(jnp.bfloat16))
    query_grad, key_grad, value_grad = lax.map(grad_block, (query_blk, key_blk, value_blk, doc_all, carry_in, carry_out, entering, leaving, attended_grads))
    return (mixed.reshape(SEQ, D), query_grad.reshape(SEQ, FEATURES), key_grad.reshape(SEQ, FEATURES), value_grad.reshape(SEQ, FEATURES))
```

```python
import functools

import jax
import jax.numpy as jnp
from jax import lax
from jax.experimental import pallas as pl
from jax.experimental.pallas import tpu as pltpu
from jax.sharding import PartitionSpec as P

DH = 128
EPS = 1e-06
F32 = jnp.float32
BF16 = jnp.bfloat16
VMEM_LIMIT = 48 * 1024 * 1024

I_BLK, I_HALF, I_DOC = 0, 1, 2


def params(n_axes=1):
    return pltpu.CompilerParams(
        vmem_limit_bytes=VMEM_LIMIT, dimension_semantics=("arbitrary",) * n_axes
    )


def cost(flops, nbytes):
    return pl.CostEstimate(flops=int(flops), bytes_accessed=int(nbytes), transcendentals=0)


def call(body, name, grid, n_scalar, in_specs, out_specs, out_shape, scratch=(), flops=0, nbytes=0):
    return pl.pallas_call(
        body,
        name=name,
        grid_spec=pltpu.PrefetchScalarGridSpec(
            num_scalar_prefetch=n_scalar,
            grid=grid,
            in_specs=in_specs,
            out_specs=out_specs,
            scratch_shapes=list(scratch),
        ),
        out_shape=out_shape,
        compiler_params=params(len(grid)),
        cost_estimate=cost(flops, nbytes),
    )


def dot(a, b, ca, cb):
    return lax.dot_general(a, b, (((ca,), (cb,)), ((), ())), preferred_element_type=F32)


def starts_of(lens_ref):
    out, at = [], jnp.int32(0)
    for j in range(lens_ref.shape[0]):
        out.append(at)
        at = at + lens_ref[j]
    return out


def start_at(starts, p):
    best = jnp.where(p >= 0, 0, -1) if not hasattr(p, "shape") or p.shape == () else None
    if best is None:
        best = jnp.where(p >= 0, jnp.zeros_like(p), -jnp.ones_like(p))
    for s in starts[1:]:
        best = jnp.where(p >= s, s, best)
    return best


def rows_pos(tok, first):
    return lax.broadcasted_iota(jnp.int32, (tok, 1), 0) + first


def carry_in_of(info_ref, lens_ref, tok):
    first = info_ref[I_BLK] * tok
    starts = starts_of(lens_ref)
    rows = start_at(starts, rows_pos(tok, first))
    return rows == start_at(starts, first - 1)


def carry_out_of(info_ref, lens_ref, tok):
    first = info_ref[I_BLK] * tok
    starts = starts_of(lens_ref)
    rows = start_at(starts, rows_pos(tok, first))
    return rows == start_at(starts, first + tok - 1)


def mask_of(info_ref, lens_ref, tok, r0, rn, cn):
    first = info_ref[I_BLK] * tok
    starts = starts_of(lens_ref)
    low = start_at(starts, rows_pos(rn, first + r0)) - first
    row = lax.broadcasted_iota(jnp.int32, (rn, cn), 0) + r0
    col = lax.broadcasted_iota(jnp.int32, (rn, cn), 1)
    return (col <= row) & (col >= low)


def state_body(info_ref, lens_ref, k_ref, v_ref, send_ref, keep_ref):
    i = pl.program_id(0)
    half = pl.num_programs(0) // 2
    tok = k_ref.shape[0]
    keep = carry_out_of(info_ref, lens_ref, tok)
    kept = jnp.where(keep, k_ref[...], jnp.zeros((), BF16))
    state = dot(kept, v_ref[...], 0, 0).astype(BF16)

    @pl.when(i < half)
    def _():
        send_ref[0] = state

    @pl.when(i >= half)
    def _():
        keep_ref[0] = state


def local_states(info, lens, k, v):
    tok, wide = k.shape
    heads = wide // DH
    half = heads // 2

    def head_of(i, info, lens):
        return (0, lax.rem(i + half * (1 - info[I_HALF]), heads))

    return call(
        state_body,
        "local_states",
        (heads,),
        2,
        [pl.BlockSpec((tok, DH), head_of), pl.BlockSpec((tok, DH), head_of)],
        [
            pl.BlockSpec((1, DH, DH), lambda i, *_: (jnp.minimum(i, half - 1), 0, 0)),
            pl.BlockSpec((1, DH, DH), lambda i, *_: (jnp.maximum(i - half, 0), 0, 0)),
        ],
        [jax.ShapeDtypeStruct((half, DH, DH), BF16)] * 2,
        flops=2 * tok * DH * wide,
        nbytes=4 * tok * wide,
    )(info, lens, k, v)


def intra_body(info_ref, lens_ref, q_ref, k_ref, v_ref, out_ref):
    tok = q_ref.shape[0]
    hb = tok // 2
    for part in range(2):
        r0, n = part * hb, (part + 1) * hb
        s = dot(q_ref[r0:r0 + hb, :], k_ref[:n, :], 1, 1)
        s = jnp.where(mask_of(info_ref, lens_ref, tok, r0, hb, n), s, 0.0).astype(BF16)
        out_ref[r0:r0 + hb, :] = dot(s, v_ref[:n, :], 1, 0)


def col(tok):
    return pl.BlockSpec((tok, DH), lambda h, *_: (0, h))


def state_spec():
    return pl.BlockSpec((1, DH, DH), lambda h, *_: (h, 0, 0))


def intra(info, lens, q, k, v):
    tok, wide = q.shape
    return call(
        intra_body,
        "intra",
        (wide // DH,),
        2,
        [col(tok)] * 3,
        col(tok),
        jax.ShapeDtypeStruct((tok, wide), F32),
        flops=3 * tok * tok * wide,
        nbytes=10 * tok * wide,
    )(info, lens, q, k, v)


def norm_body(info_ref, lens_ref, q_ref, e_ref, a_ref, att_ref, n_ref):
    tok = q_ref.shape[0]
    keep = carry_in_of(info_ref, lens_ref, tok)
    inter = dot(q_ref[...], e_ref[0], 1, 0)
    att = a_ref[...] + jnp.where(keep, inter, 0.0)
    att_ref[...] = att
    inv = lax.rsqrt(jnp.mean(att * att, axis=-1, keepdims=True) + EPS)
    n_ref[...] = (att * inv).astype(BF16)


def normalise(info, lens, q, entering, a):
    tok, wide = q.shape
    return call(
        norm_body,
        "normalise",
        (wide // DH,),
        2,
        [col(tok), state_spec(), col(tok)],
        [col(tok), col(tok)],
        [jax.ShapeDtypeStruct((tok, wide), F32), jax.ShapeDtypeStruct((tok, wide), BF16)],
        flops=2 * tok * DH * wide,
        nbytes=12 * tok * wide,
    )(info, lens, q, entering, a)


def proj_body(b_ref, n_ref, w_ref, o_ref):
    o_ref[...] = dot(n_ref[...], w_ref[...], 1, 0).astype(BF16)


def project(block, normed, w, width):
    tok, feats = normed.shape
    tile = 256
    steps = width // tile
    return call(
        proj_body,
        "project",
        (steps,),
        1,
        [
            pl.BlockSpec((tok, feats), lambda i, b: (0, 0)),
            pl.BlockSpec((feats, tile), lambda i, b: (0, b[0] * steps + i)),
        ],
        pl.BlockSpec((tok, tile), lambda i, b: (0, i)),
        jax.ShapeDtypeStruct((tok, width), BF16),
        flops=2 * tok * feats * width,
        nbytes=2 * (tok * feats + feats * width + tok * width),
    )(block, normed, w)


def back_body(n, b_ref, *refs):
    acc = None
    for i in range(n):
        part = dot(refs[2 * i][...], refs[2 * i + 1][...], 1, 1)
        acc = part if acc is None else acc + part
    if len(refs) == 2 * n + 2:
        acc = acc + refs[2 * n][...]
    refs[-1][...] = acc


def back_project(blocks, grads, w, base=None):
    tok, width = grads[0].shape
    feats = w.shape[0]
    tile = 256
    n = len(grads)
    specs = []
    args = []
    for i in range(n):
        specs.append(pl.BlockSpec((tok, width), lambda f, b: (0, 0)))
        specs.append(pl.BlockSpec((tile, width), lambda f, b, i=i: (f, b[i])))
        args += [grads[i], w]
    if base is not None:
        specs.append(pl.BlockSpec((tok, tile), lambda f, b: (0, f)))
        args.append(base)
    return call(
        functools.partial(back_body, n),
        "back_project",
        (feats // tile,),
        1,
        specs,
        pl.BlockSpec((tok, tile), lambda f, b: (0, f)),
        jax.ShapeDtypeStruct((tok, feats), F32),
        flops=2 * n * tok * feats * width,
        nbytes=n * 2 * (tok * width + feats * width) + 8 * tok * feats,
    )(blocks, *args)


def att_grad_body(info_ref, lens_ref, b_ref, x_ref, w_ref, base_ref, att_ref, q_ref, ag_ref, send_ref, keep_ref):
    i = pl.program_id(0)
    half = pl.num_programs(0) // 2
    tok = x_ref.shape[0]
    ng2 = base_ref[...] + dot(x_ref[...], w_ref[...], 1, 1)
    keep = carry_in_of(info_ref, lens_ref, tok)
    states = []
    for j in range(2):
        at = slice(j * DH, (j + 1) * DH)
        ng, att = ng2[:, at], att_ref[:, at]
        inv = lax.rsqrt(jnp.mean(att * att, axis=-1, keepdims=True) + EPS)
        normed = att * inv
        proj = jnp.mean(ng * normed, axis=-1, keepdims=True)
        ag = ((ng - normed * proj) * inv).astype(BF16)
        ag_ref[:, at] = ag
        kept = jnp.where(keep, q_ref[:, at], jnp.zeros((), BF16))
        states.append(dot(kept, ag, 0, 0).astype(BF16))

    @pl.when(i < half)
    def _():
        send_ref[0] = states[0]
        send_ref[1] = states[1]

    @pl.when(i >= half)
    def _():
        keep_ref[0] = states[0]
        keep_ref[1] = states[1]


def attended_grads(info, lens, block, x, w, base, att, q):
    tok, wide = q.shape
    width = x.shape[1]
    pairs = wide // DH // 2
    half = pairs // 2

    def pair_of(i, info, lens, b):
        return lax.rem(i + half * (1 - info[I_HALF]), pairs)

    def cols(i, info, lens, b):
        return (0, pair_of(i, info, lens, b))

    two = pl.BlockSpec((tok, 2 * DH), cols)
    return call(
        att_grad_body,
        "attended_grads",
        (pairs,),
        3,
        [
            pl.BlockSpec((tok, width), lambda i, *_: (0, 0)),
            pl.BlockSpec((2 * DH, width), lambda i, info, lens, b: (pair_of(i, info, lens, b), b[0])),
            two,
            two,
            two,
        ],
        [
            two,
            pl.BlockSpec((2, DH, DH), lambda i, *_: (jnp.minimum(i, half - 1), 0, 0)),
            pl.BlockSpec((2, DH, DH), lambda i, *_: (jnp.maximum(i - half, 0), 0, 0)),
        ],
        [
            jax.ShapeDtypeStruct((tok, wide), BF16),
            jax.ShapeDtypeStruct((2 * half, DH, DH), BF16),
            jax.ShapeDtypeStruct((2 * half, DH, DH), BF16),
        ],
        flops=2 * tok * wide * width + 2 * tok * DH * wide,
        nbytes=2 * (tok * width + width * wide) + 12 * tok * wide,
    )(info, lens, block, x, w, base, att, q)


def grads_body(info_ref, lens_ref, q_ref, k_ref, v_ref, ag_ref, e_ref, qg_ref, kg_ref, vg_ref):
    tok = q_ref.shape[0]
    hb = tok // 2
    keep = carry_in_of(info_ref, lens_ref, tok)
    inter = jnp.where(keep, dot(ag_ref[...], e_ref[0], 1, 1), 0.0)
    for part in range(2):
        r0, n = part * hb, (part + 1) * hb
        mask = mask_of(info_ref, lens_ref, tok, r0, hb, n)
        q, ag = q_ref[r0:n, :], ag_ref[r0:n, :]
        s = jnp.where(mask, dot(q, k_ref[:n, :], 1, 1), 0.0).astype(BF16)
        g = jnp.where(mask, dot(ag, v_ref[:n, :], 1, 1), 0.0).astype(BF16)
        qg_ref[r0:n, :] = (dot(g, k_ref[:n, :], 1, 0) + inter[r0:n]).astype(BF16)
        kg, vg = dot(g, q, 0, 0), dot(s, ag, 0, 0)
        if part == 0:
            kg_ref[:n, :] = kg
            vg_ref[:n, :] = vg
        else:
            kg_ref[:hb, :] += kg[:hb]
            vg_ref[:hb, :] += vg[:hb]
            kg_ref[hb:, :] = kg[hb:]
            vg_ref[hb:, :] = vg[hb:]


def block_grads(info, lens, q, k, v, ag, entering):
    tok, wide = q.shape
    return call(
        grads_body,
        "block_grads",
        (wide // DH,),
        2,
        [col(tok)] * 4 + [state_spec()],
        [col(tok)] * 3,
        [
            jax.ShapeDtypeStruct((tok, wide), BF16),
            jax.ShapeDtypeStruct((tok, wide), F32),
            jax.ShapeDtypeStruct((tok, wide), F32),
        ],
        flops=8 * tok * tok * wide,
        nbytes=18 * tok * wide,
    )(info, lens, q, k, v, ag, entering)


def last_body(info_ref, lens_ref, k_ref, v_ref, l_ref, kp_ref, vp_ref, kg_ref, vg_ref):
    tok = k_ref.shape[0]
    keep = carry_out_of(info_ref, lens_ref, tok)
    kg = jnp.where(keep, dot(v_ref[...], l_ref[0], 1, 1), 0.0)
    vg = jnp.where(keep, dot(k_ref[...], l_ref[0], 1, 0), 0.0)
    kg_ref[...] = (kp_ref[...] + kg).astype(BF16)
    vg_ref[...] = (vp_ref[...] + vg).astype(BF16)


def last_grads(info, lens, k, v, leaving, kp, vp):
    tok, wide = k.shape
    return call(
        last_body,
        "last_grads",
        (wide // DH,),
        2,
        [col(tok), col(tok), state_spec(), col(tok), col(tok)],
        [col(tok)] * 2,
        [jax.ShapeDtypeStruct((tok, wide), BF16)] * 2,
        flops=4 * tok * DH * wide,
        nbytes=16 * tok * wide,
    )(info, lens, k, v, leaving, kp, vp)


def doc_start_scalars(lens):
    out, at = [], jnp.int32(0)
    for j in range(lens.shape[0] - 1):
        at = at + lens[j]
        out.append(at)
    return out


def exchange(send, keep, lens, tok, forward):
    n = lax.axis_size("ctx")
    me = lax.axis_index("ctx")
    starts = doc_start_scalars(lens)

    def same(a, b):
        pa, pb = a * tok + tok - 1, b * tok + tok - 1
        one = (a >= 0) | (b < 0)
        for s in starts:
            one = one & ~((pa < s) & (s <= pb))
        return one.astype(F32)

    swap = [(i, i ^ 1) for i in range(n)]
    core = me % 2
    first, second = me - core, me - core + 1
    is_second = (core == 1).astype(F32)
    is_first = 1.0 - is_second
    got = lax.ppermute(send, "ctx", swap).astype(F32)
    mine = keep.astype(F32)
    if forward:
        link = same(first, second)
        total = mine * (is_second + is_first * link) + got * (is_first + is_second * link)
    else:
        link = same(first - 1, first)
        total = mine * (is_first + is_second * link) + got * (is_second + is_first * link)
    total = total.astype(BF16)
    entering = None
    low, high = first, second
    m = 2
    while m < n:
        last = 2 * m >= n
        up = (me // m) % 2 == 1
        if last:
            pairs = [(i, i ^ m) for i in range(n) if ((i // m) % 2 == 0) == forward]
        else:
            pairs = [(i, i ^ m) for i in range(n)]
        other = lax.ppermute(total, "ctx", pairs).astype(F32)
        group_low = (me // (2 * m)) * 2 * m
        edge = group_low + m - 1
        if forward:
            weight = jnp.where(up, same(edge, first - 1), 0.0)
        else:
            weight = jnp.where(up, 0.0, same(second, edge))
        part = other * weight
        if not last:
            if forward:
                through = same(edge, group_low + 2 * m - 1)
                near = up
            else:
                through = same(group_low - 1, edge)
                near = jnp.logical_not(up)
            own_w = jnp.where(near, 1.0, through)
            other_w = jnp.where(near, through, 1.0)
            total = (total.astype(F32) * own_w + other * other_w).astype(BF16)
        entering = part if entering is None else entering + part
        m *= 2
    if entering is None:
        entering = jnp.zeros_like(mine)
    if forward:
        link = same(first - 1, first)
        near, far = is_first, is_second
    else:
        link = same(first, second)
        near, far = is_second, is_first
    chained = mine * near + got * far + link * entering
    own = entering * near + chained * far
    away = chained * near + entering * far
    own, away = own.astype(BF16), away.astype(BF16)
    back = lax.ppermute(away, "ctx", swap)
    return jnp.where(
        core == 0, jnp.concatenate([own, back], 0), jnp.concatenate([back, own], 0)
    )


def add(*parts):
    total = parts[0].astype(F32)
    for part in parts[1:]:
        total = total + part.astype(F32)
    return total.astype(BF16)


def shards(q, k, v, lens, w, grad):
    tok, width = grad.shape
    blk = lax.axis_index("ctx").astype(jnp.int32)
    z = lax.axis_index("head").astype(jnp.int32)
    info = jnp.stack([blk, blk % 2])

    def at(*blocks):
        return jnp.stack(blocks).astype(jnp.int32)

    up = [(0, 1), (1, 2), (2, 3)]
    down = [(1, 0), (2, 1), (3, 2)]
    u1 = lax.ppermute(grad, "head", up)
    d1 = lax.ppermute(grad, "head", down)
    send, keep = local_states(info, lens, k, v)
    entering = exchange(send, keep, lens, tok, True)
    intra_part = intra(info, lens, q, k, v)
    att, normed = normalise(info, lens, q, entering, intra_part)
    u2 = lax.ppermute(u1, "head", [(1, 2), (2, 3)])
    d2 = lax.ppermute(d1, "head", [(2, 1), (1, 0)])
    pa = project(at(jnp.where(z == 0, 3, 0)), normed, w, width)
    ra = lax.ppermute(pa, "head", [(0, 1), (3, 2)])
    p2 = project(at((z + 2) % 4), normed, w, width)
    p1 = project(at((z + 1) % 4), normed, w, width)
    p3 = project(at((z + 3) % 4), normed, w, width)
    p0 = project(at(z), normed, w, width)
    base = back_project(at(z, (z + 3) % 4, (z + 1) % 4), [grad, u1, d1], w)
    bo = lax.ppermute(p2, "head", [(0, 1), (3, 2)])
    x2 = u2 + d2
    x3 = lax.ppermute(x2, "head", [(2, 3), (1, 0)])
    bi = lax.ppermute(add(p2, ra), "head", [(1, 2), (2, 1)])
    base = back_project(at((z + 2) % 4), [x2], w, base)
    cu = lax.ppermute(add(p1, jnp.where(z == 1, bo, bi)), "head", up)
    cd = lax.ppermute(add(p3, jnp.where(z == 2, bo, bi)), "head", down)
    ag, gsend, gkeep = attended_grads(
        info, lens, at(jnp.where(z == 3, 0, 3)), x3, w, base, att, q
    )
    leaving = exchange(gsend, gkeep, lens, tok, False)
    query_grad, kp, vp = block_grads(info, lens, q, k, v, ag, entering)
    key_grad, value_grad = last_grads(info, lens, k, v, leaving, kp, vp)
    mixed = add(p0, cu, cd)
    return mixed, query_grad, key_grad, value_grad


def solution(mesh):
    return jax.shard_map(
        shards,
        mesh=mesh,
        in_specs=(
            P("ctx", "head"),
            P("ctx", "head"),
            P("ctx", "head"),
            P(),
            P("head", None),
            P("ctx", "head"),
        ),
        out_specs=(P("ctx", "head"), P("ctx", "head"), P("ctx", "head"), P("ctx", "head")),
        check_vma=False,
    )
```

```python
import functools

import jax
import jax.numpy as jnp
from jax import lax
from jax.experimental import pallas as pl
from jax.experimental.pallas import tpu as pltpu
from jax.sharding import PartitionSpec as P

DH = 128
EPS = 1e-06
F32 = jnp.float32
BF16 = jnp.bfloat16
MIB = 1024 * 1024

I_BLK, I_CORE, I_Z = 0, 1, 2


def kernel(body, name, info, lens, ins, outs, deps=(), spare=8, scratch=()):
    n_in, n_dep = len(ins), len(deps)

    def inner(info_ref, lens_ref, *refs):
        body(info_ref, lens_ref, *refs[:n_in], *refs[n_in + n_dep:])

    size = sum(a.size * a.dtype.itemsize for a in list(ins) + list(outs))
    smem = pl.BlockSpec(memory_space=pltpu.SMEM)
    vmem = pl.BlockSpec(memory_space=pltpu.VMEM)
    hbm = pl.BlockSpec(memory_space=pl.ANY)
    return pl.pallas_call(
        inner,
        name=name,
        in_specs=[smem, smem] + [vmem] * n_in + [hbm] * n_dep,
        out_specs=[vmem] * len(outs),
        out_shape=list(outs),
        scratch_shapes=list(scratch),
        compiler_params=pltpu.CompilerParams(vmem_limit_bytes=size + spare * MIB),
    )(info, lens, *ins, *deps)


def like(shape, dtype):
    return jax.ShapeDtypeStruct(shape, dtype)


def dot(a, b, ca, cb):
    return lax.dot_general(a, b, (((ca,), (cb,)), ((), ())), preferred_element_type=F32)


def head(h):
    return slice(h * DH, (h + 1) * DH)


def starts_of(lens_ref):
    out, at = [], jnp.int32(0)
    for j in range(lens_ref.shape[0] - 1):
        at = at + lens_ref[j]
        out.append(at)
    return out


def start_at(starts, p):
    best = jnp.minimum(p, 0)
    best = jnp.maximum(best, -1)
    for s in starts:
        best = jnp.where(p >= s, s, best)
    return best


def line(tok, axis):
    return lax.broadcasted_iota(jnp.int32, (tok, 1) if axis == 0 else (1, tok), axis)


def carries_in(info_ref, lens_ref, tok):
    first = info_ref[I_BLK] * tok
    starts = starts_of(lens_ref)
    return start_at(starts, line(tok, 0) + first) == start_at(starts, first - 1)


def carries_out(info_ref, lens_ref, tok):
    first = info_ref[I_BLK] * tok
    starts = starts_of(lens_ref)
    return start_at(starts, line(tok, 0) + first) == start_at(starts, first + tok - 1)


def visible(info_ref, lens_ref, tok, axis):
    first = info_ref[I_BLK] * tok
    t, s = line(tok, axis), line(tok, 1 - axis)
    low = start_at(starts_of(lens_ref), t + first) - first
    return (s <= t) & (s >= low)


def same(starts, tok, a, b):
    pa, pb = a * tok + tok - 1, b * tok + tok - 1
    one = (a >= 0) | (b < 0)
    for s in starts:
        one = jnp.logical_and(one, jnp.logical_not(jnp.logical_and(pa < s, s <= pb)))
    return jnp.where(one, 1.0, 0.0).astype(F32)


def states_body(half, info_ref, lens_ref, k_ref, v_ref, send_ref, keep_ref):
    keep = carries_out(info_ref, lens_ref, k_ref.shape[0])
    zero = jnp.zeros((), BF16)
    core = info_ref[I_CORE]
    states = []
    for h in range(2 * half):
        kept = jnp.where(keep, k_ref[:, head(h)], zero)
        states.append(dot(kept, v_ref[:, head(h)], 0, 0).astype(BF16))
    for i in range(half):
        keep_ref[i] = jnp.where(core == 0, states[i], states[i + half])
        send_ref[i] = jnp.where(core == 0, states[i + half], states[i])


def intra_body(info_ref, lens_ref, q_ref, k_ref, v_ref, out_ref):
    tok, wide = q_ref.shape
    mask = visible(info_ref, lens_ref, tok, 0)
    for h in range(wide // DH):
        s = dot(q_ref[:, head(h)], k_ref[:, head(h)], 1, 1)
        s = jnp.where(mask, s, 0.0).astype(BF16)
        out_ref[:, head(h)] = dot(s, v_ref[:, head(h)], 1, 0)


def pick(info_ref, own_ref, back_ref, h):
    half = own_ref.shape[0]
    return jnp.where(info_ref[I_CORE] == h // half, own_ref[h % half], back_ref[h % half])


def norm_body(info_ref, lens_ref, q_ref, own_ref, back_ref, a_ref, att_ref, n_ref):
    tok, wide = q_ref.shape
    keep = carries_in(info_ref, lens_ref, tok)
    for h in range(wide // DH):
        inter = dot(q_ref[:, head(h)], pick(info_ref, own_ref, back_ref, h), 1, 0)
        att = a_ref[:, head(h)] + jnp.where(keep, inter, 0.0)
        att_ref[:, head(h)] = att
        inv = lax.rsqrt(jnp.mean(att * att, axis=-1, keepdims=True) + EPS)
        n_ref[:, head(h)] = (att * inv).astype(BF16)


TILE = 256


def project_body(blocks, info_ref, lens_ref, n_ref, w_ref, *out_refs):
    tok, width = out_refs[0].shape
    for block, out_ref in zip(blocks, out_refs, strict=True):
        base = block(info_ref[I_Z]) * width
        for i in range(width // TILE):
            at = pl.multiple_of(base + i * TILE, TILE)
            out_ref[:, i * TILE:(i + 1) * TILE] = dot(
                n_ref[...], w_ref[:, pl.ds(at, TILE)], 1, 0
            ).astype(BF16)


def back_body(blocks, based, info_ref, lens_ref, w_ref, *refs):
    out_ref = refs[-1]
    feats = out_ref.shape[1]
    for i in range(feats // TILE):
        rows = slice(i * TILE, (i + 1) * TILE)
        acc = refs[-2][:, rows] if based else None
        for block, g_ref in zip(blocks, refs, strict=False):
            width = g_ref.shape[1]
            at = pl.multiple_of(block(info_ref[I_Z]) * width, TILE)
            part = dot(g_ref[...], w_ref[rows, pl.ds(at, width)], 1, 1)
            acc = part if acc is None else acc + part
        out_ref[:, rows] = acc


def att_grad_body(block, info_ref, lens_ref, w_ref, x_ref, base_ref, att_ref, q_ref, ag_ref, send_ref, keep_ref):
    tok, wide = q_ref.shape
    width = x_ref.shape[1]
    keep = carries_in(info_ref, lens_ref, tok)
    core = info_ref[I_CORE]
    zero = jnp.zeros((), BF16)
    at = pl.multiple_of(block(info_ref[I_Z]) * width, TILE)
    states = []
    for i in range(wide // TILE):
        rows = slice(i * TILE, (i + 1) * TILE)
        ng2 = base_ref[:, rows] + dot(x_ref[...], w_ref[rows, pl.ds(at, width)], 1, 1)
        for j in range(TILE // DH):
            h = i * (TILE // DH) + j
            ng, att = ng2[:, head(j)], att_ref[:, head(h)]
            inv = lax.rsqrt(jnp.mean(att * att, axis=-1, keepdims=True) + EPS)
            normed = att * inv
            proj = jnp.mean(ng * normed, axis=-1, keepdims=True)
            ag = ((ng - normed * proj) * inv).astype(BF16)
            ag_ref[:, head(h)] = ag
            kept = jnp.where(keep, q_ref[:, head(h)], zero)
            states.append(dot(kept, ag, 0, 0).astype(BF16))
    half = len(states) // 2
    for i in range(half):
        keep_ref[i] = jnp.where(core == 0, states[i], states[i + half])
        send_ref[i] = jnp.where(core == 0, states[i + half], states[i])


def grads_body(info_ref, lens_ref, q_ref, k_ref, v_ref, ag_ref, own_ref, back_ref, qg_ref, kg_ref, vg_ref):
    tok, wide = q_ref.shape
    keep = carries_in(info_ref, lens_ref, tok)
    mask = visible(info_ref, lens_ref, tok, 0)
    mask_t = visible(info_ref, lens_ref, tok, 1)
    for h in range(wide // DH):
        q, k, v, ag = (r[:, head(h)] for r in (q_ref, k_ref, v_ref, ag_ref))
        inter = dot(ag, pick(info_ref, own_ref, back_ref, h), 1, 1)
        st = jnp.where(mask_t, dot(k, q, 1, 1), 0.0).astype(BF16)
        vg_ref[:, head(h)] = dot(st, ag, 1, 0)
        g = jnp.where(mask, dot(ag, v, 1, 1), 0.0).astype(BF16)
        qg_ref[:, head(h)] = (dot(g, k, 1, 0) + jnp.where(keep, inter, 0.0)).astype(BF16)
        kg_ref[:, head(h)] = dot(g, q, 0, 0)


def last_body(info_ref, lens_ref, k_ref, v_ref, own_ref, back_ref, kp_ref, vp_ref, kg_ref, vg_ref):
    tok, wide = k_ref.shape
    keep = carries_out(info_ref, lens_ref, tok)
    for h in range(wide // DH):
        leaving = pick(info_ref, own_ref, back_ref, h)
        kg = jnp.where(keep, dot(v_ref[:, head(h)], leaving, 1, 1), 0.0)
        vg = jnp.where(keep, dot(k_ref[:, head(h)], leaving, 1, 0), 0.0)
        kg_ref[:, head(h)] = (kp_ref[:, head(h)] + kg).astype(BF16)
        vg_ref[:, head(h)] = (vp_ref[:, head(h)] + vg).astype(BF16)


def sum_body(info_ref, lens_ref, *refs):
    total = refs[0][...].astype(F32)
    for r in refs[1:-1]:
        total = total + r[...].astype(F32)
    refs[-1][...] = total.astype(BF16)


def fold_body(info_ref, lens_ref, p1_ref, p3_ref, bo_ref, bi_ref, up_ref, down_ref):
    z = info_ref[I_Z]
    bo, bi = bo_ref[...], bi_ref[...]
    up_ref[...] = (p1_ref[...].astype(F32) + jnp.where(z == 1, bo, bi).astype(F32)).astype(BF16)
    down_ref[...] = (p3_ref[...].astype(F32) + jnp.where(z == 2, bo, bi).astype(F32)).astype(BF16)


def pair_body(forward, tok, info_ref, lens_ref, mine_ref, got_ref, total_ref):
    starts = starts_of(lens_ref)
    blk, core = info_ref[I_BLK], info_ref[I_CORE]
    first = blk - core
    if forward:
        far, link = core == 0, same(starts, tok, first, first + 1)
    else:
        far, link = core == 1, same(starts, tok, first - 1, first)
    a, b = jnp.where(far, link, 1.0), jnp.where(far, 1.0, link)
    total_ref[...] = (mine_ref[...].astype(F32) * a + got_ref[...].astype(F32) * b).astype(BF16)


def step_body(forward, tok, m, last, begun, info_ref, lens_ref, *refs):
    starts = starts_of(lens_ref)
    blk, core = info_ref[I_BLK], info_ref[I_CORE]
    first = blk - core
    second = first + 1
    up = lax.rem(blk // m, 2) == 1
    low = blk // (2 * m) * (2 * m)
    edge = low + m - 1
    refs = list(refs)
    other = refs.pop(0)[...].astype(F32)
    if forward:
        entering = other * jnp.where(up, same(starts, tok, edge, first - 1), 0.0)
    else:
        entering = other * jnp.where(up, 0.0, same(starts, tok, second, edge))
    if begun:
        entering = entering + refs.pop(0)[...]
    if not last:
        total_ref, new_total_ref, entering_ref = refs
        entering_ref[...] = entering
        if forward:
            near, through = up, same(starts, tok, edge, low + 2 * m - 1)
        else:
            near, through = jnp.logical_not(up), same(starts, tok, low - 1, edge)
        a, b = jnp.where(near, 1.0, through), jnp.where(near, through, 1.0)
        new_total_ref[...] = (total_ref[...].astype(F32) * a + other * b).astype(BF16)
        return
    mine_ref, got_ref, own_ref, away_ref = refs
    if forward:
        near, link = core == 0, same(starts, tok, first - 1, first)
    else:
        near, link = core == 1, same(starts, tok, first, second)
    nearer = jnp.where(near, mine_ref[...], got_ref[...]).astype(F32)
    chained = nearer + link * entering
    own_ref[...] = jnp.where(near, entering, chained).astype(BF16)
    away_ref[...] = jnp.where(near, chained, entering).astype(BF16)


def exchange(send, keep, info, lens, tok, forward, deps):
    n = lax.axis_size("ctx")
    swap = [(i, i ^ 1) for i in range(n)]
    half = like(keep.shape, BF16)
    deps = list(deps)
    got = lax.ppermute(send, "ctx", swap)
    (total,) = kernel(
        functools.partial(pair_body, forward, tok), "pair_total", info, lens, [keep, got], [half],
        deps.pop(0) if deps else (),
    )
    entering, m = [], 2
    while m < n:
        last = 2 * m >= n
        pairs = [(i, i ^ m) for i in range(n) if not last or ((i // m) % 2 == 0) == forward]
        other = lax.ppermute(total, "ctx", pairs)
        body = functools.partial(step_body, forward, tok, m, last, bool(entering))
        more = deps.pop(0) if deps else ()
        if last:
            own, away = kernel(
                body, "exchange_last", info, lens, [other, *entering, keep, got], [half, half], more
            )
        else:
            total, e = kernel(
                body, "exchange_step", info, lens, [other, *entering, total],
                [half, like(keep.shape, F32)], more,
            )
            entering = [e]
        m *= 2
    return own, lax.ppermute(away, "ctx", swap)


def shards(q, k, v, lens, w, grad):
    tok, width = grad.shape
    feats = w.shape[0]
    heads = feats // DH
    half = heads // 2
    blk = lax.axis_index("ctx").astype(jnp.int32)
    z = lax.axis_index("head").astype(jnp.int32)
    info = jnp.stack([blk, blk % 2, z])
    run = lambda body, name, ins, outs, deps=(), spare=8: kernel(
        body, name, info, lens, ins, outs, deps, spare
    )
    part = like((tok, width), BF16)
    wide_b, wide_f = like((tok, feats), BF16), like((tok, feats), F32)
    state = like((half, DH, DH), BF16)

    def project(blocks, name, deps=()):
        return run(functools.partial(project_body, blocks), name, [normed, w], [part] * len(blocks), deps)

    def back_project(blocks, name, grads, base=None, deps=()):
        body = functools.partial(back_body, blocks, base is not None)
        return run(body, name, [w, *grads] + ([] if base is None else [base]), [wide_f], deps)[0]

    up = [(0, 1), (1, 2), (2, 3)]
    down = [(1, 0), (2, 1), (3, 2)]
    outer = [(0, 1), (3, 2)]
    u1 = lax.ppermute(grad, "head", up)
    d1 = lax.ppermute(grad, "head", down)
    send, keep = run(functools.partial(states_body, half), "local_states", [k, v], [state, state])
    (inside,) = run(intra_body, "intra", [q, k, v], [wide_f], [send])
    base = back_project([lambda z: z], "back_own", [grad], None, [inside])
    own, other = exchange(send, keep, info, lens, tok, True, [(), (inside,), (base,)])
    att, normed = run(norm_body, "normalise", [q, own, other, inside], [wide_f, wide_b])
    u2 = lax.ppermute(u1, "head", [(1, 2), (2, 3)])
    d2 = lax.ppermute(d1, "head", [(2, 1), (1, 0)])
    (pa,) = project([lambda z: jnp.where(z == 0, 3, 0)], "project_far")
    ra = lax.ppermute(pa, "head", outer)
    p2, p1, p3, p0 = project(
        [lambda z: lax.rem(z + 2, 4), lambda z: lax.rem(z + 1, 4), lambda z: lax.rem(z + 3, 4), lambda z: z],
        "project_rest", [pa],
    )
    base = back_project(
        [lambda z: lax.rem(z + 3, 4), lambda z: lax.rem(z + 1, 4)], "back_near", [u1, d1], base, [p2]
    )
    (x2,) = run(sum_body, "join", [u2, d2], [part], [base])
    x3 = lax.ppermute(x2, "head", [(2, 3), (1, 0)])
    (b2,) = run(sum_body, "fold", [p2, ra], [part], [base])
    bo = lax.ppermute(p2, "head", outer)
    bi = lax.ppermute(b2, "head", [(1, 2), (2, 1)])
    base = back_project([lambda z: lax.rem(z + 2, 4)], "back_far", [x2], base, [b2])
    cu, cd = run(fold_body, "fold_both", [p1, p3, bo, bi], [part, part], [base])
    gu = lax.ppermute(cu, "head", up)
    gd = lax.ppermute(cd, "head", down)
    ag, gsend, gkeep = run(
        functools.partial(att_grad_body, lambda z: jnp.where(z == 3, 0, 3)), "attended_grads",
        [w, x3, base, att, q], [wide_b, state, state], [cu],
    )
    query_grad, kp, vp = run(
        grads_body, "block_grads", [q, k, v, ag, own, other], [wide_b, wide_f, wide_f], [gsend]
    )
    leaving, leaving_other = exchange(gsend, gkeep, info, lens, tok, False, [(), (query_grad,), ()])
    key_grad, value_grad = run(
        last_body, "last_grads", [k, v, leaving, leaving_other, kp, vp], [wide_b, wide_b]
    )
    (mixed,) = run(sum_body, "mixed", [p0, gu, gd], [part], [key_grad])
    return mixed, query_grad, key_grad, value_grad


def solution(mesh):
    return jax.shard_map(
        shards,
        mesh=mesh,
        in_specs=(
            P("ctx", "head"),
            P("ctx", "head"),
            P("ctx", "head"),
            P(),
            P("head", None),
            P("ctx", "head"),
        ),
        out_specs=(P("ctx", "head"), P("ctx", "head"), P("ctx", "head"), P("ctx", "head")),
        check_vma=False,
    )
```

```python
import functools

import jax
import jax.numpy as jnp
from jax import lax
from jax.experimental import pallas as pl
from jax.experimental.pallas import tpu as pltpu
from jax.sharding import PartitionSpec as P

DH = 128
EPS = 1e-06
F32 = jnp.float32
BF16 = jnp.bfloat16
MIB = 1024 * 1024

RATE = 10**8
MICROSECONDS = {
    "setup": 100.0, "local_states": 0.8, "intra": 3.0, "back_own": 1.8, "pair_total": 0.1, "exchange_stage": 0.1,
    "exchange_last": 0.1, "normalise": 0.9, "project_3": 1.8, "project_2": 1.8, "project_1": 1.8,
    "project_0": 1.8, "back_1": 1.8, "pick": 0.3, "turn": 0.5, "back_2": 1.8, "attended_grads": 4.1,
    "query_grad": 3.0, "key_value_grads": 5.0, "last_grads": 2.5, "mixed": 1.3,
}

I_BLK, I_CORE, I_Z, I_DOCS = 0, 1, 2, 3


def kernel(body, name, smem, ins, outs, deps=(), spare=8):
    n, n_dep = len(smem) + len(ins), len(deps)

    def inner(*refs):
        body(*refs[:n], *refs[n + n_dep:])

    size = sum(a.size * a.dtype.itemsize for a in list(ins) + list(outs))
    spec = lambda space: pl.BlockSpec(memory_space=space)
    return pl.pallas_call(
        inner,
        name=name,
        in_specs=[spec(pltpu.SMEM)] * len(smem) + [spec(pltpu.VMEM)] * len(ins) + [spec(pl.ANY)] * n_dep,
        out_specs=[spec(pltpu.VMEM)] * len(outs),
        out_shape=list(outs),
        compiler_params=pltpu.CompilerParams(vmem_limit_bytes=size + spare * MIB),
        cost_estimate=pl.CostEstimate(
            flops=int(MICROSECONDS[name] * RATE), bytes_accessed=0, transcendentals=0
        ),
    )(*smem, *ins, *deps)


def like(shape, dtype):
    return jax.ShapeDtypeStruct(shape, dtype)


def dot(a, b, ca, cb):
    return lax.dot_general(a, b, (((ca,), (cb,)), ((), ())), preferred_element_type=F32)


def head(h):
    return slice(h * DH, (h + 1) * DH)


def starts_of(info_ref):
    out, at = [], jnp.int32(0)
    for j in range(I_DOCS, info_ref.shape[0] - 1):
        at = at + info_ref[j]
        out.append(at)
    return out


def start_at(starts, p):
    best = jnp.minimum(p, 0)
    best = jnp.maximum(best, -1)
    for s in starts:
        best = jnp.where(p >= s, s, best)
    return best


def line(tok, axis):
    return lax.broadcasted_iota(jnp.int32, (tok, 1) if axis == 0 else (1, tok), axis)


def carries(info_ref, tok):
    first = info_ref[I_BLK] * tok
    starts = starts_of(info_ref)
    rows = start_at(starts, line(tok, 0) + first)
    return rows == start_at(starts, first - 1), rows == start_at(starts, first + tok - 1)


def visible(low_ref, axis):
    if axis == 0:
        tok = low_ref.shape[0]
        low = low_ref[:, :1]
    else:
        tok = low_ref.shape[1]
        low = low_ref[:1, :]
    t, s = line(tok, axis), line(tok, 1 - axis)
    return (s <= t) & (s >= low)


def same(starts, tok, a, b):
    pa, pb = a * tok + tok - 1, b * tok + tok - 1
    one = (a >= 0) | (b < 0)
    for s in starts:
        one = jnp.logical_and(one, jnp.logical_not(jnp.logical_and(pa < s, s <= pb)))
    return jnp.where(one, 1.0, 0.0).astype(F32)


def stages(n, forward):
    out, m = [], 2
    while m < n:
        r = 2
        out.append((m, r, m * r >= n))
        m *= r
    return out


def coefficients(starts, tok, n, blk, forward):
    link = functools.partial(same, starts, tok)
    core = lax.rem(blk, 2)
    first = blk - core
    one, none = jnp.float32(1.0), jnp.float32(0.0)
    if forward:
        near, inner, outer = core == 0, link(first, first + 1), link(first - 1, first)
    else:
        near, inner, outer = core == 1, link(first - 1, first), link(first, first + 1)
    out = [jnp.where(near, inner, one), jnp.where(near, one, inner)]
    for m, r, last in stages(n, forward):
        low = blk // (m * r) * (m * r)
        digit = lax.rem(blk // m, r)
        for x in range(1, r):
            j = jnp.bitwise_xor(digit, x)
            if forward:
                out.append(jnp.where(j < digit, link(low + (j + 1) * m - 1, first - 1), none))
            else:
                out.append(jnp.where(j > digit, link(first + 1, low + j * m - 1), none))
        if not last:
            for x in range(r):
                j = jnp.bitwise_xor(digit, x)
                if forward:
                    out.append(link(low + (j + 1) * m - 1, low + r * m - 1))
                else:
                    out.append(link(low - 1, low + j * m - 1))
    return out + [jnp.where(near, one, none), outer]


def pair_body(c_ref, mine_ref, got_ref, total_ref):
    a, b = c_ref[0:1, :], c_ref[1:2, :]
    total_ref[...] = (mine_ref[...].astype(F32) * a + got_ref[...].astype(F32) * b).astype(BF16)


def stage_body(row, r, last, begun, c_ref, *refs):
    refs = list(refs)
    others = [refs.pop(0)[...].astype(F32) for _ in range(r - 1)]
    entering = refs.pop(0)[...] if begun else None
    for other in others:
        part = other * c_ref[row:row + 1, :]
        entering = part if entering is None else entering + part
        row += 1
    if not last:
        total_ref, new_total_ref, entering_ref = refs
        entering_ref[...] = entering
        total = total_ref[...].astype(F32) * c_ref[row:row + 1, :]
        for other in others:
            row += 1
            total = total + other * c_ref[row:row + 1, :]
        new_total_ref[...] = total.astype(BF16)
        return
    mine_ref, got_ref, own_ref, away_ref = refs
    near, outer = c_ref[row:row + 1, :], c_ref[row + 1:row + 2, :]
    nearer = mine_ref[...].astype(F32) * near + got_ref[...].astype(F32) * (1.0 - near)
    chained = nearer + outer * entering
    own_ref[...] = (entering * near + chained * (1.0 - near)).astype(BF16)
    away_ref[...] = (chained * near + entering * (1.0 - near)).astype(BF16)


def pair_total(send, keep, coef):
    n = lax.axis_size("ctx")
    got = lax.ppermute(send, "ctx", [(i, i ^ 1) for i in range(n)])
    (total,) = kernel(pair_body, "pair_total", [], [coef, keep, got], [like(keep.shape, BF16)])
    return got, total


def exchange(total, keep, got, coef, forward, beside):
    n = lax.axis_size("ctx")
    swap = [(i, i ^ 1) for i in range(n)]
    half = like(keep.shape, BF16)
    entering, row = [], 2
    for m, r, last in stages(n, forward):
        others = []
        for x in range(1, r):
            pairs = [
                (i, i ^ (x * m)) for i in range(n)
                if not last or ((i // m % r) < (i // m % r ^ x)) == forward
            ]
            others.append(lax.ppermute(total, "ctx", pairs))
        deps = beside.pop(0)(total) if beside else ()
        body = functools.partial(stage_body, row, r, last, bool(entering))
        if last:
            own, away = kernel(
                body, "exchange_last", [], [coef, *others, *entering, keep, got], [half, half], deps
            )
        else:
            total, e = kernel(
                body, "exchange_stage", [], [coef, *others, *entering, total],
                [half, like(keep.shape, F32)], deps,
            )
            entering = [e]
            row += 2 * r - 1
    return own, lax.ppermute(away, "ctx", swap)


TILE = 256
ROWS = 32
C_CORE, C_END = ROWS - 1, ROWS - 2


def put_states(states, c_ref, keep_ref, send_ref):
    half = len(states) // 2
    core0 = c_ref[C_CORE:C_CORE + 1, :] > 0.5
    for i in range(half):
        keep_ref[i] = jnp.where(core0, states[i], states[i + half]).astype(BF16)
        send_ref[i] = jnp.where(core0, states[i + half], states[i]).astype(BF16)


def setup_body(n, tok, info_ref, coef_ref, coefb_ref, cin_ref, cout_ref, low_ref, low_t_ref):
    blk, core = info_ref[I_BLK], info_ref[I_CORE]
    starts = starts_of(info_ref)
    for ref, forward in ((coef_ref, True), (coefb_ref, False)):
        ref[...] = jnp.zeros_like(ref)
        for i, c in enumerate(coefficients(starts, tok, n, blk, forward)):
            ref[i:i + 1, :] = jnp.full((1, DH), c, F32)
        ref[C_CORE:C_CORE + 1, :] = jnp.full((1, DH), jnp.where(core == 0, 1.0, 0.0), F32)
        end = jnp.logical_or(info_ref[I_Z] == 0, info_ref[I_Z] == 3)
        ref[C_END:C_END + 1, :] = jnp.full((1, DH), jnp.where(end, 1.0, 0.0), F32)
    cin, cout = carries(info_ref, tok)
    cin_ref[...] = jnp.broadcast_to(jnp.where(cin, 1.0, 0.0), cin_ref.shape)
    cout_ref[...] = jnp.broadcast_to(jnp.where(cout, 1.0, 0.0), cout_ref.shape)
    first = blk * tok
    for ref, axis in ((low_ref, 0), (low_t_ref, 1)):
        low = start_at(starts, line(tok, axis) + first) - first
        ref[...] = jnp.broadcast_to(low, ref.shape)


def states_body(c_ref, cout_ref, k_ref, v_ref, send_ref, keep_ref):
    zero = jnp.zeros((), BF16)
    cout = cout_ref[...] > 0.5
    states = []
    for h in range(k_ref.shape[1] // DH):
        kept = jnp.where(cout, k_ref[:, head(h)], zero)
        states.append(dot(kept, v_ref[:, head(h)], 0, 0))
    put_states(states, c_ref, keep_ref, send_ref)


def intra_body(low_ref, q_ref, k_ref, v_ref, out_ref):
    mask = visible(low_ref, 0)
    for h in range(q_ref.shape[1] // DH):
        s = dot(q_ref[:, head(h)], k_ref[:, head(h)], 1, 1)
        s = jnp.where(mask, s, 0.0).astype(BF16)
        out_ref[:, head(h)] = dot(s, v_ref[:, head(h)], 1, 0)


def pick(c_ref, own_ref, back_ref, h):
    half = own_ref.shape[0]
    core0 = c_ref[C_CORE:C_CORE + 1, :] > 0.5
    a, b = own_ref[h % half].astype(F32), back_ref[h % half].astype(F32)
    return (jnp.where(core0, a, b) if h < half else jnp.where(core0, b, a)).astype(BF16)


def norm_body(c_ref, cin_ref, q_ref, own_ref, back_ref, a_ref, normed_ref, inv_ref, n_ref):
    wide = q_ref.shape[1]
    for h in range(wide // DH):
        inter = dot(q_ref[:, head(h)], pick(c_ref, own_ref, back_ref, h), 1, 0)
        att = a_ref[:, head(h)] + cin_ref[...] * inter
        inv = lax.rsqrt(jnp.mean(att * att, axis=-1, keepdims=True) + EPS)
        normed = att * inv
        inv_ref[:, head(h)] = jnp.broadcast_to(inv, att.shape)
        normed_ref[:, head(h)] = normed
        n_ref[:, head(h)] = normed.astype(BF16)


def columns(info_ref, block, width):
    return pl.multiple_of(jnp.bitwise_xor(info_ref[I_Z], block) * width, width)


def project_body(block, info_ref, n_ref, w_ref, out_ref):
    width = out_ref.shape[1]
    base = columns(info_ref, block, width)
    for i in range(width // TILE):
        at = pl.multiple_of(base + i * TILE, TILE)
        out_ref[:, i * TILE:(i + 1) * TILE] = dot(
            n_ref[...], w_ref[:, pl.ds(at, TILE)], 1, 0
        ).astype(BF16)


def back_body(blocks, based, info_ref, w_ref, *refs):
    out_ref = refs[-1]
    feats = out_ref.shape[1]
    for i in range(feats // TILE):
        rows = slice(i * TILE, (i + 1) * TILE)
        acc = refs[-2][:, rows] if based else None
        for block, g_ref in zip(blocks, refs, strict=False):
            width = g_ref.shape[1]
            at = columns(info_ref, block, width)
            part = dot(g_ref[...], w_ref[rows, pl.ds(at, width)], 1, 1)
            acc = part if acc is None else acc + part
        out_ref[:, rows] = acc


def att_grad_body(block, info_ref, w_ref, x_ref, base_ref, normed_ref, inv_ref, q_ref, c_ref, cin_ref, ag_ref, send_ref, keep_ref):
    wide = q_ref.shape[1]
    width = x_ref.shape[1]
    at = columns(info_ref, block, width)
    zero = jnp.zeros((), BF16)
    cin = cin_ref[...] > 0.5
    states = []
    for i in range(wide // TILE):
        rows = slice(i * TILE, (i + 1) * TILE)
        ng2 = base_ref[:, rows] + dot(x_ref[...], w_ref[rows, pl.ds(at, width)], 1, 1)
        for j in range(TILE // DH):
            h = i * (TILE // DH) + j
            ng, normed = ng2[:, head(j)], normed_ref[:, head(h)]
            proj = jnp.mean(ng * normed, axis=-1, keepdims=True)
            ag = ((ng - normed * proj) * inv_ref[:, head(h)]).astype(BF16)
            ag_ref[:, head(h)] = ag
            kept = jnp.where(cin, q_ref[:, head(h)], zero)
            states.append(dot(kept, ag, 0, 0))
    put_states(states, c_ref, keep_ref, send_ref)


def query_grad_body(low_ref, c_ref, cin_ref, k_ref, v_ref, ag_ref, own_ref, back_ref, qg_ref, mark_ref):
    mask = visible(low_ref, 0)
    mark_ref[...] = jnp.zeros_like(mark_ref)
    for h in range(k_ref.shape[1] // DH):
        ag = ag_ref[:, head(h)]
        inter = dot(ag, pick(c_ref, own_ref, back_ref, h), 1, 1)
        g = jnp.where(mask, dot(ag, v_ref[:, head(h)], 1, 1), 0.0).astype(BF16)
        qg_ref[:, head(h)] = (dot(g, k_ref[:, head(h)], 1, 0) + cin_ref[...] * inter).astype(BF16)


def key_value_body(low_t_ref, q_ref, k_ref, v_ref, ag_ref, kg_ref, vg_ref):
    mask = visible(low_t_ref, 1)
    for h in range(q_ref.shape[1] // DH):
        q, k, v, ag = (r[:, head(h)] for r in (q_ref, k_ref, v_ref, ag_ref))
        st = jnp.where(mask, dot(k, q, 1, 1), 0.0).astype(BF16)
        vg_ref[:, head(h)] = dot(st, ag, 1, 0)
        gt = jnp.where(mask, dot(v, ag, 1, 1), 0.0).astype(BF16)
        kg_ref[:, head(h)] = dot(gt, q, 1, 0)


def last_body(c_ref, cout_ref, k_ref, v_ref, own_ref, back_ref, kp_ref, vp_ref, kg_ref, vg_ref, mark_ref):
    mark_ref[...] = jnp.zeros_like(mark_ref)
    wide = k_ref.shape[1]
    cout = cout_ref[...]
    for h in range(wide // DH):
        leaving = pick(c_ref, own_ref, back_ref, h)
        kg = cout * dot(v_ref[:, head(h)], leaving, 1, 1)
        vg = cout * dot(k_ref[:, head(h)], leaving, 1, 0)
        kg_ref[:, head(h)] = (kp_ref[:, head(h)] + kg).astype(BF16)
        vg_ref[:, head(h)] = (vp_ref[:, head(h)] + vg).astype(BF16)


def sum_body(*refs):
    total = refs[0][...].astype(F32)
    for r in refs[1:-1]:
        total = total + r[...].astype(F32)
    refs[-1][...] = total.astype(BF16)


def at_end(c_ref):
    return c_ref[C_END:C_END + 1, :].astype(BF16)


def end_body(c_ref, a_ref, b_ref, out_ref):
    end = at_end(c_ref)
    for i in range(out_ref.shape[1] // DH):
        out_ref[:, head(i)] = a_ref[:, head(i)] * end + b_ref[:, head(i)]


def turn_body(c_ref, n2_ref, p2_ref, i2_ref, s2_ref, n3_ref):
    s2_ref[...] = p2_ref[...] + n2_ref[...]
    end_body(c_ref, p2_ref, i2_ref, n3_ref)


def turn_again_body(n3_ref, i3_ref, p3_ref, p1_ref, s3_ref, s1_ref):
    s3_ref[...] = p3_ref[...] + n3_ref[...]
    s1_ref[...] = p1_ref[...] + i3_ref[...]


def shards(q, k, v, lens, w, grad):
    tok, width = grad.shape
    feats = w.shape[0]
    heads = feats // DH
    half = heads // 2
    n = lax.axis_size("ctx")
    blk = lax.axis_index("ctx").astype(jnp.int32)
    z = lax.axis_index("head").astype(jnp.int32)
    info = jnp.concatenate([jnp.stack([blk, blk % 2, z]), lens])
    part = like((tok, width), BF16)
    wide_b, wide_f = like((tok, feats), BF16), like((tok, feats), F32)
    state = like((half, DH, DH), BF16)
    lanes = like((tok, DH), F32)
    table = like((ROWS, DH), F32)

    def project(block, name, deps=()):
        body = functools.partial(project_body, block)
        return kernel(body, name, [info], [normed, w], [part], deps)[0]

    def back_project(blocks, name, grads, base=None, deps=()):
        body = functools.partial(back_body, blocks, base is not None)
        return kernel(body, name, [info], [w, *grads] + ([] if base is None else [base]), [wide_f], deps)[0]

    neighbours = [(0, 1), (1, 0), (2, 3), (3, 2)]
    inner = [(1, 2), (2, 1)]
    g1 = lax.ppermute(grad, "head", neighbours)
    g3_inner = lax.ppermute(grad, "head", inner)
    coef, coefb, cin, cout, low, low_t = kernel(
        functools.partial(setup_body, n, tok), "setup", [info], [],
        [table, table, lanes, lanes, like((tok, DH), jnp.int32), like((8, tok), jnp.int32)],
    )
    send, keep = kernel(states_body, "local_states", [], [coef, cout, k, v], [state, state])
    got, total = pair_total(send, keep, coef)
    (inside,) = kernel(intra_body, "intra", [], [low, q, k, v], [wide_f], [total])
    base = back_project([0], "back_own", [grad], None, [inside])
    own, other = exchange(total, keep, got, coef, True, [lambda _: [inside], lambda _: [base]])
    normed_f, inv, normed = kernel(
        norm_body, "normalise", [], [coef, cin, q, own, other, inside], [wide_f, wide_f, wide_b]
    )
    p3 = project(3, "project_3")
    g1, g3_inner, _ = lax.optimization_barrier((g1, g3_inner, p3))
    (n2,) = kernel(end_body, "pick", [], [coef, p3, g3_inner], [part], [g1])
    n2 = lax.ppermute(n2, "head", neighbours)
    i2 = lax.ppermute(g1, "head", inner)
    p2 = project(2, "project_2", [p3])
    p1 = project(1, "project_1", [p2])
    p0 = project(0, "project_0", [p1])
    base = back_project([1], "back_1", [g1], base, [p0])
    s2, n3 = kernel(turn_body, "turn", [], [coef, n2, p2, i2], [part, part], [base])
    i3 = lax.ppermute(s2, "head", inner)
    n3 = lax.ppermute(n3, "head", neighbours)
    (g2,) = kernel(end_body, "pick", [], [coef, n2, i2], [part], [s2])
    base = back_project([2], "back_2", [g2], base)
    s3, s1 = kernel(turn_again_body, "turn", [], [n3, i3, p3, p1], [part, part], [base])
    n4 = lax.ppermute(s1, "head", neighbours)
    i4 = lax.ppermute(s3, "head", inner)
    (g3,) = kernel(end_body, "pick", [], [coef, n3, g3_inner], [part], [s1])
    ag, gsend, gkeep = kernel(
        functools.partial(att_grad_body, 3), "attended_grads", [info],
        [w, g3, base, normed_f, inv, q, coef, cin], [wide_b, state, state], [s1],
    )
    ggot, gtotal = pair_total(gsend, gkeep, coefb)
    grads = []

    def beside_first(sent):
        grads.extend(kernel(
            query_grad_body, "query_grad", [], [low, coef, cin, k, v, ag, own, other],
            [wide_b, like((8, DH), F32)], [sent],
        ))
        return grads[1:2]

    def beside_second(sent):
        grads.extend(kernel(
            key_value_body, "key_value_grads", [], [low_t, q, k, v, ag], [wide_f, wide_f], [sent]
        ))
        return grads[2:3]

    leaving, leaving_other = exchange(gtotal, gkeep, ggot, coefb, False, [beside_first, beside_second])
    query_grad, _, kp, vp = grads
    key_grad, value_grad, mark = kernel(
        last_body, "last_grads", [], [coef, cout, k, v, leaving, leaving_other, kp, vp],
        [wide_b, wide_b, like((8, DH), F32)],
    )
    (mixed,) = kernel(sum_body, "turn", [], [p0, n4], [part], [mark])
    (mixed,) = kernel(sum_body, "mixed", [], [mixed, i4], [part])
    return mixed, query_grad, key_grad, value_grad


def solution(mesh):
    return jax.shard_map(
        shards,
        mesh=mesh,
        in_specs=(
            P("ctx", "head"),
            P("ctx", "head"),
            P("ctx", "head"),
            P(),
            P("head", None),
            P("ctx", "head"),
        ),
        out_specs=(P("ctx", "head"), P("ctx", "head"), P("ctx", "head"), P("ctx", "head")),
        check_vma=False,
    )
```

```python
import functools

import jax
import jax.numpy as jnp
from jax import lax
from jax.experimental import pallas as pl
from jax.experimental.pallas import tpu as pltpu
from jax.sharding import PartitionSpec as P

DH = 128
EPS = 1e-06
F32 = jnp.float32
BF16 = jnp.bfloat16
MIB = 1024 * 1024

RATE = 10**8
MICROSECONDS = {
    "setup": 100.0, "local_states": 0.8, "intra": 3.0, "back_own": 1.8, "pair_total": 0.1, "exchange_stage": 0.1,
    "exchange_last": 0.1, "normalise": 0.9, "project_3": 1.8, "project_2": 1.8, "project_1": 1.8,
    "project_0": 1.8, "back_1": 1.8, "pick": 0.3, "turn": 0.5, "back_2": 1.8, "attended_grads": 4.1,
    "query_grad": 0.01, "key_value_grads": 0.01, "last_grads": 0.01, "mixed": 1.3,
}

I_BLK, I_CORE, I_Z, I_DOCS = 0, 1, 2, 3


def kernel(body, name, smem, ins, outs, deps=(), spare=8):
    n, n_dep = len(smem) + len(ins), len(deps)

    def inner(*refs):
        body(*refs[:n], *refs[n + n_dep:])

    size = sum(a.size * a.dtype.itemsize for a in list(ins) + list(outs))
    spec = lambda space: pl.BlockSpec(memory_space=space)
    return pl.pallas_call(
        inner,
        name=name,
        in_specs=[spec(pltpu.SMEM)] * len(smem) + [spec(pltpu.VMEM)] * len(ins) + [spec(pl.ANY)] * n_dep,
        out_specs=[spec(pltpu.VMEM)] * len(outs),
        out_shape=list(outs),
        compiler_params=pltpu.CompilerParams(vmem_limit_bytes=size + spare * MIB),
        cost_estimate=pl.CostEstimate(
            flops=int(MICROSECONDS[name] * RATE), bytes_accessed=0, transcendentals=0
        ),
    )(*smem, *ins, *deps)


def like(shape, dtype):
    return jax.ShapeDtypeStruct(shape, dtype)


def dot(a, b, ca, cb):
    return lax.dot_general(a, b, (((ca,), (cb,)), ((), ())), preferred_element_type=F32)


def head(h):
    return slice(h * DH, (h + 1) * DH)


def starts_of(info_ref):
    out, at = [], jnp.int32(0)
    for j in range(I_DOCS, info_ref.shape[0] - 1):
        at = at + info_ref[j]
        out.append(at)
    return out


def start_at(starts, p):
    best = jnp.minimum(p, 0)
    best = jnp.maximum(best, -1)
    for s in starts:
        best = jnp.where(p >= s, s, best)
    return best


def line(tok, axis):
    return lax.broadcasted_iota(jnp.int32, (tok, 1) if axis == 0 else (1, tok), axis)


def carries(info_ref, tok):
    first = info_ref[I_BLK] * tok
    starts = starts_of(info_ref)
    rows = start_at(starts, line(tok, 0) + first)
    return rows == start_at(starts, first - 1), rows == start_at(starts, first + tok - 1)


def visible(low_ref, axis):
    if axis == 0:
        tok = low_ref.shape[0]
        low = low_ref[:, :1]
    else:
        tok = low_ref.shape[1]
        low = low_ref[:1, :]
    t, s = line(tok, axis), line(tok, 1 - axis)
    return (s <= t) & (s >= low)


def same(starts, tok, a, b):
    pa, pb = a * tok + tok - 1, b * tok + tok - 1
    one = (a >= 0) | (b < 0)
    for s in starts:
        one = jnp.logical_and(one, jnp.logical_not(jnp.logical_and(pa < s, s <= pb)))
    return jnp.where(one, 1.0, 0.0).astype(F32)


def stages(n, forward):
    out, m = [], 2
    while m < n:
        r = 2
        out.append((m, r, m * r >= n))
        m *= r
    return out


def coefficients(starts, tok, n, blk, forward):
    link = functools.partial(same, starts, tok)
    core = lax.rem(blk, 2)
    first = blk - core
    one, none = jnp.float32(1.0), jnp.float32(0.0)
    if forward:
        near, inner, outer = core == 0, link(first, first + 1), link(first - 1, first)
    else:
        near, inner, outer = core == 1, link(first - 1, first), link(first, first + 1)
    out = [jnp.where(near, inner, one), jnp.where(near, one, inner)]
    for m, r, last in stages(n, forward):
        low = blk // (m * r) * (m * r)
        digit = lax.rem(blk // m, r)
        for x in range(1, r):
            j = jnp.bitwise_xor(digit, x)
            if forward:
                out.append(jnp.where(j < digit, link(low + (j + 1) * m - 1, first - 1), none))
            else:
                out.append(jnp.where(j > digit, link(first + 1, low + j * m - 1), none))
        if not last:
            for x in range(r):
                j = jnp.bitwise_xor(digit, x)
                if forward:
                    out.append(link(low + (j + 1) * m - 1, low + r * m - 1))
                else:
                    out.append(link(low - 1, low + j * m - 1))
    return out + [jnp.where(near, one, none), outer]


def pair_body(c_ref, mine_ref, got_ref, total_ref):
    a, b = c_ref[0:1, :], c_ref[1:2, :]
    total_ref[...] = (mine_ref[...].astype(F32) * a + got_ref[...].astype(F32) * b).astype(BF16)


def stage_body(row, r, last, begun, c_ref, *refs):
    refs = list(refs)
    others = [refs.pop(0)[...].astype(F32) for _ in range(r - 1)]
    entering = refs.pop(0)[...] if begun else None
    for other in others:
        part = other * c_ref[row:row + 1, :]
        entering = part if entering is None else entering + part
        row += 1
    if not last:
        total_ref, new_total_ref, entering_ref = refs
        entering_ref[...] = entering
        total = total_ref[...].astype(F32) * c_ref[row:row + 1, :]
        for other in others:
            row += 1
            total = total + other * c_ref[row:row + 1, :]
        new_total_ref[...] = total.astype(BF16)
        return
    mine_ref, got_ref, own_ref, away_ref = refs
    near, outer = c_ref[row:row + 1, :], c_ref[row + 1:row + 2, :]
    nearer = mine_ref[...].astype(F32) * near + got_ref[...].astype(F32) * (1.0 - near)
    chained = nearer + outer * entering
    own_ref[...] = (entering * near + chained * (1.0 - near)).astype(BF16)
    away_ref[...] = (chained * near + entering * (1.0 - near)).astype(BF16)


def pair_total(send, keep, coef):
    n = lax.axis_size("ctx")
    got = lax.ppermute(send, "ctx", [(i, i ^ 1) for i in range(n)])
    (total,) = kernel(pair_body, "pair_total", [], [coef, keep, got], [like(keep.shape, BF16)])
    return got, total


def exchange(total, keep, got, coef, forward, beside):
    n = lax.axis_size("ctx")
    swap = [(i, i ^ 1) for i in range(n)]
    half = like(keep.shape, BF16)
    entering, row = [], 2
    for m, r, last in stages(n, forward):
        others = []
        for x in range(1, r):
            pairs = [
                (i, i ^ (x * m)) for i in range(n)
                if not last or ((i // m % r) < (i // m % r ^ x)) == forward
            ]
            others.append(lax.ppermute(total, "ctx", pairs))
        deps = beside.pop(0)(total) if beside else ()
        body = functools.partial(stage_body, row, r, last, bool(entering))
        if last:
            own, away = kernel(
                body, "exchange_last", [], [coef, *others, *entering, keep, got], [half, half], deps
            )
        else:
            total, e = kernel(
                body, "exchange_stage", [], [coef, *others, *entering, total],
                [half, like(keep.shape, F32)], deps,
            )
            entering = [e]
            row += 2 * r - 1
    return own, lax.ppermute(away, "ctx", swap)


TILE = 256
ROWS = 32
C_CORE, C_END = ROWS - 1, ROWS - 2


def put_states(states, c_ref, keep_ref, send_ref):
    half = len(states) // 2
    core0 = c_ref[C_CORE:C_CORE + 1, :] > 0.5
    for i in range(half):
        keep_ref[i] = jnp.where(core0, states[i], states[i + half]).astype(BF16)
        send_ref[i] = jnp.where(core0, states[i + half], states[i]).astype(BF16)


def setup_body(n, tok, info_ref, coef_ref, coefb_ref, cin_ref, cout_ref, low_ref, low_t_ref):
    blk, core = info_ref[I_BLK], info_ref[I_CORE]
    starts = starts_of(info_ref)
    for ref, forward in ((coef_ref, True), (coefb_ref, False)):
        ref[...] = jnp.zeros_like(ref)
        for i, c in enumerate(coefficients(starts, tok, n, blk, forward)):
            ref[i:i + 1, :] = jnp.full((1, DH), c, F32)
        ref[C_CORE:C_CORE + 1, :] = jnp.full((1, DH), jnp.where(core == 0, 1.0, 0.0), F32)
        end = jnp.logical_or(info_ref[I_Z] == 0, info_ref[I_Z] == 3)
        ref[C_END:C_END + 1, :] = jnp.full((1, DH), jnp.where(end, 1.0, 0.0), F32)
    cin, cout = carries(info_ref, tok)
    cin_ref[...] = jnp.broadcast_to(jnp.where(cin, 1.0, 0.0), cin_ref.shape)
    cout_ref[...] = jnp.broadcast_to(jnp.where(cout, 1.0, 0.0), cout_ref.shape)
    first = blk * tok
    for ref, axis in ((low_ref, 0), (low_t_ref, 1)):
        low = start_at(starts, line(tok, axis) + first) - first
        ref[...] = jnp.broadcast_to(low, ref.shape)


def states_body(c_ref, cout_ref, k_ref, v_ref, send_ref, keep_ref):
    zero = jnp.zeros((), BF16)
    cout = cout_ref[...] > 0.5
    states = []
    for h in range(k_ref.shape[1] // DH):
        kept = jnp.where(cout, k_ref[:, head(h)], zero)
        states.append(dot(kept, v_ref[:, head(h)], 0, 0))
    put_states(states, c_ref, keep_ref, send_ref)


def intra_body(low_ref, q_ref, k_ref, v_ref, out_ref):
    mask = visible(low_ref, 0)
    for h in range(q_ref.shape[1] // DH):
        s = dot(q_ref[:, head(h)], k_ref[:, head(h)], 1, 1)
        s = jnp.where(mask, s, 0.0).astype(BF16)
        out_ref[:, head(h)] = dot(s, v_ref[:, head(h)], 1, 0)


def pick(c_ref, own_ref, back_ref, h):
    half = own_ref.shape[0]
    core0 = c_ref[C_CORE:C_CORE + 1, :] > 0.5
    a, b = own_ref[h % half].astype(F32), back_ref[h % half].astype(F32)
    return (jnp.where(core0, a, b) if h < half else jnp.where(core0, b, a)).astype(BF16)


def norm_body(c_ref, cin_ref, q_ref, own_ref, back_ref, a_ref, normed_ref, inv_ref, n_ref):
    wide = q_ref.shape[1]
    for h in range(wide // DH):
        inter = dot(q_ref[:, head(h)], pick(c_ref, own_ref, back_ref, h), 1, 0)
        att = a_ref[:, head(h)] + cin_ref[...] * inter
        inv = lax.rsqrt(jnp.mean(att * att, axis=-1, keepdims=True) + EPS)
        normed = att * inv
        inv_ref[:, head(h)] = jnp.broadcast_to(inv, att.shape)
        normed_ref[:, head(h)] = normed
        n_ref[:, head(h)] = normed.astype(BF16)


def columns(info_ref, block, width):
    return pl.multiple_of(jnp.bitwise_xor(info_ref[I_Z], block) * width, width)


def project_body(block, info_ref, n_ref, w_ref, out_ref):
    width = out_ref.shape[1]
    base = columns(info_ref, block, width)
    for i in range(width // TILE):
        at = pl.multiple_of(base + i * TILE, TILE)
        out_ref[:, i * TILE:(i + 1) * TILE] = dot(
            n_ref[...], w_ref[:, pl.ds(at, TILE)], 1, 0
        ).astype(BF16)


def back_body(blocks, based, info_ref, w_ref, *refs):
    out_ref = refs[-1]
    feats = out_ref.shape[1]
    for i in range(feats // TILE):
        rows = slice(i * TILE, (i + 1) * TILE)
        acc = refs[-2][:, rows] if based else None
        for block, g_ref in zip(blocks, refs, strict=False):
            width = g_ref.shape[1]
            at = columns(info_ref, block, width)
            part = dot(g_ref[...], w_ref[rows, pl.ds(at, width)], 1, 1)
            acc = part if acc is None else acc + part
        out_ref[:, rows] = acc


def att_grad_body(block, info_ref, w_ref, x_ref, base_ref, normed_ref, inv_ref, q_ref, c_ref, cin_ref, ag_ref, send_ref, keep_ref):
    wide = q_ref.shape[1]
    width = x_ref.shape[1]
    at = columns(info_ref, block, width)
    zero = jnp.zeros((), BF16)
    cin = cin_ref[...] > 0.5
    states = []
    for i in range(wide // TILE):
        rows = slice(i * TILE, (i + 1) * TILE)
        ng2 = base_ref[:, rows] + dot(x_ref[...], w_ref[rows, pl.ds(at, width)], 1, 1)
        for j in range(TILE // DH):
            h = i * (TILE // DH) + j
            ng, normed = ng2[:, head(j)], normed_ref[:, head(h)]
            proj = jnp.mean(ng * normed, axis=-1, keepdims=True)
            ag = ((ng - normed * proj) * inv_ref[:, head(h)]).astype(BF16)
            ag_ref[:, head(h)] = ag
            kept = jnp.where(cin, q_ref[:, head(h)], zero)
            states.append(dot(kept, ag, 0, 0))
    put_states(states, c_ref, keep_ref, send_ref)


def query_grad_body(low_ref, c_ref, cin_ref, k_ref, v_ref, ag_ref, own_ref, back_ref, qg_ref, mark_ref):
    mask = visible(low_ref, 0)
    mark_ref[...] = jnp.zeros_like(mark_ref)
    for h in range(k_ref.shape[1] // DH):
        ag = ag_ref[:, head(h)]
        inter = dot(ag, pick(c_ref, own_ref, back_ref, h), 1, 1)
        g = jnp.where(mask, dot(ag, v_ref[:, head(h)], 1, 1), 0.0).astype(BF16)
        qg_ref[:, head(h)] = (dot(g, k_ref[:, head(h)], 1, 0) + cin_ref[...] * inter).astype(BF16)


def key_value_body(low_t_ref, q_ref, k_ref, v_ref, ag_ref, kg_ref, vg_ref):
    mask = visible(low_t_ref, 1)
    for h in range(q_ref.shape[1] // DH):
        q, k, v, ag = (r[:, head(h)] for r in (q_ref, k_ref, v_ref, ag_ref))
        st = jnp.where(mask, dot(k, q, 1, 1), 0.0).astype(BF16)
        vg_ref[:, head(h)] = dot(st, ag, 1, 0)
        gt = jnp.where(mask, dot(v, ag, 1, 1), 0.0).astype(BF16)
        kg_ref[:, head(h)] = dot(gt, q, 1, 0)


def last_body(c_ref, cout_ref, k_ref, v_ref, own_ref, back_ref, kp_ref, vp_ref, kg_ref, vg_ref, mark_ref):
    mark_ref[...] = jnp.zeros_like(mark_ref)
    wide = k_ref.shape[1]
    cout = cout_ref[...]
    for h in range(wide // DH):
        leaving = pick(c_ref, own_ref, back_ref, h)
        kg = cout * dot(v_ref[:, head(h)], leaving, 1, 1)
        vg = cout * dot(k_ref[:, head(h)], leaving, 1, 0)
        kg_ref[:, head(h)] = (kp_ref[:, head(h)] + kg).astype(BF16)
        vg_ref[:, head(h)] = (vp_ref[:, head(h)] + vg).astype(BF16)


def sum_body(*refs):
    total = refs[0][...].astype(F32)
    for r in refs[1:-1]:
        total = total + r[...].astype(F32)
    refs[-1][...] = total.astype(BF16)


def at_end(c_ref):
    return c_ref[C_END:C_END + 1, :].astype(BF16)


def end_body(c_ref, a_ref, b_ref, out_ref):
    end = at_end(c_ref)
    for i in range(out_ref.shape[1] // DH):
        out_ref[:, head(i)] = a_ref[:, head(i)] * end + b_ref[:, head(i)]


def first_body(c_ref, g1_ref, p3_ref, g3_ref, *out_refs):
    r0 = 0
    for n_ref, i_ref in zip(out_refs[::2], out_refs[1::2], strict=True):
        rows = slice(r0, r0 + n_ref.shape[0])
        i_ref[...] = g1_ref[rows, :]
        end_body(c_ref, p3_ref.at[rows, :], g3_ref.at[rows, :], n_ref)
        r0 = rows.stop


def ends_body(c_ref, *refs):
    out_ref = refs[-1]
    r0 = 0
    for a_ref, b_ref in zip(refs[:-1:2], refs[1:-1:2], strict=True):
        rows = slice(r0, r0 + a_ref.shape[0])
        end_body(c_ref, a_ref, b_ref, out_ref.at[rows, :])
        r0 = rows.stop


def ends_whole_body(c_ref, a0_ref, a1_ref, b_ref, out_ref):
    r1 = a0_ref.shape[0]
    end_body(c_ref, a0_ref, b_ref.at[:r1, :], out_ref.at[:r1, :])
    end_body(c_ref, a1_ref, b_ref.at[r1:, :], out_ref.at[r1:, :])


def turn_body(rows, c_ref, n2_ref, p2_ref, i2_ref, s2_ref, n3_ref):
    s2_ref[...] = p2_ref[rows, :] + n2_ref[...]
    end_body(c_ref, p2_ref.at[rows, :], i2_ref, n3_ref)


def turn_again_body(rows, n3_ref, i3_ref, p3_ref, p1_ref, s3_ref, s1_ref):
    s3_ref[...] = p3_ref[rows, :] + n3_ref[...]
    s1_ref[...] = p1_ref[rows, :] + i3_ref[...]


def mixed_body(p_ref, *refs):
    out_ref = refs[-1]
    r0 = 0
    for a_ref, b_ref in zip(refs[:-1:2], refs[1:-1:2], strict=True):
        rows = slice(r0, r0 + a_ref.shape[0])
        total = p_ref[rows, :].astype(F32) + a_ref[...].astype(F32) + b_ref[...].astype(F32)
        out_ref[rows, :] = total.astype(BF16)
        r0 = rows.stop


def shards(q, k, v, lens, w, grad):
    tok, width = grad.shape
    feats = w.shape[0]
    heads = feats // DH
    half = heads // 2
    n = lax.axis_size("ctx")
    blk = lax.axis_index("ctx").astype(jnp.int32)
    z = lax.axis_index("head").astype(jnp.int32)
    info = jnp.concatenate([jnp.stack([blk, blk % 2, z]), lens])
    part = like((tok, width), BF16)
    wide_b, wide_f = like((tok, feats), BF16), like((tok, feats), F32)
    state = like((half, DH, DH), BF16)
    lanes = like((tok, DH), F32)
    table = like((ROWS, DH), F32)

    def project(block, name, deps=()):
        body = functools.partial(project_body, block)
        return kernel(body, name, [info], [normed, w], [part], deps)[0]

    def back_project(blocks, name, grads, base=None, deps=()):
        body = functools.partial(back_body, blocks, base is not None)
        return kernel(body, name, [info], [w, *grads] + ([] if base is None else [base]), [wide_f], deps)[0]

    neighbours = [(0, 1), (1, 0), (2, 3), (3, 2)]
    inner = [(1, 2), (2, 1)]
    g1 = lax.ppermute(grad, "head", neighbours)
    g3_inner = lax.ppermute(grad, "head", inner)
    coef, coefb, cin, cout, low, low_t = kernel(
        functools.partial(setup_body, n, tok), "setup", [info], [],
        [table, table, lanes, lanes, like((tok, DH), jnp.int32), like((8, tok), jnp.int32)],
    )
    send, keep = kernel(states_body, "local_states", [], [coef, cout, k, v], [state, state])
    got, total = pair_total(send, keep, coef)
    (inside,) = kernel(intra_body, "intra", [], [low, q, k, v], [wide_f], [total])
    base = back_project([0], "back_own", [grad], None, [inside])
    own, other = exchange(total, keep, got, coef, True, [lambda _: [inside], lambda _: [base]])
    normed_f, inv, normed = kernel(
        norm_body, "normalise", [], [coef, cin, q, own, other, inside], [wide_f, wide_f, wide_b]
    )
    lot = like((tok // 2, width), BF16)
    rows = [slice(0, tok // 2), slice(tok // 2, tok)]

    def both(arrays, kind):
        return [lax.ppermute(a, "head", kind) for a in arrays]

    def turn(h, deps):
        return kernel(functools.partial(turn_body, rows[h]), "turn", [], [coef, n2[h], p2, i2[h]], [lot, lot], deps)

    def turn_again(h, deps):
        return kernel(functools.partial(turn_again_body, rows[h]), "turn", [], [n3[h], i3[h], p3, p1], [lot, lot], deps)

    p3 = project(3, "project_3")
    g1, g3_inner, _ = lax.optimization_barrier((g1, g3_inner, p3))
    n2a, i2a, n2b, i2b = kernel(first_body, "pick", [], [coef, g1, p3, g3_inner], [lot] * 4)
    n2a, i2a = lax.ppermute(n2a, "head", neighbours), lax.ppermute(i2a, "head", inner)
    n2b, i2b = lax.ppermute(n2b, "head", neighbours), lax.ppermute(i2b, "head", inner)
    n2, i2 = [n2a, n2b], [i2a, i2b]
    p2 = project(2, "project_2", [p3])
    s2a, n3a = turn(0, [])
    i3a, n3a = lax.ppermute(s2a, "head", inner), lax.ppermute(n3a, "head", neighbours)
    p1 = project(1, "project_1", [s2a])
    p0 = project(0, "project_0", [p1])
    base = back_project([1], "back_1", [g1], base, [p0])
    s2b, n3b = turn(1, [base])
    i3b, n3b = lax.ppermute(s2b, "head", inner), lax.ppermute(n3b, "head", neighbours)
    n3, i3 = [n3a, n3b], [i3a, i3b]
    (g2,) = kernel(ends_body, "pick", [], [coef, n2a, i2a, n2b, i2b], [part], [s2b])
    base = back_project([2], "back_2", [g2], base)
    s3a, s1a = turn_again(0, [base])
    n4a, i4a = lax.ppermute(s1a, "head", neighbours), lax.ppermute(s3a, "head", inner)
    (g3,) = kernel(ends_whole_body, "pick", [], [coef, n3a, n3b, g3_inner], [part], [s1a])
    ag, gsend, gkeep = kernel(
        functools.partial(att_grad_body, 3), "attended_grads", [info],
        [w, g3, base, normed_f, inv, q, coef, cin], [wide_b, state, state],
    )
    s3b, s1b = turn_again(1, [gsend])
    n4b, i4b = lax.ppermute(s1b, "head", neighbours), lax.ppermute(s3b, "head", inner)
    ggot, gtotal = pair_total(gsend, gkeep, coefb)
    grads = []

    def beside_first(sent):
        grads.extend(kernel(
            query_grad_body, "query_grad", [], [low, coef, cin, k, v, ag, own, other],
            [wide_b, like((8, DH), F32)], [sent],
        ))
        return grads[1:2]

    def beside_second(sent):
        grads.extend(kernel(
            key_value_body, "key_value_grads", [], [low_t, q, k, v, ag], [wide_f, wide_f], [sent]
        ))
        return grads[2:3]

    leaving, leaving_other = exchange(gtotal, gkeep, ggot, coefb, False, [beside_first, beside_second])
    query_grad, _, kp, vp = grads
    key_grad, value_grad, mark = kernel(
        last_body, "last_grads", [], [coef, cout, k, v, leaving, leaving_other, kp, vp],
        [wide_b, wide_b, like((8, DH), F32)],
    )
    (mixed,) = kernel(mixed_body, "mixed", [], [p0, n4a, i4a, n4b, i4b], [part], [mark])
    return mixed, query_grad, key_grad, value_grad


def solution(mesh):
    return jax.shard_map(
        shards,
        mesh=mesh,
        in_specs=(
            P("ctx", "head"),
            P("ctx", "head"),
            P("ctx", "head"),
            P(),
            P("head", None),
            P("ctx", "head"),
        ),
        out_specs=(P("ctx", "head"), P("ctx", "head"), P("ctx", "head"), P("ctx", "head")),
        check_vma=False,
    )
```

```python
import functools

import jax
import jax.numpy as jnp
from jax import lax
from jax.experimental import pallas as pl
from jax.experimental.pallas import tpu as pltpu
from jax.sharding import PartitionSpec as P

DH = 128
EPS = 1e-06
F32 = jnp.float32
BF16 = jnp.bfloat16
MIB = 1024 * 1024

RATE = 10**8
MICROSECONDS = {
    "setup": 100.0, "local_states": 0.8, "intra": 3.0, "back_own": 1.8, "pair_total": 0.1, "exchange_stage": 0.1,
    "exchange_last": 0.1, "normalise": 0.9, "project_3": 1.8, "project_2": 1.8, "project_1": 1.8,
    "project_0": 1.8, "back_1": 1.8, "pick": 0.3, "turn": 0.5, "back_2": 1.8, "attended_grads": 2.0, "first_grads": 2.0, "block": 0.5,
    "query_grad": 0.01, "key_value_grads": 0.01, "last_grads": 0.01, "mixed": 1.3,
}

I_BLK, I_CORE, I_Z, I_DOCS = 0, 1, 2, 3


def kernel(body, name, smem, ins, outs, deps=(), spare=8):
    n, n_dep = len(smem) + len(ins), len(deps)

    def inner(*refs):
        body(*refs[:n], *refs[n + n_dep:])

    size = sum(a.size * a.dtype.itemsize for a in list(ins) + list(outs))
    spec = lambda space: pl.BlockSpec(memory_space=space)
    return pl.pallas_call(
        inner,
        name=name,
        in_specs=[spec(pltpu.SMEM)] * len(smem) + [spec(pltpu.VMEM)] * len(ins) + [spec(pl.ANY)] * n_dep,
        out_specs=[spec(pltpu.VMEM)] * len(outs),
        out_shape=list(outs),
        compiler_params=pltpu.CompilerParams(vmem_limit_bytes=size + spare * MIB),
        cost_estimate=pl.CostEstimate(
            flops=int(MICROSECONDS[name] * RATE), bytes_accessed=0, transcendentals=0
        ),
    )(*smem, *ins, *deps)


def like(shape, dtype):
    return jax.ShapeDtypeStruct(shape, dtype)


def dot(a, b, ca, cb):
    return lax.dot_general(a, b, (((ca,), (cb,)), ((), ())), preferred_element_type=F32)


def head(h):
    return slice(h * DH, (h + 1) * DH)


def starts_of(info_ref):
    out, at = [], jnp.int32(0)
    for j in range(I_DOCS, info_ref.shape[0] - 1):
        at = at + info_ref[j]
        out.append(at)
    return out


def start_at(starts, p):
    best = jnp.minimum(p, 0)
    best = jnp.maximum(best, -1)
    for s in starts:
        best = jnp.where(p >= s, s, best)
    return best


def line(tok, axis):
    return lax.broadcasted_iota(jnp.int32, (tok, 1) if axis == 0 else (1, tok), axis)


def carries(info_ref, tok):
    first = info_ref[I_BLK] * tok
    starts = starts_of(info_ref)
    rows = start_at(starts, line(tok, 0) + first)
    return rows == start_at(starts, first - 1), rows == start_at(starts, first + tok - 1)


def visible(low_ref, axis, t0, t1, s1):
    low = low_ref[t0:t1, :1] if axis == 0 else low_ref[:1, t0:t1]
    t, s = line(t1 - t0, axis) + t0, line(s1, 1 - axis)
    return (s <= t) & (s >= low)


def same(starts, tok, a, b):
    pa, pb = a * tok + tok - 1, b * tok + tok - 1
    one = (a >= 0) | (b < 0)
    for s in starts:
        one = jnp.logical_and(one, jnp.logical_not(jnp.logical_and(pa < s, s <= pb)))
    return jnp.where(one, 1.0, 0.0).astype(F32)


def stages(n, forward):
    out, m = [], 2
    while m < n:
        r = 2
        out.append((m, r, m * r >= n))
        m *= r
    return out


def coefficients(starts, tok, n, blk, forward):
    link = functools.partial(same, starts, tok)
    core = lax.rem(blk, 2)
    first = blk - core
    one, none = jnp.float32(1.0), jnp.float32(0.0)
    if forward:
        near, inner, outer = core == 0, link(first, first + 1), link(first - 1, first)
    else:
        near, inner, outer = core == 1, link(first - 1, first), link(first, first + 1)
    out = [jnp.where(near, inner, one), jnp.where(near, one, inner)]
    for m, r, last in stages(n, forward):
        low = blk // (m * r) * (m * r)
        digit = lax.rem(blk // m, r)
        for x in range(1, r):
            j = jnp.bitwise_xor(digit, x)
            if forward:
                out.append(jnp.where(j < digit, link(low + (j + 1) * m - 1, first - 1), none))
            else:
                out.append(jnp.where(j > digit, link(first + 1, low + j * m - 1), none))
        if not last:
            for x in range(r):
                j = jnp.bitwise_xor(digit, x)
                if forward:
                    out.append(link(low + (j + 1) * m - 1, low + r * m - 1))
                else:
                    out.append(link(low - 1, low + j * m - 1))
    return out + [jnp.where(near, one, none), outer]


def pair_body(c_ref, mine_ref, got_ref, total_ref):
    a, b = c_ref[0:1, :], c_ref[1:2, :]
    total_ref[...] = (mine_ref[...].astype(F32) * a + got_ref[...].astype(F32) * b).astype(BF16)


def stage_body(row, r, last, begun, c_ref, *refs):
    refs = list(refs)
    others = [refs.pop(0)[...].astype(F32) for _ in range(r - 1)]
    entering = refs.pop(0)[...] if begun else None
    for other in others:
        part = other * c_ref[row:row + 1, :]
        entering = part if entering is None else entering + part
        row += 1
    if not last:
        total_ref, new_total_ref, entering_ref = refs
        entering_ref[...] = entering
        total = total_ref[...].astype(F32) * c_ref[row:row + 1, :]
        for other in others:
            row += 1
            total = total + other * c_ref[row:row + 1, :]
        new_total_ref[...] = total.astype(BF16)
        return
    mine_ref, got_ref, own_ref, away_ref = refs
    near, outer = c_ref[row:row + 1, :], c_ref[row + 1:row + 2, :]
    nearer = mine_ref[...].astype(F32) * near + got_ref[...].astype(F32) * (1.0 - near)
    chained = nearer + outer * entering
    own_ref[...] = (entering * near + chained * (1.0 - near)).astype(BF16)
    away_ref[...] = (chained * near + entering * (1.0 - near)).astype(BF16)


def pair_total(send, keep, coef):
    n = lax.axis_size("ctx")
    got = lax.ppermute(send, "ctx", [(i, i ^ 1) for i in range(n)])
    (total,) = kernel(pair_body, "pair_total", [], [coef, keep, got], [like(keep.shape, BF16)])
    return got, total


def exchange(total, keep, got, coef, forward, beside):
    n = lax.axis_size("ctx")
    swap = [(i, i ^ 1) for i in range(n)]
    half = like(keep.shape, BF16)
    entering, row = [], 2
    for m, r, last in stages(n, forward):
        others = []
        for x in range(1, r):
            pairs = [
                (i, i ^ (x * m)) for i in range(n)
                if not last or ((i // m % r) < (i // m % r ^ x)) == forward
            ]
            others.append(lax.ppermute(total, "ctx", pairs))
        deps = beside.pop(0)(total) if beside else ()
        body = functools.partial(stage_body, row, r, last, bool(entering))
        if last:
            own, away = kernel(
                body, "exchange_last", [], [coef, *others, *entering, keep, got], [half, half], deps
            )
        else:
            total, e = kernel(
                body, "exchange_stage", [], [coef, *others, *entering, total],
                [half, like(keep.shape, F32)], deps,
            )
            entering = [e]
            row += 2 * r - 1
    return own, lax.ppermute(away, "ctx", swap)


TILE = 256
ROWS = 32
C_CORE, C_END = ROWS - 1, ROWS - 2


def put_states(states, c_ref, keep_ref, send_ref):
    half = len(states) // 2
    core0 = c_ref[C_CORE:C_CORE + 1, :] > 0.5
    for i in range(half):
        keep_ref[i] = jnp.where(core0, states[i], states[i + half]).astype(BF16)
        send_ref[i] = jnp.where(core0, states[i + half], states[i]).astype(BF16)


def setup_body(n, tok, info_ref, coef_ref, coefb_ref, cin_ref, cout_ref, low_ref, low_t_ref):
    blk, core = info_ref[I_BLK], info_ref[I_CORE]
    starts = starts_of(info_ref)
    for ref, forward in ((coef_ref, True), (coefb_ref, False)):
        ref[...] = jnp.zeros_like(ref)
        for i, c in enumerate(coefficients(starts, tok, n, blk, forward)):
            ref[i:i + 1, :] = jnp.full((1, DH), c, F32)
        ref[C_CORE:C_CORE + 1, :] = jnp.full((1, DH), jnp.where(core == 0, 1.0, 0.0), F32)
        end = jnp.logical_or(info_ref[I_Z] == 0, info_ref[I_Z] == 3)
        ref[C_END:C_END + 1, :] = jnp.full((1, DH), jnp.where(end, 1.0, 0.0), F32)
    cin, cout = carries(info_ref, tok)
    cin_ref[...] = jnp.broadcast_to(jnp.where(cin, 1.0, 0.0), cin_ref.shape)
    cout_ref[...] = jnp.broadcast_to(jnp.where(cout, 1.0, 0.0), cout_ref.shape)
    first = blk * tok
    for ref, axis in ((low_ref, 0), (low_t_ref, 1)):
        low = start_at(starts, line(tok, axis) + first) - first
        ref[...] = jnp.broadcast_to(low, ref.shape)


def states_body(c_ref, cout_ref, k_ref, v_ref, send_ref, keep_ref):
    zero = jnp.zeros((), BF16)
    cout = cout_ref[...] > 0.5
    states = []
    for h in range(k_ref.shape[1] // DH):
        kept = jnp.where(cout, k_ref[:, head(h)], zero)
        states.append(dot(kept, v_ref[:, head(h)], 0, 0))
    put_states(states, c_ref, keep_ref, send_ref)


def intra_body(low_ref, q_ref, k_ref, v_ref, out_ref):
    tok = q_ref.shape[0]
    mask = visible(low_ref, 0, 0, tok, tok)
    for h in range(q_ref.shape[1] // DH):
        s = dot(q_ref[:, head(h)], k_ref[:, head(h)], 1, 1)
        s = jnp.where(mask, s, 0.0).astype(BF16)
        out_ref[:, head(h)] = dot(s, v_ref[:, head(h)], 1, 0)


def pick(c_ref, own_ref, back_ref, h):
    half = own_ref.shape[0]
    core0 = c_ref[C_CORE:C_CORE + 1, :] > 0.5
    a, b = own_ref[h % half].astype(F32), back_ref[h % half].astype(F32)
    return (jnp.where(core0, a, b) if h < half else jnp.where(core0, b, a)).astype(BF16)


def norm_body(c_ref, cin_ref, q_ref, own_ref, back_ref, a_ref, normed_ref, inv_ref, n_ref):
    wide = q_ref.shape[1]
    for h in range(wide // DH):
        inter = dot(q_ref[:, head(h)], pick(c_ref, own_ref, back_ref, h), 1, 0)
        att = a_ref[:, head(h)] + cin_ref[...] * inter
        inv = lax.rsqrt(jnp.mean(att * att, axis=-1, keepdims=True) + EPS)
        normed = att * inv
        inv_ref[:, head(h)] = jnp.broadcast_to(inv, att.shape)
        normed_ref[:, head(h)] = normed
        n_ref[:, head(h)] = normed.astype(BF16)


def columns(info_ref, block, width):
    return pl.multiple_of(jnp.bitwise_xor(info_ref[I_Z], block) * width, width)


def project_body(block, info_ref, n_ref, w_ref, out_ref):
    width = out_ref.shape[1]
    base = columns(info_ref, block, width)
    for i in range(width // TILE):
        at = pl.multiple_of(base + i * TILE, TILE)
        out_ref[:, i * TILE:(i + 1) * TILE] = dot(
            n_ref[...], w_ref[:, pl.ds(at, TILE)], 1, 0
        ).astype(BF16)


def back_body(blocks, based, info_ref, w_ref, *refs):
    out_ref = refs[-1]
    feats = out_ref.shape[1]
    for i in range(feats // TILE):
        rows = slice(i * TILE, (i + 1) * TILE)
        acc = refs[-2][:, rows] if based else None
        for block, g_ref in zip(blocks, refs, strict=False):
            width = g_ref.shape[1]
            at = columns(info_ref, block, width)
            part = dot(g_ref[...], w_ref[rows, pl.ds(at, width)], 1, 1)
            acc = part if acc is None else acc + part
        out_ref[:, rows] = acc


def block_body(block, info_ref, w_ref, out_ref):
    width = out_ref.shape[1]
    out_ref[...] = w_ref[:, pl.ds(columns(info_ref, block, width), width)]


def att_grad(rows, c_ref, cin_ref, w_ref, n_ref, g_ref, base_ref, normed_ref, inv_ref, q_ref, ag_ref):
    wide = q_ref.shape[1]
    x = n_ref[...] * at_end(c_ref)[:, :1] + g_ref[rows, :]
    zero = jnp.zeros((), BF16)
    cin = cin_ref[rows, :] > 0.5
    states = []
    for i in range(wide // TILE):
        feats = slice(i * TILE, (i + 1) * TILE)
        ng2 = base_ref[rows, feats] + dot(x, w_ref[feats, :], 1, 1)
        for j in range(TILE // DH):
            at = head(i * (TILE // DH) + j)
            ng, normed = ng2[:, head(j)], normed_ref[rows, at]
            proj = jnp.mean(ng * normed, axis=-1, keepdims=True)
            ag = ((ng - normed * proj) * inv_ref[rows, at]).astype(BF16)
            ag_ref[:, at] = ag
            states.append(dot(jnp.where(cin, q_ref[rows, at], zero), ag, 0, 0))
    return states


def att_grad_first_body(rows, *refs):
    for h, state in enumerate(att_grad(rows, *refs[:-1])):
        refs[-1][h] = state


def att_grad_second_body(rows, before_ref, *refs):
    send_ref, keep_ref = refs[-2:]
    states = att_grad(rows, *refs[:-2])
    put_states([before_ref[h] + state for h, state in enumerate(states)], refs[0], keep_ref, send_ref)


def query_grad(h, rows, s1, mask, c_ref, cin_ref, k_ref, v_ref, ag_ref, own_ref, back_ref):
    ag, at = ag_ref[:, head(h)], head(h)
    inter = dot(ag, pick(c_ref, own_ref, back_ref, h), 1, 1)
    g = jnp.where(mask, dot(ag, v_ref[:s1, at], 1, 1), 0.0).astype(BF16)
    return (dot(g, k_ref[:s1, at], 1, 0) + cin_ref[rows, :] * inter).astype(BF16)


def key_value_grad(h, rows, s1, mask, q_ref, k_ref, v_ref, ag_ref):
    at = head(h)
    q, ag = q_ref[rows, at], ag_ref[:, at]
    st = jnp.where(mask, dot(k_ref[:s1, at], q, 1, 1), 0.0).astype(BF16)
    gt = jnp.where(mask, dot(v_ref[:s1, at], ag, 1, 1), 0.0).astype(BF16)
    return dot(gt, q, 1, 0), dot(st, ag, 1, 0)


def first_grads_body(rows, low_ref, low_t_ref, c_ref, cin_ref, q_ref, k_ref, v_ref, ag_ref, own_ref, back_ref, qg_ref, kg_ref, vg_ref):
    r1 = rows.stop
    mask, mask_t = visible(low_ref, 0, 0, r1, r1), visible(low_t_ref, 1, 0, r1, r1)
    for h in range(q_ref.shape[1] // DH):
        qg_ref[:, head(h)] = query_grad(h, rows, r1, mask, c_ref, cin_ref, k_ref, v_ref, ag_ref, own_ref, back_ref)
        kg, vg = key_value_grad(h, rows, r1, mask_t, q_ref, k_ref, v_ref, ag_ref)
        kg_ref[:, head(h)] = kg
        vg_ref[:, head(h)] = vg


def query_grad_body(rows, low_ref, c_ref, cin_ref, k_ref, v_ref, ag_ref, own_ref, back_ref, first_ref, qg_ref, mark_ref):
    r0, r1 = rows.start, rows.stop
    mask = visible(low_ref, 0, r0, r1, r1)
    mark_ref[...] = jnp.zeros_like(mark_ref)
    qg_ref[:r0, :] = first_ref[...]
    for h in range(k_ref.shape[1] // DH):
        qg_ref[rows, head(h)] = query_grad(h, rows, r1, mask, c_ref, cin_ref, k_ref, v_ref, ag_ref, own_ref, back_ref)


def key_value_body(rows, low_t_ref, q_ref, k_ref, v_ref, ag_ref, k_first_ref, v_first_ref, kg_ref, vg_ref):
    r0, r1 = rows.start, rows.stop
    mask = visible(low_t_ref, 1, r0, r1, r1)
    for h in range(q_ref.shape[1] // DH):
        at = head(h)
        kg, vg = key_value_grad(h, rows, r1, mask, q_ref, k_ref, v_ref, ag_ref)
        for ref, first_ref, new in ((kg_ref, k_first_ref, kg), (vg_ref, v_first_ref, vg)):
            ref[:r0, at] = first_ref[:, at] + new[:r0]
            ref[r0:, at] = new[r0:]


def last_body(c_ref, cout_ref, k_ref, v_ref, own_ref, back_ref, kp_ref, vp_ref, kg_ref, vg_ref, mark_ref):
    mark_ref[...] = jnp.zeros_like(mark_ref)
    wide = k_ref.shape[1]
    cout = cout_ref[...]
    for h in range(wide // DH):
        leaving = pick(c_ref, own_ref, back_ref, h)
        kg = cout * dot(v_ref[:, head(h)], leaving, 1, 1)
        vg = cout * dot(k_ref[:, head(h)], leaving, 1, 0)
        kg_ref[:, head(h)] = (kp_ref[:, head(h)] + kg).astype(BF16)
        vg_ref[:, head(h)] = (vp_ref[:, head(h)] + vg).astype(BF16)


def sum_body(*refs):
    total = refs[0][...].astype(F32)
    for r in refs[1:-1]:
        total = total + r[...].astype(F32)
    refs[-1][...] = total.astype(BF16)


def at_end(c_ref):
    return c_ref[C_END:C_END + 1, :].astype(BF16)


def end_body(c_ref, a_ref, b_ref, out_ref):
    end = at_end(c_ref)
    for i in range(out_ref.shape[1] // DH):
        out_ref[:, head(i)] = a_ref[:, head(i)] * end + b_ref[:, head(i)]


def first_body(c_ref, g1_ref, p3_ref, g3_ref, *out_refs):
    r0 = 0
    for n_ref, i_ref in zip(out_refs[::2], out_refs[1::2], strict=True):
        rows = slice(r0, r0 + n_ref.shape[0])
        i_ref[...] = g1_ref[rows, :]
        end_body(c_ref, p3_ref.at[rows, :], g3_ref.at[rows, :], n_ref)
        r0 = rows.stop


def ends_body(c_ref, *refs):
    out_ref = refs[-1]
    r0 = 0
    for a_ref, b_ref in zip(refs[:-1:2], refs[1:-1:2], strict=True):
        rows = slice(r0, r0 + a_ref.shape[0])
        end_body(c_ref, a_ref, b_ref, out_ref.at[rows, :])
        r0 = rows.stop


def turn_body(rows, c_ref, n2_ref, p2_ref, i2_ref, s2_ref, n3_ref):
    s2_ref[...] = p2_ref[rows, :] + n2_ref[...]
    end_body(c_ref, p2_ref.at[rows, :], i2_ref, n3_ref)


def turn_again_body(rows, n3_ref, i3_ref, p3_ref, p1_ref, s3_ref, s1_ref):
    s3_ref[...] = p3_ref[rows, :] + n3_ref[...]
    s1_ref[...] = p1_ref[rows, :] + i3_ref[...]


def mixed_body(p_ref, *refs):
    out_ref = refs[-1]
    r0 = 0
    for a_ref, b_ref in zip(refs[:-1:2], refs[1:-1:2], strict=True):
        rows = slice(r0, r0 + a_ref.shape[0])
        total = p_ref[rows, :].astype(F32) + a_ref[...].astype(F32) + b_ref[...].astype(F32)
        out_ref[rows, :] = total.astype(BF16)
        r0 = rows.stop


def shards(q, k, v, lens, w, grad):
    tok, width = grad.shape
    feats = w.shape[0]
    heads = feats // DH
    half = heads // 2
    n = lax.axis_size("ctx")
    blk = lax.axis_index("ctx").astype(jnp.int32)
    z = lax.axis_index("head").astype(jnp.int32)
    info = jnp.concatenate([jnp.stack([blk, blk % 2, z]), lens])
    part = like((tok, width), BF16)
    wide_b, wide_f = like((tok, feats), BF16), like((tok, feats), F32)
    state = like((half, DH, DH), BF16)
    lanes = like((tok, DH), F32)
    table = like((ROWS, DH), F32)

    def project(block, name, deps=()):
        body = functools.partial(project_body, block)
        return kernel(body, name, [info], [normed, w], [part], deps)[0]

    def back_project(blocks, name, grads, base=None, deps=()):
        body = functools.partial(back_body, blocks, base is not None)
        return kernel(body, name, [info], [w, *grads] + ([] if base is None else [base]), [wide_f], deps)[0]

    neighbours = [(0, 1), (1, 0), (2, 3), (3, 2)]
    inner = [(1, 2), (2, 1)]
    g1 = lax.ppermute(grad, "head", neighbours)
    g3_inner = lax.ppermute(grad, "head", inner)
    coef, coefb, cin, cout, low, low_t = kernel(
        functools.partial(setup_body, n, tok), "setup", [info], [],
        [table, table, lanes, lanes, like((tok, DH), jnp.int32), like((8, tok), jnp.int32)],
    )
    send, keep = kernel(states_body, "local_states", [], [coef, cout, k, v], [state, state])
    got, total = pair_total(send, keep, coef)
    (inside,) = kernel(intra_body, "intra", [], [low, q, k, v], [wide_f], [total])
    base = back_project([0], "back_own", [grad], None, [inside])
    own, other = exchange(total, keep, got, coef, True, [lambda _: [inside], lambda _: [base]])
    normed_f, inv, normed = kernel(
        norm_body, "normalise", [], [coef, cin, q, own, other, inside], [wide_f, wide_f, wide_b]
    )
    lot = like((tok // 2, width), BF16)
    rows = [slice(0, tok // 2), slice(tok // 2, tok)]

    def both(arrays, kind):
        return [lax.ppermute(a, "head", kind) for a in arrays]

    def turn(h, deps):
        return kernel(functools.partial(turn_body, rows[h]), "turn", [], [coef, n2[h], p2, i2[h]], [lot, lot], deps)

    def turn_again(h, deps):
        return kernel(functools.partial(turn_again_body, rows[h]), "turn", [], [n3[h], i3[h], p3, p1], [lot, lot], deps)

    p3 = project(3, "project_3")
    g1, g3_inner, _ = lax.optimization_barrier((g1, g3_inner, p3))
    n2a, i2a, n2b, i2b = kernel(first_body, "pick", [], [coef, g1, p3, g3_inner], [lot] * 4)
    n2a, i2a = lax.ppermute(n2a, "head", neighbours), lax.ppermute(i2a, "head", inner)
    n2b, i2b = lax.ppermute(n2b, "head", neighbours), lax.ppermute(i2b, "head", inner)
    n2, i2 = [n2a, n2b], [i2a, i2b]
    p2 = project(2, "project_2", [p3])
    s2a, n3a = turn(0, [])
    i3a, n3a = lax.ppermute(s2a, "head", inner), lax.ppermute(n3a, "head", neighbours)
    p1 = project(1, "project_1", [s2a])
    p0 = project(0, "project_0", [p1])
    base = back_project([1], "back_1", [g1], base, [p0])
    s2b, n3b = turn(1, [base])
    i3b, n3b = lax.ppermute(s2b, "head", inner), lax.ppermute(n3b, "head", neighbours)
    n3, i3 = [n3a, n3b], [i3a, i3b]
    (g2,) = kernel(ends_body, "pick", [], [coef, n2a, i2a, n2b, i2b], [part], [s2b])
    base = back_project([2], "back_2", [g2], base)
    (w3,) = kernel(functools.partial(block_body, 3), "block", [info], [w], [like((feats, width), BF16)], [base])
    s3a, s1a = turn_again(0, [w3])
    n4a = lax.ppermute(s1a, "head", neighbours)
    ag_ins = [g3_inner, base, normed_f, inv, q]
    aga, states = kernel(
        functools.partial(att_grad_first_body, rows[0]), "attended_grads", [], [coef, cin, w3, n3a, *ag_ins],
        [like((tok // 2, feats), BF16), like((heads, DH, DH), F32)], [s1a],
    )
    s3a, _ = lax.optimization_barrier((s3a, aga))
    i4a = lax.ppermute(s3a, "head", inner)
    half_f = like((tok // 2, feats), F32)
    qga, kga, vga = kernel(
        functools.partial(first_grads_body, rows[0]), "first_grads", [],
        [low, low_t, coef, cin, q, k, v, aga, own, other], [like((tok // 2, feats), BF16), half_f, half_f],
    )
    ag, gsend, gkeep = kernel(
        functools.partial(att_grad_second_body, rows[1]), "attended_grads", [],
        [states, coef, cin, w3, n3b, *ag_ins], [like((tok // 2, feats), BF16), state, state], [qga],
    )
    s3b, s1b = turn_again(1, [gsend])
    n4b, i4b = lax.ppermute(s1b, "head", neighbours), lax.ppermute(s3b, "head", inner)
    ggot, gtotal = pair_total(gsend, gkeep, coefb)
    grads = []

    def beside_first(sent):
        grads.extend(kernel(
            functools.partial(query_grad_body, rows[1]), "query_grad", [],
            [low, coef, cin, k, v, ag, own, other, qga],
            [wide_b, like((8, DH), F32)], [sent],
        ))
        return grads[1:2]

    def beside_second(sent):
        grads.extend(kernel(
            functools.partial(key_value_body, rows[1]), "key_value_grads", [],
            [low_t, q, k, v, ag, kga, vga], [wide_f, wide_f], [sent],
        ))
        return grads[2:3]

    leaving, leaving_other = exchange(gtotal, gkeep, ggot, coefb, False, [beside_first, beside_second])
    query_grad, _, kp, vp = grads
    key_grad, value_grad, mark = kernel(
        last_body, "last_grads", [], [coef, cout, k, v, leaving, leaving_other, kp, vp],
        [wide_b, wide_b, like((8, DH), F32)],
    )
    (mixed,) = kernel(mixed_body, "mixed", [], [p0, n4a, i4a, n4b, i4b], [part], [mark])
    return mixed, query_grad, key_grad, value_grad


def solution(mesh):
    return jax.shard_map(
        shards,
        mesh=mesh,
        in_specs=(
            P("ctx", "head"),
            P("ctx", "head"),
            P("ctx", "head"),
            P(),
            P("head", None),
            P("ctx", "head"),
        ),
        out_specs=(P("ctx", "head"), P("ctx", "head"), P("ctx", "head"), P("ctx", "head")),
        check_vma=False,
    )
```

```python
import functools

import jax
import jax.numpy as jnp
from jax import lax
from jax.experimental import pallas as pl
from jax.experimental.pallas import tpu as pltpu
from jax.sharding import PartitionSpec as P

DH = 128
EPS = 1e-06
F32 = jnp.float32
BF16 = jnp.bfloat16
MIB = 1024 * 1024

RATE = 10**8
MICROSECONDS = {
    "setup": 100.0, "local_states": 0.8, "intra": 3.0, "back_own": 1.8, "pair_total": 0.1, "exchange_stage": 0.1,
    "exchange_last": 0.1, "normalise": 0.9, "project_3": 1.8, "project_2": 1.8, "project_1": 1.8,
    "project_0": 1.8, "back_1": 1.8, "pick": 0.3, "turn": 0.5, "back_2": 1.8, "attended_grads": 2.0, "first_grads": 2.0, "block": 0.5,
    "query_grad": 0.01, "key_value_grads": 0.01, "last_grads": 0.01,
}

I_BLK, I_CORE, I_Z, I_DOCS = 0, 1, 2, 3


def kernel(body, name, smem, ins, outs, deps=(), spare=8, hbm_outs=0, scratch=()):
    n, n_dep = len(smem) + len(ins), len(deps)

    def inner(*refs):
        body(*refs[:n], *refs[n + n_dep:])

    size = sum(a.size * a.dtype.itemsize for a in list(ins) + list(outs))
    spec = lambda space: pl.BlockSpec(memory_space=space)
    return pl.pallas_call(
        inner,
        name=name,
        in_specs=[spec(pltpu.SMEM)] * len(smem) + [spec(pltpu.VMEM)] * len(ins) + [spec(pl.ANY)] * n_dep,
        out_specs=[spec(pltpu.HBM)] * hbm_outs + [spec(pltpu.VMEM)] * (len(outs) - hbm_outs),
        out_shape=list(outs),
        scratch_shapes=list(scratch),
        compiler_params=pltpu.CompilerParams(vmem_limit_bytes=size + spare * MIB),
        cost_estimate=pl.CostEstimate(
            flops=int(MICROSECONDS[name] * RATE), bytes_accessed=0, transcendentals=0
        ),
    )(*smem, *ins, *deps)


def like(shape, dtype):
    return jax.ShapeDtypeStruct(shape, dtype)


def dot(a, b, ca, cb):
    return lax.dot_general(a, b, (((ca,), (cb,)), ((), ())), preferred_element_type=F32)


def head(h):
    return slice(h * DH, (h + 1) * DH)


def starts_of(info_ref):
    out, at = [], jnp.int32(0)
    for j in range(I_DOCS, info_ref.shape[0] - 1):
        at = at + info_ref[j]
        out.append(at)
    return out


def start_at(starts, p):
    best = jnp.minimum(p, 0)
    best = jnp.maximum(best, -1)
    for s in starts:
        best = jnp.where(p >= s, s, best)
    return best


def line(tok, axis):
    return lax.broadcasted_iota(jnp.int32, (tok, 1) if axis == 0 else (1, tok), axis)


def carries(info_ref, tok):
    first = info_ref[I_BLK] * tok
    starts = starts_of(info_ref)
    rows = start_at(starts, line(tok, 0) + first)
    return rows == start_at(starts, first - 1), rows == start_at(starts, first + tok - 1)


def visible(low_ref, axis, t0, t1, s1):
    low = low_ref[t0:t1, :1] if axis == 0 else low_ref[:1, t0:t1]
    t, s = line(t1 - t0, axis) + t0, line(s1, 1 - axis)
    return (s <= t) & (s >= low)


def same(starts, tok, a, b):
    pa, pb = a * tok + tok - 1, b * tok + tok - 1
    one = (a >= 0) | (b < 0)
    for s in starts:
        one = jnp.logical_and(one, jnp.logical_not(jnp.logical_and(pa < s, s <= pb)))
    return jnp.where(one, 1.0, 0.0).astype(F32)


def stages(n, forward):
    out, m = [], 2
    while m < n:
        r = 2
        out.append((m, r, m * r >= n))
        m *= r
    return out


def coefficients(starts, tok, n, blk, forward):
    link = functools.partial(same, starts, tok)
    core = lax.rem(blk, 2)
    first = blk - core
    one, none = jnp.float32(1.0), jnp.float32(0.0)
    if forward:
        near, inner, outer = core == 0, link(first, first + 1), link(first - 1, first)
    else:
        near, inner, outer = core == 1, link(first - 1, first), link(first, first + 1)
    out = [jnp.where(near, inner, one), jnp.where(near, one, inner)]
    for m, r, last in stages(n, forward):
        low = blk // (m * r) * (m * r)
        digit = lax.rem(blk // m, r)
        for x in range(1, r):
            j = jnp.bitwise_xor(digit, x)
            if forward:
                out.append(jnp.where(j < digit, link(low + (j + 1) * m - 1, first - 1), none))
            else:
                out.append(jnp.where(j > digit, link(first + 1, low + j * m - 1), none))
        if not last:
            for x in range(r):
                j = jnp.bitwise_xor(digit, x)
                if forward:
                    out.append(link(low + (j + 1) * m - 1, low + r * m - 1))
                else:
                    out.append(link(low - 1, low + j * m - 1))
    return out + [jnp.where(near, one, none), outer]


def pair_body(c_ref, mine_ref, got_ref, total_ref):
    a, b = c_ref[0:1, :], c_ref[1:2, :]
    total_ref[...] = (mine_ref[...].astype(F32) * a + got_ref[...].astype(F32) * b).astype(BF16)


def stage_body(row, r, last, begun, c_ref, *refs):
    refs = list(refs)
    others = [refs.pop(0)[...].astype(F32) for _ in range(r - 1)]
    entering = refs.pop(0)[...] if begun else None
    for other in others:
        part = other * c_ref[row:row + 1, :]
        entering = part if entering is None else entering + part
        row += 1
    if not last:
        total_ref, new_total_ref, entering_ref = refs
        entering_ref[...] = entering
        total = total_ref[...].astype(F32) * c_ref[row:row + 1, :]
        for other in others:
            row += 1
            total = total + other * c_ref[row:row + 1, :]
        new_total_ref[...] = total.astype(BF16)
        return
    mine_ref, got_ref, own_ref, away_ref = refs
    near, outer = c_ref[row:row + 1, :], c_ref[row + 1:row + 2, :]
    nearer = mine_ref[...].astype(F32) * near + got_ref[...].astype(F32) * (1.0 - near)
    chained = nearer + outer * entering
    own_ref[...] = (entering * near + chained * (1.0 - near)).astype(BF16)
    away_ref[...] = (chained * near + entering * (1.0 - near)).astype(BF16)


def pair_total(send, keep, coef):
    n = lax.axis_size("ctx")
    got = lax.ppermute(send, "ctx", [(i, i ^ 1) for i in range(n)])
    (total,) = kernel(pair_body, "pair_total", [], [coef, keep, got], [like(keep.shape, BF16)])
    return got, total


def exchange(total, keep, got, coef, forward, beside):
    n = lax.axis_size("ctx")
    swap = [(i, i ^ 1) for i in range(n)]
    half = like(keep.shape, BF16)
    entering, row = [], 2
    for m, r, last in stages(n, forward):
        others = []
        for x in range(1, r):
            pairs = [
                (i, i ^ (x * m)) for i in range(n)
                if not last or ((i // m % r) < (i // m % r ^ x)) == forward
            ]
            others.append(lax.ppermute(total, "ctx", pairs))
        deps = beside.pop(0)(total) if beside else ()
        body = functools.partial(stage_body, row, r, last, bool(entering))
        if last:
            own, away = kernel(
                body, "exchange_last", [], [coef, *others, *entering, keep, got], [half, half], deps
            )
        else:
            total, e = kernel(
                body, "exchange_stage", [], [coef, *others, *entering, total],
                [half, like(keep.shape, F32)], deps,
            )
            entering = [e]
            row += 2 * r - 1
    return own, lax.ppermute(away, "ctx", swap)


TILE = 256
ROWS = 32
C_CORE, C_END = ROWS - 1, ROWS - 2


def put_states(states, c_ref, keep_ref, send_ref):
    half = len(states) // 2
    core0 = c_ref[C_CORE:C_CORE + 1, :] > 0.5
    for i in range(half):
        keep_ref[i] = jnp.where(core0, states[i], states[i + half]).astype(BF16)
        send_ref[i] = jnp.where(core0, states[i + half], states[i]).astype(BF16)


def setup_body(n, tok, info_ref, coef_ref, coefb_ref, cin_ref, cout_ref, low_ref, low_t_ref):
    blk, core = info_ref[I_BLK], info_ref[I_CORE]
    starts = starts_of(info_ref)
    for ref, forward in ((coef_ref, True), (coefb_ref, False)):
        ref[...] = jnp.zeros_like(ref)
        for i, c in enumerate(coefficients(starts, tok, n, blk, forward)):
            ref[i:i + 1, :] = jnp.full((1, DH), c, F32)
        ref[C_CORE:C_CORE + 1, :] = jnp.full((1, DH), jnp.where(core == 0, 1.0, 0.0), F32)
        end = jnp.logical_or(info_ref[I_Z] == 0, info_ref[I_Z] == 3)
        ref[C_END:C_END + 1, :] = jnp.full((1, DH), jnp.where(end, 1.0, 0.0), F32)
    cin, cout = carries(info_ref, tok)
    cin_ref[...] = jnp.broadcast_to(jnp.where(cin, 1.0, 0.0), cin_ref.shape)
    cout_ref[...] = jnp.broadcast_to(jnp.where(cout, 1.0, 0.0), cout_ref.shape)
    first = blk * tok
    for ref, axis in ((low_ref, 0), (low_t_ref, 1)):
        low = start_at(starts, line(tok, axis) + first) - first
        ref[...] = jnp.broadcast_to(low, ref.shape)


def states_body(c_ref, cout_ref, k_ref, v_ref, send_ref, keep_ref):
    zero = jnp.zeros((), BF16)
    cout = cout_ref[...] > 0.5
    states = []
    for h in range(k_ref.shape[1] // DH):
        kept = jnp.where(cout, k_ref[:, head(h)], zero)
        states.append(dot(kept, v_ref[:, head(h)], 0, 0))
    put_states(states, c_ref, keep_ref, send_ref)


def intra_body(low_ref, q_ref, k_ref, v_ref, out_ref):
    tok = q_ref.shape[0]
    mask = visible(low_ref, 0, 0, tok, tok)
    for h in range(q_ref.shape[1] // DH):
        s = dot(q_ref[:, head(h)], k_ref[:, head(h)], 1, 1)
        s = jnp.where(mask, s, 0.0).astype(BF16)
        out_ref[:, head(h)] = dot(s, v_ref[:, head(h)], 1, 0)


def pick(c_ref, own_ref, back_ref, h):
    half = own_ref.shape[0]
    core0 = c_ref[C_CORE:C_CORE + 1, :] > 0.5
    a, b = own_ref[h % half].astype(F32), back_ref[h % half].astype(F32)
    return (jnp.where(core0, a, b) if h < half else jnp.where(core0, b, a)).astype(BF16)


def norm_body(c_ref, cin_ref, q_ref, own_ref, back_ref, a_ref, normed_ref, inv_ref, n_ref):
    wide = q_ref.shape[1]
    for h in range(wide // DH):
        inter = dot(q_ref[:, head(h)], pick(c_ref, own_ref, back_ref, h), 1, 0)
        att = a_ref[:, head(h)] + cin_ref[...] * inter
        inv = lax.rsqrt(jnp.mean(att * att, axis=-1, keepdims=True) + EPS)
        normed = att * inv
        inv_ref[:, head(h)] = jnp.broadcast_to(inv, att.shape)
        normed_ref[:, head(h)] = normed
        n_ref[:, head(h)] = normed.astype(BF16)


def columns(info_ref, block, width):
    return pl.multiple_of(jnp.bitwise_xor(info_ref[I_Z], block) * width, width)


def project_body(block, info_ref, n_ref, w_ref, out_ref):
    width = out_ref.shape[1]
    base = columns(info_ref, block, width)
    for i in range(width // TILE):
        at = pl.multiple_of(base + i * TILE, TILE)
        out_ref[:, i * TILE:(i + 1) * TILE] = dot(
            n_ref[...], w_ref[:, pl.ds(at, TILE)], 1, 0
        ).astype(BF16)


def back_body(blocks, based, info_ref, w_ref, *refs):
    out_ref = refs[-1]
    feats = out_ref.shape[1]
    for i in range(feats // TILE):
        rows = slice(i * TILE, (i + 1) * TILE)
        acc = refs[-2][:, rows] if based else None
        for block, g_ref in zip(blocks, refs, strict=False):
            width = g_ref.shape[1]
            at = columns(info_ref, block, width)
            part = dot(g_ref[...], w_ref[rows, pl.ds(at, width)], 1, 1)
            acc = part if acc is None else acc + part
        out_ref[:, rows] = acc


def block_body(block, info_ref, w_ref, out_ref):
    width = out_ref.shape[1]
    out_ref[...] = w_ref[:, pl.ds(columns(info_ref, block, width), width)]


def att_grad(rows, c_ref, cin_ref, w_ref, n_ref, g_ref, base_ref, normed_ref, inv_ref, q_ref, ag_ref):
    wide = q_ref.shape[1]
    x = n_ref[...] * at_end(c_ref)[:, :1] + g_ref[rows, :]
    zero = jnp.zeros((), BF16)
    cin = cin_ref[rows, :] > 0.5
    states = []
    for i in range(wide // TILE):
        feats = slice(i * TILE, (i + 1) * TILE)
        ng2 = base_ref[rows, feats] + dot(x, w_ref[feats, :], 1, 1)
        for j in range(TILE // DH):
            at = head(i * (TILE // DH) + j)
            ng, normed = ng2[:, head(j)], normed_ref[rows, at]
            proj = jnp.mean(ng * normed, axis=-1, keepdims=True)
            ag = ((ng - normed * proj) * inv_ref[rows, at]).astype(BF16)
            ag_ref[:, at] = ag
            states.append(dot(jnp.where(cin, q_ref[rows, at], zero), ag, 0, 0))
    return states


def att_grad_first_body(rows, *refs):
    for h, state in enumerate(att_grad(rows, *refs[:-1])):
        refs[-1][h] = state


def att_grad_second_body(rows, before_ref, *refs):
    send_ref, keep_ref = refs[-2:]
    states = att_grad(rows, *refs[:-2])
    put_states([before_ref[h] + state for h, state in enumerate(states)], refs[0], keep_ref, send_ref)


def query_grad(h, rows, s1, mask, c_ref, cin_ref, k_ref, v_ref, ag_ref, own_ref, back_ref):
    ag, at = ag_ref[:, head(h)], head(h)
    inter = dot(ag, pick(c_ref, own_ref, back_ref, h), 1, 1)
    g = jnp.where(mask, dot(ag, v_ref[:s1, at], 1, 1), 0.0).astype(BF16)
    return (dot(g, k_ref[:s1, at], 1, 0) + cin_ref[rows, :] * inter).astype(BF16)


def key_value_grad(h, rows, s1, mask, q_ref, k_ref, v_ref, ag_ref):
    at = head(h)
    q, ag = q_ref[rows, at], ag_ref[:, at]
    st = jnp.where(mask, dot(k_ref[:s1, at], q, 1, 1), 0.0).astype(BF16)
    gt = jnp.where(mask, dot(v_ref[:s1, at], ag, 1, 1), 0.0).astype(BF16)
    return dot(gt, q, 1, 0), dot(st, ag, 1, 0)


def first_grads_body(rows, low_ref, low_t_ref, c_ref, cin_ref, q_ref, k_ref, v_ref, ag_ref, own_ref, back_ref, qg_ref, kg_ref, vg_ref):
    r1 = rows.stop
    mask, mask_t = visible(low_ref, 0, 0, r1, r1), visible(low_t_ref, 1, 0, r1, r1)
    for h in range(q_ref.shape[1] // DH):
        qg_ref[:, head(h)] = query_grad(h, rows, r1, mask, c_ref, cin_ref, k_ref, v_ref, ag_ref, own_ref, back_ref)
        kg, vg = key_value_grad(h, rows, r1, mask_t, q_ref, k_ref, v_ref, ag_ref)
        kg_ref[:, head(h)] = kg
        vg_ref[:, head(h)] = vg


def query_grad_body(rows, low_ref, c_ref, cin_ref, k_ref, v_ref, ag_ref, own_ref, back_ref, first_ref, qg_ref, mark_ref):
    r0, r1 = rows.start, rows.stop
    mask = visible(low_ref, 0, r0, r1, r1)
    mark_ref[...] = jnp.zeros_like(mark_ref)
    qg_ref[:r0, :] = first_ref[...]
    for h in range(k_ref.shape[1] // DH):
        qg_ref[rows, head(h)] = query_grad(h, rows, r1, mask, c_ref, cin_ref, k_ref, v_ref, ag_ref, own_ref, back_ref)


def key_value_body(rows, low_t_ref, q_ref, k_ref, v_ref, ag_ref, k_first_ref, v_first_ref, kg_ref, vg_ref):
    r0, r1 = rows.start, rows.stop
    mask = visible(low_t_ref, 1, r0, r1, r1)
    for h in range(q_ref.shape[1] // DH):
        at = head(h)
        kg, vg = key_value_grad(h, rows, r1, mask, q_ref, k_ref, v_ref, ag_ref)
        for ref, first_ref, new in ((kg_ref, k_first_ref, kg), (vg_ref, v_first_ref, vg)):
            ref[:r0, at] = first_ref[:, at] + new[:r0]
            ref[r0:, at] = new[r0:]


def last_body(c_ref, cout_ref, k_ref, v_ref, own_ref, back_ref, kp_ref, vp_ref, kg_hbm, vg_hbm, mark_ref, kg_ref, vg_ref, sem):
    mark_ref[...] = jnp.zeros_like(mark_ref)
    cout = cout_ref[...]
    copies = []
    for i in range(k_ref.shape[1] // TILE):
        for h in range(i * (TILE // DH), (i + 1) * (TILE // DH)):
            leaving = pick(c_ref, own_ref, back_ref, h)
            kg = cout * dot(v_ref[:, head(h)], leaving, 1, 1)
            vg = cout * dot(k_ref[:, head(h)], leaving, 1, 0)
            kg_ref[:, head(h)] = (kp_ref[:, head(h)] + kg).astype(BF16)
            vg_ref[:, head(h)] = (vp_ref[:, head(h)] + vg).astype(BF16)
        at = slice(i * TILE, (i + 1) * TILE)
        for j, (src, dst) in enumerate(((kg_ref, kg_hbm), (vg_ref, vg_hbm))):
            copies.append(pltpu.make_async_copy(src.at[:, at], dst.at[:, at], sem.at[j, i]))
            copies[-1].start()
    for copy in copies:
        copy.wait()


def sum_body(*refs):
    total = refs[0][...].astype(F32)
    for r in refs[1:-1]:
        total = total + r[...].astype(F32)
    refs[-1][...] = total.astype(BF16)


def at_end(c_ref):
    return c_ref[C_END:C_END + 1, :].astype(BF16)


def end_body(c_ref, a_ref, b_ref, out_ref):
    end = at_end(c_ref)
    for i in range(out_ref.shape[1] // DH):
        out_ref[:, head(i)] = a_ref[:, head(i)] * end + b_ref[:, head(i)]


def first_body(c_ref, g1_ref, p3_ref, g3_ref, *out_refs):
    r0 = 0
    for n_ref, i_ref in zip(out_refs[::2], out_refs[1::2], strict=True):
        rows = slice(r0, r0 + n_ref.shape[0])
        i_ref[...] = g1_ref[rows, :]
        end_body(c_ref, p3_ref.at[rows, :], g3_ref.at[rows, :], n_ref)
        r0 = rows.stop


def ends_body(c_ref, *refs):
    out_ref = refs[-1]
    r0 = 0
    for a_ref, b_ref in zip(refs[:-1:2], refs[1:-1:2], strict=True):
        rows = slice(r0, r0 + a_ref.shape[0])
        end_body(c_ref, a_ref, b_ref, out_ref.at[rows, :])
        r0 = rows.stop


def turn_body(rows, c_ref, n2_ref, p2_ref, i2_ref, s2_ref, n3_ref):
    s2_ref[...] = p2_ref[rows, :] + n2_ref[...]
    end_body(c_ref, p2_ref.at[rows, :], i2_ref, n3_ref)


def turn_again_body(rows, n3_ref, i3_ref, p3_ref, p1_ref, s1_ref, s3_ref):
    s3_ref[...] = p3_ref[rows, :] + n3_ref[...]
    s1_ref[...] = p1_ref[rows, :] + i3_ref[...]


def mix_body(n_dep, p_ref, a_ref, b_ref, *refs):
    total = p_ref[...].astype(F32) + a_ref[...].astype(F32) + b_ref[...].astype(F32)
    refs[n_dep][...] = total.astype(BF16)
    if len(refs) > n_dep + 1:
        refs[-1][...] = jnp.zeros_like(refs[-1])


def mix_half(half, p0, parts, deps, into=None):
    tok, width = p0.shape
    lot = tok // 2
    mine = pl.BlockSpec((lot, width), lambda i: (half, 0))
    whole = pl.BlockSpec((lot, width), lambda i: (0, 0))
    extra = list(deps) + ([] if into is None else [into])
    first = into is None
    out = pl.pallas_call(
        functools.partial(mix_body, len(extra)),
        name="mixed",
        grid=(1,),
        in_specs=[mine, whole, whole] + [pl.BlockSpec(memory_space=pl.ANY)] * len(extra),
        out_specs=[mine] + [pl.BlockSpec((8, DH), lambda i: (0, 0))] * first,
        out_shape=[like((tok, width), BF16)] + [like((8, DH), F32)] * first,
        input_output_aliases={} if first else {2 + len(extra): 0},
        compiler_params=pltpu.CompilerParams(vmem_limit_bytes=12 * MIB),
        cost_estimate=pl.CostEstimate(flops=RATE, bytes_accessed=0, transcendentals=0),
    )(p0, *parts, *extra)
    return out if first else out[0]


def shards(q, k, v, lens, w, grad):
    tok, width = grad.shape
    feats = w.shape[0]
    heads = feats // DH
    half = heads // 2
    n = lax.axis_size("ctx")
    blk = lax.axis_index("ctx").astype(jnp.int32)
    z = lax.axis_index("head").astype(jnp.int32)
    info = jnp.concatenate([jnp.stack([blk, blk % 2, z]), lens])
    part = like((tok, width), BF16)
    wide_b, wide_f = like((tok, feats), BF16), like((tok, feats), F32)
    state = like((half, DH, DH), BF16)
    lanes = like((tok, DH), F32)
    table = like((ROWS, DH), F32)

    def project(block, name, deps=()):
        body = functools.partial(project_body, block)
        return kernel(body, name, [info], [normed, w], [part], deps)[0]

    def back_project(blocks, name, grads, base=None, deps=()):
        body = functools.partial(back_body, blocks, base is not None)
        return kernel(body, name, [info], [w, *grads] + ([] if base is None else [base]), [wide_f], deps)[0]

    neighbours = [(0, 1), (1, 0), (2, 3), (3, 2)]
    inner = [(1, 2), (2, 1)]
    g1 = lax.ppermute(grad, "head", neighbours)
    g3_inner = lax.ppermute(grad, "head", inner)
    coef, coefb, cin, cout, low, low_t = kernel(
        functools.partial(setup_body, n, tok), "setup", [info], [],
        [table, table, lanes, lanes, like((tok, DH), jnp.int32), like((8, tok), jnp.int32)],
    )
    send, keep = kernel(states_body, "local_states", [], [coef, cout, k, v], [state, state])
    got, total = pair_total(send, keep, coef)
    (inside,) = kernel(intra_body, "intra", [], [low, q, k, v], [wide_f], [total])
    base = back_project([0], "back_own", [grad], None, [inside])
    own, other = exchange(total, keep, got, coef, True, [lambda _: [inside], lambda _: [base]])
    normed_f, inv, normed = kernel(
        norm_body, "normalise", [], [coef, cin, q, own, other, inside], [wide_f, wide_f, wide_b]
    )
    lot = like((tok // 2, width), BF16)
    rows = [slice(0, tok // 2), slice(tok // 2, tok)]

    def both(arrays, kind):
        return [lax.ppermute(a, "head", kind) for a in arrays]

    def turn(h, deps):
        return kernel(functools.partial(turn_body, rows[h]), "turn", [], [coef, n2[h], p2, i2[h]], [lot, lot], deps)

    def turn_again(h, deps):
        return kernel(functools.partial(turn_again_body, rows[h]), "turn", [], [n3[h], i3[h], p3, p1], [lot, lot], deps)

    p3 = project(3, "project_3")
    g1, g3_inner, _ = lax.optimization_barrier((g1, g3_inner, p3))
    n2a, i2a, n2b, i2b = kernel(first_body, "pick", [], [coef, g1, p3, g3_inner], [lot] * 4)
    n2a, i2a = lax.ppermute(n2a, "head", neighbours), lax.ppermute(i2a, "head", inner)
    n2b, i2b = lax.ppermute(n2b, "head", neighbours), lax.ppermute(i2b, "head", inner)
    n2, i2 = [n2a, n2b], [i2a, i2b]
    p2 = project(2, "project_2", [p3])
    s2a, n3a = turn(0, [])
    i3a, n3a = lax.ppermute(s2a, "head", inner), lax.ppermute(n3a, "head", neighbours)
    p1 = project(1, "project_1", [s2a])
    p0 = project(0, "project_0", [p1])
    base = back_project([1], "back_1", [g1], base, [p0])
    s2b, n3b = turn(1, [base])
    i3b, n3b = lax.ppermute(s2b, "head", inner), lax.ppermute(n3b, "head", neighbours)
    n3, i3 = [n3a, n3b], [i3a, i3b]
    (g2,) = kernel(ends_body, "pick", [], [coef, n2a, i2a, n2b, i2b], [part], [s2b])
    base = back_project([2], "back_2", [g2], base)
    (w3,) = kernel(functools.partial(block_body, 3), "block", [info], [w], [like((feats, width), BF16)], [base])
    s1a, s3a = turn_again(0, [w3])
    n4a = lax.ppermute(s1a, "head", neighbours)
    ag_ins = [g3_inner, base, normed_f, inv, q]
    aga, states = kernel(
        functools.partial(att_grad_first_body, rows[0]), "attended_grads", [], [coef, cin, w3, n3a, *ag_ins],
        [like((tok // 2, feats), BF16), like((heads, DH, DH), F32)], [s1a],
    )
    s3a, _ = lax.optimization_barrier((s3a, aga))
    i4a = lax.ppermute(s3a, "head", inner)
    half_f = like((tok // 2, feats), F32)
    qga, kga, vga = kernel(
        functools.partial(first_grads_body, rows[0]), "first_grads", [],
        [low, low_t, coef, cin, q, k, v, aga, own, other], [like((tok // 2, feats), BF16), half_f, half_f],
    )
    ag, gsend, gkeep = kernel(
        functools.partial(att_grad_second_body, rows[1]), "attended_grads", [],
        [states, coef, cin, w3, n3b, *ag_ins], [like((tok // 2, feats), BF16), state, state], [qga],
    )
    ggot, gtotal = pair_total(gsend, gkeep, coefb)
    s1b, s3b = turn_again(1, [gsend])
    n4b, i4b = lax.ppermute(s1b, "head", neighbours), lax.ppermute(s3b, "head", inner)
    kp, vp = kernel(
        functools.partial(key_value_body, rows[1]), "key_value_grads", [],
        [low_t, q, k, v, ag, kga, vga], [wide_f, wide_f], [gtotal],
    )
    grads = []

    def beside_second(sent):
        query_grad, mark = kernel(
            functools.partial(query_grad_body, rows[1]), "query_grad", [],
            [low, coef, cin, k, v, ag, own, other, qga], [wide_b, like((8, DH), F32)], [sent],
        )
        grads.append(query_grad)
        return [mark]

    leaving, leaving_other = exchange(gtotal, gkeep, ggot, coefb, False, [lambda _: [kp], beside_second])
    (query_grad,) = grads
    mixed, mark = mix_half(0, p0, [n4a, i4a], [leaving])
    key_grad, value_grad, mark = kernel(
        last_body, "last_grads", [], [coef, cout, k, v, leaving, leaving_other, kp, vp],
        [wide_b, wide_b, like((8, DH), F32)], [mark], hbm_outs=2,
        scratch=[pltpu.VMEM((tok, feats), BF16)] * 2 + [pltpu.SemaphoreType.DMA((2, feats // TILE))],
    )
    mixed = mix_half(1, p0, [n4b, i4b], [mark], mixed)
    return mixed, query_grad, key_grad, value_grad


def solution(mesh):
    return jax.shard_map(
        shards,
        mesh=mesh,
        in_specs=(
            P("ctx", "head"),
            P("ctx", "head"),
            P("ctx", "head"),
            P(),
            P("head", None),
            P("ctx", "head"),
        ),
        out_specs=(P("ctx", "head"), P("ctx", "head"), P("ctx", "head"), P("ctx", "head")),
        check_vma=False,
    )
```

```python
import functools

import jax
import jax.numpy as jnp
from jax import lax
from jax.experimental import pallas as pl
from jax.experimental.pallas import tpu as pltpu
from jax.sharding import PartitionSpec as P

DH = 128
EPS = 1e-06
F32 = jnp.float32
BF16 = jnp.bfloat16
MIB = 1024 * 1024

RATE = 10**8
MICROSECONDS = {
    "setup": 100.0, "local_states": 0.8, "intra": 3.0, "back_own": 1.8, "pair_total": 0.1, "exchange_stage": 0.1,
    "exchange_last": 0.1, "normalise": 0.9, "project_3": 1.8, "project_2": 1.8, "project_1": 1.8,
    "project_0": 1.8, "back_1": 1.8, "pick": 0.3, "turn": 0.5, "back_2": 1.8, "attended_grads": 2.0, "first_grads": 2.0, "block": 0.5,
    "query_grad": 0.01, "key_value_grads": 0.01, "last_grads": 0.01,
}

I_BLK, I_CORE, I_Z, I_DOCS = 0, 1, 2, 3


def kernel(body, name, smem, ins, outs, deps=(), spare=8, hbm_outs=0, scratch=()):
    n, n_dep = len(smem) + len(ins), len(deps)

    def inner(*refs):
        body(*refs[:n], *refs[n + n_dep:])

    size = sum(a.size * a.dtype.itemsize for a in list(ins) + list(outs))
    spec = lambda space: pl.BlockSpec(memory_space=space)
    return pl.pallas_call(
        inner,
        name=name,
        in_specs=[spec(pltpu.SMEM)] * len(smem) + [spec(pltpu.VMEM)] * len(ins) + [spec(pl.ANY)] * n_dep,
        out_specs=[spec(pltpu.HBM)] * hbm_outs + [spec(pltpu.VMEM)] * (len(outs) - hbm_outs),
        out_shape=list(outs),
        scratch_shapes=list(scratch),
        compiler_params=pltpu.CompilerParams(vmem_limit_bytes=size + spare * MIB),
        cost_estimate=pl.CostEstimate(
            flops=int(MICROSECONDS[name] * RATE), bytes_accessed=0, transcendentals=0
        ),
    )(*smem, *ins, *deps)


def like(shape, dtype):
    return jax.ShapeDtypeStruct(shape, dtype)


def dot(a, b, ca, cb):
    return lax.dot_general(a, b, (((ca,), (cb,)), ((), ())), preferred_element_type=F32)


def head(h):
    return slice(h * DH, (h + 1) * DH)


def starts_of(info_ref):
    out, at = [], jnp.int32(0)
    for j in range(I_DOCS, info_ref.shape[0] - 1):
        at = at + info_ref[j]
        out.append(at)
    return out


def start_at(starts, p):
    best = jnp.minimum(p, 0)
    best = jnp.maximum(best, -1)
    for s in starts:
        best = jnp.where(p >= s, s, best)
    return best


def line(tok, axis):
    return lax.broadcasted_iota(jnp.int32, (tok, 1) if axis == 0 else (1, tok), axis)


def carries(info_ref, tok):
    first = info_ref[I_BLK] * tok
    starts = starts_of(info_ref)
    rows = start_at(starts, line(tok, 0) + first)
    return rows == start_at(starts, first - 1), rows == start_at(starts, first + tok - 1)


def visible(low_ref, axis, t0, t1, s1):
    low = low_ref[t0:t1, :1] if axis == 0 else low_ref[:1, t0:t1]
    t, s = line(t1 - t0, axis) + t0, line(s1, 1 - axis)
    return (s <= t) & (s >= low)


def same(starts, tok, a, b):
    pa, pb = a * tok + tok - 1, b * tok + tok - 1
    one = (a >= 0) | (b < 0)
    for s in starts:
        one = jnp.logical_and(one, jnp.logical_not(jnp.logical_and(pa < s, s <= pb)))
    return jnp.where(one, 1.0, 0.0).astype(F32)


def stages(n, forward):
    out, m = [], 2
    while m < n:
        r = 2
        out.append((m, r, m * r >= n))
        m *= r
    return out


def coefficients(starts, tok, n, blk, forward):
    link = functools.partial(same, starts, tok)
    core = lax.rem(blk, 2)
    first = blk - core
    one, none = jnp.float32(1.0), jnp.float32(0.0)
    if forward:
        near, inner, outer = core == 0, link(first, first + 1), link(first - 1, first)
    else:
        near, inner, outer = core == 1, link(first - 1, first), link(first, first + 1)
    out = [jnp.where(near, inner, one), jnp.where(near, one, inner)]
    for m, r, last in stages(n, forward):
        low = blk // (m * r) * (m * r)
        digit = lax.rem(blk // m, r)
        for x in range(1, r):
            j = jnp.bitwise_xor(digit, x)
            if forward:
                out.append(jnp.where(j < digit, link(low + (j + 1) * m - 1, first - 1), none))
            else:
                out.append(jnp.where(j > digit, link(first + 1, low + j * m - 1), none))
        if not last:
            for x in range(r):
                j = jnp.bitwise_xor(digit, x)
                if forward:
                    out.append(link(low + (j + 1) * m - 1, low + r * m - 1))
                else:
                    out.append(link(low - 1, low + j * m - 1))
    return out + [jnp.where(near, one, none), outer]


def pair_body(c_ref, mine_ref, got_ref, total_ref):
    a, b = c_ref[0:1, :], c_ref[1:2, :]
    total_ref[...] = (mine_ref[...].astype(F32) * a + got_ref[...].astype(F32) * b).astype(BF16)


def stage_body(row, r, last, begun, c_ref, *refs):
    refs = list(refs)
    others = [refs.pop(0)[...].astype(F32) for _ in range(r - 1)]
    entering = refs.pop(0)[...] if begun else None
    for other in others:
        part = other * c_ref[row:row + 1, :]
        entering = part if entering is None else entering + part
        row += 1
    if not last:
        total_ref, new_total_ref, entering_ref = refs
        entering_ref[...] = entering
        total = total_ref[...].astype(F32) * c_ref[row:row + 1, :]
        for other in others:
            row += 1
            total = total + other * c_ref[row:row + 1, :]
        new_total_ref[...] = total.astype(BF16)
        return
    mine_ref, got_ref, own_ref, away_ref = refs
    near, outer = c_ref[row:row + 1, :], c_ref[row + 1:row + 2, :]
    nearer = mine_ref[...].astype(F32) * near + got_ref[...].astype(F32) * (1.0 - near)
    chained = nearer + outer * entering
    own_ref[...] = (entering * near + chained * (1.0 - near)).astype(BF16)
    away_ref[...] = (chained * near + entering * (1.0 - near)).astype(BF16)


def pair_total(send, keep, coef):
    n = lax.axis_size("ctx")
    got = lax.ppermute(send, "ctx", [(i, i ^ 1) for i in range(n)])
    (total,) = kernel(pair_body, "pair_total", [], [coef, keep, got], [like(keep.shape, BF16)])
    return got, total


def exchange(total, keep, got, coef, forward, beside):
    n = lax.axis_size("ctx")
    swap = [(i, i ^ 1) for i in range(n)]
    half = like(keep.shape, BF16)
    entering, row = [], 2
    for m, r, last in stages(n, forward):
        others = []
        for x in range(1, r):
            others.append(lax.ppermute(total, "ctx", [(i, i ^ (x * m)) for i in range(n)]))
        deps = beside.pop(0)(total) if beside else ()
        body = functools.partial(stage_body, row, r, last, bool(entering))
        if last:
            own, away = kernel(
                body, "exchange_last", [], [coef, *others, *entering, keep, got], [half, half], deps
            )
        else:
            total, e = kernel(
                body, "exchange_stage", [], [coef, *others, *entering, total],
                [half, like(keep.shape, F32)], deps,
            )
            entering = [e]
            row += 2 * r - 1
    return own, lax.ppermute(away, "ctx", swap)


TILE = 256
ROWS = 32
C_CORE, C_END = ROWS - 1, ROWS - 2


def put_states(states, c_ref, keep_ref, send_ref):
    half = len(states) // 2
    core0 = c_ref[C_CORE:C_CORE + 1, :] > 0.5
    for i in range(half):
        keep_ref[i] = jnp.where(core0, states[i], states[i + half]).astype(BF16)
        send_ref[i] = jnp.where(core0, states[i + half], states[i]).astype(BF16)


def setup_body(n, tok, info_ref, coef_ref, coefb_ref, cin_ref, cout_ref, low_ref, low_t_ref):
    blk, core = info_ref[I_BLK], info_ref[I_CORE]
    starts = starts_of(info_ref)
    for ref, forward in ((coef_ref, True), (coefb_ref, False)):
        ref[...] = jnp.zeros_like(ref)
        for i, c in enumerate(coefficients(starts, tok, n, blk, forward)):
            ref[i:i + 1, :] = jnp.full((1, DH), c, F32)
        ref[C_CORE:C_CORE + 1, :] = jnp.full((1, DH), jnp.where(core == 0, 1.0, 0.0), F32)
        end = jnp.logical_or(info_ref[I_Z] == 0, info_ref[I_Z] == 3)
        ref[C_END:C_END + 1, :] = jnp.full((1, DH), jnp.where(end, 1.0, 0.0), F32)
    cin, cout = carries(info_ref, tok)
    cin_ref[...] = jnp.broadcast_to(jnp.where(cin, 1.0, 0.0), cin_ref.shape)
    cout_ref[...] = jnp.broadcast_to(jnp.where(cout, 1.0, 0.0), cout_ref.shape)
    first = blk * tok
    for ref, axis in ((low_ref, 0), (low_t_ref, 1)):
        low = start_at(starts, line(tok, axis) + first) - first
        ref[...] = jnp.broadcast_to(low, ref.shape)


def states_body(c_ref, cout_ref, k_ref, v_ref, send_ref, keep_ref):
    zero = jnp.zeros((), BF16)
    cout = cout_ref[...] > 0.5
    states = []
    for h in range(k_ref.shape[1] // DH):
        kept = jnp.where(cout, k_ref[:, head(h)], zero)
        states.append(dot(kept, v_ref[:, head(h)], 0, 0))
    put_states(states, c_ref, keep_ref, send_ref)


def intra_body(low_ref, q_ref, k_ref, v_ref, out_ref):
    tok = q_ref.shape[0]
    mask = visible(low_ref, 0, 0, tok, tok)
    for h in range(q_ref.shape[1] // DH):
        s = dot(q_ref[:, head(h)], k_ref[:, head(h)], 1, 1)
        s = jnp.where(mask, s, 0.0).astype(BF16)
        out_ref[:, head(h)] = dot(s, v_ref[:, head(h)], 1, 0)


def pick(c_ref, own_ref, back_ref, h):
    half = own_ref.shape[0]
    core0 = c_ref[C_CORE:C_CORE + 1, :] > 0.5
    a, b = own_ref[h % half].astype(F32), back_ref[h % half].astype(F32)
    return (jnp.where(core0, a, b) if h < half else jnp.where(core0, b, a)).astype(BF16)


def norm_body(c_ref, cin_ref, q_ref, own_ref, back_ref, a_ref, normed_ref, inv_ref, n_ref):
    wide = q_ref.shape[1]
    for h in range(wide // DH):
        inter = dot(q_ref[:, head(h)], pick(c_ref, own_ref, back_ref, h), 1, 0)
        att = a_ref[:, head(h)] + cin_ref[...] * inter
        inv = lax.rsqrt(jnp.mean(att * att, axis=-1, keepdims=True) + EPS)
        normed = att * inv
        inv_ref[:, head(h)] = jnp.broadcast_to(inv, att.shape)
        normed_ref[:, head(h)] = normed
        n_ref[:, head(h)] = normed.astype(BF16)


def columns(info_ref, block, width):
    return pl.multiple_of(jnp.bitwise_xor(info_ref[I_Z], block) * width, width)


def project_body(block, info_ref, n_ref, w_ref, out_ref):
    width = out_ref.shape[1]
    base = columns(info_ref, block, width)
    for i in range(width // TILE):
        at = pl.multiple_of(base + i * TILE, TILE)
        out_ref[:, i * TILE:(i + 1) * TILE] = dot(
            n_ref[...], w_ref[:, pl.ds(at, TILE)], 1, 0
        ).astype(BF16)


def back_body(blocks, based, info_ref, w_ref, *refs):
    out_ref = refs[-1]
    feats = out_ref.shape[1]
    for i in range(feats // TILE):
        rows = slice(i * TILE, (i + 1) * TILE)
        acc = refs[-2][:, rows] if based else None
        for block, g_ref in zip(blocks, refs, strict=False):
            width = g_ref.shape[1]
            at = columns(info_ref, block, width)
            part = dot(g_ref[...], w_ref[rows, pl.ds(at, width)], 1, 1)
            acc = part if acc is None else acc + part
        out_ref[:, rows] = acc


def block_body(block, info_ref, w_ref, out_ref):
    width = out_ref.shape[1]
    out_ref[...] = w_ref[:, pl.ds(columns(info_ref, block, width), width)]


def att_grad(rows, c_ref, cin_ref, w_ref, n_ref, g_ref, base_ref, normed_ref, inv_ref, q_ref, ag_ref):
    wide = q_ref.shape[1]
    x = n_ref[...] * at_end(c_ref)[:, :1] + g_ref[rows, :]
    zero = jnp.zeros((), BF16)
    cin = cin_ref[rows, :] > 0.5
    states = []
    for i in range(wide // TILE):
        feats = slice(i * TILE, (i + 1) * TILE)
        ng2 = base_ref[rows, feats] + dot(x, w_ref[feats, :], 1, 1)
        for j in range(TILE // DH):
            at = head(i * (TILE // DH) + j)
            ng, normed = ng2[:, head(j)], normed_ref[rows, at]
            proj = jnp.mean(ng * normed, axis=-1, keepdims=True)
            ag = ((ng - normed * proj) * inv_ref[rows, at]).astype(BF16)
            ag_ref[:, at] = ag
            states.append(dot(jnp.where(cin, q_ref[rows, at], zero), ag, 0, 0))
    return states


def att_grad_first_body(rows, *refs):
    for h, state in enumerate(att_grad(rows, *refs[:-1])):
        refs[-1][h] = state


def att_grad_second_body(rows, before_ref, *refs):
    send_ref, keep_ref = refs[-2:]
    states = att_grad(rows, *refs[:-2])
    put_states([before_ref[h] + state for h, state in enumerate(states)], refs[0], keep_ref, send_ref)


def query_grad(h, rows, s1, mask, c_ref, cin_ref, k_ref, v_ref, ag_ref, own_ref, back_ref):
    ag, at = ag_ref[:, head(h)], head(h)
    inter = dot(ag, pick(c_ref, own_ref, back_ref, h), 1, 1)
    g = jnp.where(mask, dot(ag, v_ref[:s1, at], 1, 1), 0.0).astype(BF16)
    return (dot(g, k_ref[:s1, at], 1, 0) + cin_ref[rows, :] * inter).astype(BF16)


def key_value_grad(h, rows, s1, mask, q_ref, k_ref, v_ref, ag_ref):
    at = head(h)
    q, ag = q_ref[rows, at], ag_ref[:, at]
    st = jnp.where(mask, dot(k_ref[:s1, at], q, 1, 1), 0.0).astype(BF16)
    gt = jnp.where(mask, dot(v_ref[:s1, at], ag, 1, 1), 0.0).astype(BF16)
    return dot(gt, q, 1, 0), dot(st, ag, 1, 0)


def first_grads_body(rows, low_ref, low_t_ref, c_ref, cin_ref, q_ref, k_ref, v_ref, ag_ref, own_ref, back_ref, qg_ref, kg_ref, vg_ref):
    r1 = rows.stop
    mask, mask_t = visible(low_ref, 0, 0, r1, r1), visible(low_t_ref, 1, 0, r1, r1)
    for h in range(q_ref.shape[1] // DH):
        qg_ref[:, head(h)] = query_grad(h, rows, r1, mask, c_ref, cin_ref, k_ref, v_ref, ag_ref, own_ref, back_ref)
        kg, vg = key_value_grad(h, rows, r1, mask_t, q_ref, k_ref, v_ref, ag_ref)
        kg_ref[:, head(h)] = kg
        vg_ref[:, head(h)] = vg


def query_grad_body(rows, low_ref, c_ref, cin_ref, k_ref, v_ref, ag_ref, own_ref, back_ref, first_ref, qg_ref, mark_ref):
    r0, r1 = rows.start, rows.stop
    mask = visible(low_ref, 0, r0, r1, r1)
    mark_ref[...] = jnp.zeros_like(mark_ref)
    qg_ref[:r0, :] = first_ref[...]
    for h in range(k_ref.shape[1] // DH):
        qg_ref[rows, head(h)] = query_grad(h, rows, r1, mask, c_ref, cin_ref, k_ref, v_ref, ag_ref, own_ref, back_ref)


def key_value_body(rows, low_t_ref, q_ref, k_ref, v_ref, ag_ref, k_first_ref, v_first_ref, kg_ref, vg_ref):
    r0, r1 = rows.start, rows.stop
    mask = visible(low_t_ref, 1, r0, r1, r1)
    for h in range(q_ref.shape[1] // DH):
        at = head(h)
        kg, vg = key_value_grad(h, rows, r1, mask, q_ref, k_ref, v_ref, ag_ref)
        for ref, first_ref, new in ((kg_ref, k_first_ref, kg), (vg_ref, v_first_ref, vg)):
            ref[:r0, at] = first_ref[:, at] + new[:r0]
            ref[r0:, at] = new[r0:]


def last_body(c_ref, cout_ref, k_ref, v_ref, own_ref, back_ref, kp_ref, vp_ref, kg_hbm, vg_hbm, mark_ref, kg_ref, vg_ref, sem):
    mark_ref[...] = jnp.zeros_like(mark_ref)
    cout = cout_ref[...]
    copies = []
    for i in range(k_ref.shape[1] // TILE):
        for h in range(i * (TILE // DH), (i + 1) * (TILE // DH)):
            leaving = pick(c_ref, own_ref, back_ref, h)
            kg = cout * dot(v_ref[:, head(h)], leaving, 1, 1)
            vg = cout * dot(k_ref[:, head(h)], leaving, 1, 0)
            kg_ref[:, head(h)] = (kp_ref[:, head(h)] + kg).astype(BF16)
            vg_ref[:, head(h)] = (vp_ref[:, head(h)] + vg).astype(BF16)
        at = slice(i * TILE, (i + 1) * TILE)
        for j, (src, dst) in enumerate(((kg_ref, kg_hbm), (vg_ref, vg_hbm))):
            copies.append(pltpu.make_async_copy(src.at[:, at], dst.at[:, at], sem.at[j, i]))
            copies[-1].start()
    for copy in copies:
        copy.wait()


def sum_body(*refs):
    total = refs[0][...].astype(F32)
    for r in refs[1:-1]:
        total = total + r[...].astype(F32)
    refs[-1][...] = total.astype(BF16)


def at_end(c_ref):
    return c_ref[C_END:C_END + 1, :].astype(BF16)


def end_body(c_ref, a_ref, b_ref, out_ref):
    end = at_end(c_ref)
    for i in range(out_ref.shape[1] // DH):
        out_ref[:, head(i)] = a_ref[:, head(i)] * end + b_ref[:, head(i)]


def first_body(c_ref, g1_ref, p3_ref, g3_ref, *out_refs):
    r0 = 0
    for n_ref, i_ref in zip(out_refs[::2], out_refs[1::2], strict=True):
        rows = slice(r0, r0 + n_ref.shape[0])
        i_ref[...] = g1_ref[rows, :]
        end_body(c_ref, p3_ref.at[rows, :], g3_ref.at[rows, :], n_ref)
        r0 = rows.stop


def ends_body(c_ref, *refs):
    out_ref = refs[-1]
    r0 = 0
    for a_ref, b_ref in zip(refs[:-1:2], refs[1:-1:2], strict=True):
        rows = slice(r0, r0 + a_ref.shape[0])
        end_body(c_ref, a_ref, b_ref, out_ref.at[rows, :])
        r0 = rows.stop


def turn_body(rows, c_ref, n2_ref, p2_ref, i2_ref, s2_ref, n3_ref):
    s2_ref[...] = p2_ref[rows, :] + n2_ref[...]
    end_body(c_ref, p2_ref.at[rows, :], i2_ref, n3_ref)


def turn_again_body(rows, n3_ref, i3_ref, p3_ref, p1_ref, s1_ref, s3_ref):
    s3_ref[...] = p3_ref[rows, :] + n3_ref[...]
    s1_ref[...] = p1_ref[rows, :] + i3_ref[...]


def mix_body(n_dep, p_ref, a_ref, b_ref, *refs):
    total = p_ref[...].astype(F32) + a_ref[...].astype(F32) + b_ref[...].astype(F32)
    refs[n_dep][...] = total.astype(BF16)
    if len(refs) > n_dep + 1:
        refs[-1][...] = jnp.zeros_like(refs[-1])


def mix_half(half, p0, parts, deps, into=None):
    tok, width = p0.shape
    lot = tok // 2
    mine = pl.BlockSpec((lot, width), lambda i: (half, 0))
    whole = pl.BlockSpec((lot, width), lambda i: (0, 0))
    extra = list(deps) + ([] if into is None else [into])
    first = into is None
    out = pl.pallas_call(
        functools.partial(mix_body, len(extra)),
        name="mixed",
        grid=(1,),
        in_specs=[mine, whole, whole] + [pl.BlockSpec(memory_space=pl.ANY)] * len(extra),
        out_specs=[mine] + [pl.BlockSpec((8, DH), lambda i: (0, 0))] * first,
        out_shape=[like((tok, width), BF16)] + [like((8, DH), F32)] * first,
        input_output_aliases={} if first else {2 + len(extra): 0},
        compiler_params=pltpu.CompilerParams(vmem_limit_bytes=12 * MIB),
        cost_estimate=pl.CostEstimate(flops=RATE, bytes_accessed=0, transcendentals=0),
    )(p0, *parts, *extra)
    return out if first else out[0]


def shards(q, k, v, lens, w, grad):
    tok, width = grad.shape
    feats = w.shape[0]
    heads = feats // DH
    half = heads // 2
    n = lax.axis_size("ctx")
    blk = lax.axis_index("ctx").astype(jnp.int32)
    z = lax.axis_index("head").astype(jnp.int32)
    info = jnp.concatenate([jnp.stack([blk, blk % 2, z]), lens])
    part = like((tok, width), BF16)
    wide_b, wide_f = like((tok, feats), BF16), like((tok, feats), F32)
    state = like((half, DH, DH), BF16)
    lanes = like((tok, DH), F32)
    table = like((ROWS, DH), F32)

    def project(block, name, deps=()):
        body = functools.partial(project_body, block)
        return kernel(body, name, [info], [normed, w], [part], deps)[0]

    def back_project(blocks, name, grads, base=None, deps=()):
        body = functools.partial(back_body, blocks, base is not None)
        return kernel(body, name, [info], [w, *grads] + ([] if base is None else [base]), [wide_f], deps)[0]

    neighbours = [(0, 1), (1, 0), (2, 3), (3, 2)]
    inner = [(1, 2), (2, 1)]
    g1 = lax.ppermute(grad, "head", neighbours)
    g3_inner = lax.ppermute(grad, "head", inner)
    coef, coefb, cin, cout, low, low_t = kernel(
        functools.partial(setup_body, n, tok), "setup", [info], [],
        [table, table, lanes, lanes, like((tok, DH), jnp.int32), like((8, tok), jnp.int32)],
    )
    send, keep = kernel(states_body, "local_states", [], [coef, cout, k, v], [state, state])
    got, total = pair_total(send, keep, coef)
    (inside,) = kernel(intra_body, "intra", [], [low, q, k, v], [wide_f], [total])
    base = back_project([0], "back_own", [grad], None, [inside])
    own, other = exchange(total, keep, got, coef, True, [lambda _: [inside], lambda _: [base]])
    normed_f, inv, normed = kernel(
        norm_body, "normalise", [], [coef, cin, q, own, other, inside], [wide_f, wide_f, wide_b]
    )
    lot = like((tok // 2, width), BF16)
    rows = [slice(0, tok // 2), slice(tok // 2, tok)]

    def both(arrays, kind):
        return [lax.ppermute(a, "head", kind) for a in arrays]

    def turn(h, deps):
        return kernel(functools.partial(turn_body, rows[h]), "turn", [], [coef, n2[h], p2, i2[h]], [lot, lot], deps)

    def turn_again(h, deps):
        return kernel(functools.partial(turn_again_body, rows[h]), "turn", [], [n3[h], i3[h], p3, p1], [lot, lot], deps)

    p3 = project(3, "project_3")
    g1, g3_inner, _ = lax.optimization_barrier((g1, g3_inner, p3))
    n2a, i2a, n2b, i2b = kernel(first_body, "pick", [], [coef, g1, p3, g3_inner], [lot] * 4)
    n2a, i2a = lax.ppermute(n2a, "head", neighbours), lax.ppermute(i2a, "head", inner)
    n2b, i2b = lax.ppermute(n2b, "head", neighbours), lax.ppermute(i2b, "head", inner)
    n2, i2 = [n2a, n2b], [i2a, i2b]
    p2 = project(2, "project_2", [p3])
    s2a, n3a = turn(0, [])
    i3a, n3a = lax.ppermute(s2a, "head", inner), lax.ppermute(n3a, "head", neighbours)
    p1 = project(1, "project_1", [s2a])
    p0 = project(0, "project_0", [p1])
    base = back_project([1], "back_1", [g1], base, [p0])
    s2b, n3b = turn(1, [base])
    i3b, n3b = lax.ppermute(s2b, "head", inner), lax.ppermute(n3b, "head", neighbours)
    n3, i3 = [n3a, n3b], [i3a, i3b]
    (g2,) = kernel(ends_body, "pick", [], [coef, n2a, i2a, n2b, i2b], [part], [s2b])
    base = back_project([2], "back_2", [g2], base)
    (w3,) = kernel(functools.partial(block_body, 3), "block", [info], [w], [like((feats, width), BF16)], [base])
    s1a, s3a = turn_again(0, [w3])
    n4a = lax.ppermute(s1a, "head", neighbours)
    ag_ins = [g3_inner, base, normed_f, inv, q]
    aga, states = kernel(
        functools.partial(att_grad_first_body, rows[0]), "attended_grads", [], [coef, cin, w3, n3a, *ag_ins],
        [like((tok // 2, feats), BF16), like((heads, DH, DH), F32)], [s1a],
    )
    s3a, _ = lax.optimization_barrier((s3a, aga))
    i4a = lax.ppermute(s3a, "head", inner)
    half_f = like((tok // 2, feats), F32)
    qga, kga, vga = kernel(
        functools.partial(first_grads_body, rows[0]), "first_grads", [],
        [low, low_t, coef, cin, q, k, v, aga, own, other], [like((tok // 2, feats), BF16), half_f, half_f],
    )
    ag, gsend, gkeep = kernel(
        functools.partial(att_grad_second_body, rows[1]), "attended_grads", [],
        [states, coef, cin, w3, n3b, *ag_ins], [like((tok // 2, feats), BF16), state, state], [qga],
    )
    ggot, gtotal = pair_total(gsend, gkeep, coefb)
    s1b, s3b = turn_again(1, [gsend])
    n4b, i4b = lax.ppermute(s1b, "head", neighbours), lax.ppermute(s3b, "head", inner)
    kp, vp = kernel(
        functools.partial(key_value_body, rows[1]), "key_value_grads", [],
        [low_t, q, k, v, ag, kga, vga], [wide_f, wide_f], [gtotal],
    )
    grads = []

    def beside_second(sent):
        query_grad, mark = kernel(
            functools.partial(query_grad_body, rows[1]), "query_grad", [],
            [low, coef, cin, k, v, ag, own, other, qga], [wide_b, like((8, DH), F32)], [sent],
        )
        grads.append(query_grad)
        return [mark]

    leaving, leaving_other = exchange(gtotal, gkeep, ggot, coefb, False, [lambda _: [kp], beside_second])
    (query_grad,) = grads
    mixed, mark = mix_half(0, p0, [n4a, i4a], [leaving])
    key_grad, value_grad, mark = kernel(
        last_body, "last_grads", [], [coef, cout, k, v, leaving, leaving_other, kp, vp],
        [wide_b, wide_b, like((8, DH), F32)], [mark], hbm_outs=2,
        scratch=[pltpu.VMEM((tok, feats), BF16)] * 2 + [pltpu.SemaphoreType.DMA((2, feats // TILE))],
    )
    mixed = mix_half(1, p0, [n4b, i4b], [mark], mixed)
    return mixed, query_grad, key_grad, value_grad


def solution(mesh):
    return jax.shard_map(
        shards,
        mesh=mesh,
        in_specs=(
            P("ctx", "head"),
            P("ctx", "head"),
            P("ctx", "head"),
            P(),
            P("head", None),
            P("ctx", "head"),
        ),
        out_specs=(P("ctx", "head"), P("ctx", "head"), P("ctx", "head"), P("ctx", "head")),
        check_vma=False,
    )
```

```python
import functools

import jax
import jax.numpy as jnp
from jax import lax
from jax.experimental import pallas as pl
from jax.experimental.pallas import tpu as pltpu
from jax.sharding import PartitionSpec as P

DH = 128
EPS = 1e-06
F32 = jnp.float32
BF16 = jnp.bfloat16
MIB = 1024 * 1024

RATE = 10**8
MICROSECONDS = {
    "setup": 100.0, "local_states": 0.8, "intra": 3.0, "back_own": 1.8, "pair_total": 0.1, "exchange_stage": 0.1,
    "exchange_last": 0.1, "normalise": 0.9, "project_3": 1.8, "project_2": 1.8, "project_1": 1.8,
    "project_0": 1.8, "back_1": 1.8, "pick": 0.3, "turn": 0.5, "back_2": 1.8, "attended_grads": 2.0, "first_grads": 2.0, "block": 0.5,
    "query_grad": 0.01, "key_value_grads": 0.01, "last_grads": 0.01,
}

I_BLK, I_CORE, I_Z, I_DOCS = 0, 1, 2, 3


def kernel(body, name, smem, ins, outs, deps=(), spare=8, hbm_outs=0, scratch=()):
    n, n_dep = len(smem) + len(ins), len(deps)

    def inner(*refs):
        body(*refs[:n], *refs[n + n_dep:])

    size = sum(a.size * a.dtype.itemsize for a in list(ins) + list(outs))
    spec = lambda space: pl.BlockSpec(memory_space=space)
    return pl.pallas_call(
        inner,
        name=name,
        in_specs=[spec(pltpu.SMEM)] * len(smem) + [spec(pltpu.VMEM)] * len(ins) + [spec(pl.ANY)] * n_dep,
        out_specs=[spec(pltpu.HBM)] * hbm_outs + [spec(pltpu.VMEM)] * (len(outs) - hbm_outs),
        out_shape=list(outs),
        scratch_shapes=list(scratch),
        compiler_params=pltpu.CompilerParams(vmem_limit_bytes=size + spare * MIB),
        cost_estimate=pl.CostEstimate(
            flops=int(MICROSECONDS[name] * RATE), bytes_accessed=0, transcendentals=0
        ),
    )(*smem, *ins, *deps)


def like(shape, dtype):
    return jax.ShapeDtypeStruct(shape, dtype)


def dot(a, b, ca, cb):
    return lax.dot_general(a, b, (((ca,), (cb,)), ((), ())), preferred_element_type=F32)


def head(h):
    return slice(h * DH, (h + 1) * DH)


def starts_of(info_ref):
    out, at = [], jnp.int32(0)
    for j in range(I_DOCS, info_ref.shape[0] - 1):
        at = at + info_ref[j]
        out.append(at)
    return out


def start_at(starts, p):
    best = jnp.minimum(p, 0)
    best = jnp.maximum(best, -1)
    for s in starts:
        best = jnp.where(p >= s, s, best)
    return best


def line(tok, axis):
    return lax.broadcasted_iota(jnp.int32, (tok, 1) if axis == 0 else (1, tok), axis)


def carries(info_ref, tok):
    first = info_ref[I_BLK] * tok
    starts = starts_of(info_ref)
    rows = start_at(starts, line(tok, 0) + first)
    return rows == start_at(starts, first - 1), rows == start_at(starts, first + tok - 1)


def visible(low_ref, axis, t0, t1, s1):
    low = low_ref[t0:t1, :1] if axis == 0 else low_ref[:1, t0:t1]
    t, s = line(t1 - t0, axis) + t0, line(s1, 1 - axis)
    return (s <= t) & (s >= low)


def same(starts, tok, a, b):
    pa, pb = a * tok + tok - 1, b * tok + tok - 1
    one = (a >= 0) | (b < 0)
    for s in starts:
        one = jnp.logical_and(one, jnp.logical_not(jnp.logical_and(pa < s, s <= pb)))
    return jnp.where(one, 1.0, 0.0).astype(F32)


def stages(n, forward):
    out, m = [], 2
    while m < n:
        r = 2
        out.append((m, r, m * r >= n))
        m *= r
    return out


def coefficients(starts, tok, n, blk, forward):
    link = functools.partial(same, starts, tok)
    core = lax.rem(blk, 2)
    first = blk - core
    one, none = jnp.float32(1.0), jnp.float32(0.0)
    if forward:
        near, inner, outer = core == 0, link(first, first + 1), link(first - 1, first)
    else:
        near, inner, outer = core == 1, link(first - 1, first), link(first, first + 1)
    out = [jnp.where(near, inner, one), jnp.where(near, one, inner)]
    for m, r, last in stages(n, forward):
        low = blk // (m * r) * (m * r)
        digit = lax.rem(blk // m, r)
        for x in range(1, r):
            j = jnp.bitwise_xor(digit, x)
            if forward:
                out.append(jnp.where(j < digit, link(low + (j + 1) * m - 1, first - 1), none))
            else:
                out.append(jnp.where(j > digit, link(first + 1, low + j * m - 1), none))
        if not last:
            for x in range(r):
                j = jnp.bitwise_xor(digit, x)
                if forward:
                    out.append(link(low + (j + 1) * m - 1, low + r * m - 1))
                else:
                    out.append(link(low - 1, low + j * m - 1))
    return out + [jnp.where(near, one, none), outer]


def pair_body(c_ref, mine_ref, got_ref, total_ref):
    a, b = c_ref[0:1, :], c_ref[1:2, :]
    total_ref[...] = (mine_ref[...].astype(F32) * a + got_ref[...].astype(F32) * b).astype(BF16)


def stage_body(row, r, last, begun, c_ref, *refs):
    refs = list(refs)
    others = [refs.pop(0)[...].astype(F32) for _ in range(r - 1)]
    entering = refs.pop(0)[...] if begun else None
    for other in others:
        part = other * c_ref[row:row + 1, :]
        entering = part if entering is None else entering + part
        row += 1
    if not last:
        total_ref, new_total_ref, entering_ref = refs
        entering_ref[...] = entering
        total = total_ref[...].astype(F32) * c_ref[row:row + 1, :]
        for other in others:
            row += 1
            total = total + other * c_ref[row:row + 1, :]
        new_total_ref[...] = total.astype(BF16)
        return
    mine_ref, got_ref, own_ref, away_ref = refs
    near, outer = c_ref[row:row + 1, :], c_ref[row + 1:row + 2, :]
    nearer = mine_ref[...].astype(F32) * near + got_ref[...].astype(F32) * (1.0 - near)
    chained = nearer + outer * entering
    own_ref[...] = (entering * near + chained * (1.0 - near)).astype(BF16)
    away_ref[...] = (chained * near + entering * (1.0 - near)).astype(BF16)


def pair_total(send, keep, coef):
    n = lax.axis_size("ctx")
    got = lax.ppermute(send, "ctx", [(i, i ^ 1) for i in range(n)])
    (total,) = kernel(pair_body, "pair_total", [], [coef, keep, got], [like(keep.shape, BF16)])
    return got, total


def exchange(total, keep, got, coef, forward, beside):
    n = lax.axis_size("ctx")
    swap = [(i, i ^ 1) for i in range(n)]
    half = like(keep.shape, BF16)
    entering, row = [], 2
    for m, r, last in stages(n, forward):
        others = []
        for x in range(1, r):
            others.append(lax.ppermute(total, "ctx", [(i, i ^ (x * m)) for i in range(n)]))
        deps = beside.pop(0)(total) if beside else ()
        body = functools.partial(stage_body, row, r, last, bool(entering))
        if last:
            own, away = kernel(
                body, "exchange_last", [], [coef, *others, *entering, keep, got], [half, half], deps
            )
        else:
            total, e = kernel(
                body, "exchange_stage", [], [coef, *others, *entering, total],
                [half, like(keep.shape, F32)], deps,
            )
            entering = [e]
            row += 2 * r - 1
    return own, lax.ppermute(away, "ctx", swap)


TILE = 256
ROWS = 32
C_CORE, C_END = ROWS - 1, ROWS - 2


def put_states(states, c_ref, keep_ref, send_ref):
    half = len(states) // 2
    core0 = c_ref[C_CORE:C_CORE + 1, :] > 0.5
    for i in range(half):
        keep_ref[i] = jnp.where(core0, states[i], states[i + half]).astype(BF16)
        send_ref[i] = jnp.where(core0, states[i + half], states[i]).astype(BF16)


def setup_body(n, tok, info_ref, coef_ref, coefb_ref, cin_ref, cout_ref, low_ref, low_t_ref):
    blk, core = info_ref[I_BLK], info_ref[I_CORE]
    starts = starts_of(info_ref)
    for ref, forward in ((coef_ref, True), (coefb_ref, False)):
        ref[...] = jnp.zeros_like(ref)
        for i, c in enumerate(coefficients(starts, tok, n, blk, forward)):
            ref[i:i + 1, :] = jnp.full((1, DH), c, F32)
        ref[C_CORE:C_CORE + 1, :] = jnp.full((1, DH), jnp.where(core == 0, 1.0, 0.0), F32)
        end = jnp.logical_or(info_ref[I_Z] == 0, info_ref[I_Z] == 3)
        ref[C_END:C_END + 1, :] = jnp.full((1, DH), jnp.where(end, 1.0, 0.0), F32)
    cin, cout = carries(info_ref, tok)
    cin_ref[...] = jnp.broadcast_to(jnp.where(cin, 1.0, 0.0), cin_ref.shape)
    cout_ref[...] = jnp.broadcast_to(jnp.where(cout, 1.0, 0.0), cout_ref.shape)
    first = blk * tok
    for ref, axis in ((low_ref, 0), (low_t_ref, 1)):
        low = start_at(starts, line(tok, axis) + first) - first
        ref[...] = jnp.broadcast_to(low, ref.shape)


def states_body(c_ref, cout_ref, k_ref, v_ref, send_ref, keep_ref):
    zero = jnp.zeros((), BF16)
    cout = cout_ref[...] > 0.5
    states = []
    for h in range(k_ref.shape[1] // DH):
        kept = jnp.where(cout, k_ref[:, head(h)], zero)
        states.append(dot(kept, v_ref[:, head(h)], 0, 0))
    put_states(states, c_ref, keep_ref, send_ref)


def intra_body(low_ref, q_ref, k_ref, v_ref, out_ref):
    tok = q_ref.shape[0]
    mask = visible(low_ref, 0, 0, tok, tok)
    for h in range(q_ref.shape[1] // DH):
        s = dot(q_ref[:, head(h)], k_ref[:, head(h)], 1, 1)
        s = jnp.where(mask, s, 0.0).astype(BF16)
        out_ref[:, head(h)] = dot(s, v_ref[:, head(h)], 1, 0)


def pick(c_ref, own_ref, back_ref, h):
    half = own_ref.shape[0]
    core0 = c_ref[C_CORE:C_CORE + 1, :] > 0.5
    a, b = own_ref[h % half].astype(F32), back_ref[h % half].astype(F32)
    return (jnp.where(core0, a, b) if h < half else jnp.where(core0, b, a)).astype(BF16)


def norm_body(c_ref, cin_ref, q_ref, own_ref, back_ref, a_ref, normed_ref, inv_ref, n_ref):
    wide = q_ref.shape[1]
    for h in range(wide // DH):
        inter = dot(q_ref[:, head(h)], pick(c_ref, own_ref, back_ref, h), 1, 0)
        att = a_ref[:, head(h)] + cin_ref[...] * inter
        inv = lax.rsqrt(jnp.mean(att * att, axis=-1, keepdims=True) + EPS)
        normed = att * inv
        inv_ref[:, head(h)] = jnp.broadcast_to(inv, att.shape)
        normed_ref[:, head(h)] = normed
        n_ref[:, head(h)] = normed.astype(BF16)


def columns(info_ref, block, width):
    return pl.multiple_of(jnp.bitwise_xor(info_ref[I_Z], block) * width, width)


def project_body(block, info_ref, n_ref, w_ref, out_ref):
    width = out_ref.shape[1]
    base = columns(info_ref, block, width)
    for i in range(width // TILE):
        at = pl.multiple_of(base + i * TILE, TILE)
        out_ref[:, i * TILE:(i + 1) * TILE] = dot(
            n_ref[...], w_ref[:, pl.ds(at, TILE)], 1, 0
        ).astype(BF16)


def back_body(blocks, based, info_ref, w_ref, *refs):
    out_ref = refs[-1]
    feats = out_ref.shape[1]
    for i in range(feats // TILE):
        rows = slice(i * TILE, (i + 1) * TILE)
        acc = refs[-2][:, rows] if based else None
        for block, g_ref in zip(blocks, refs, strict=False):
            width = g_ref.shape[1]
            at = columns(info_ref, block, width)
            part = dot(g_ref[...], w_ref[rows, pl.ds(at, width)], 1, 1)
            acc = part if acc is None else acc + part
        out_ref[:, rows] = acc


def block_body(block, info_ref, w_ref, out_ref):
    width = out_ref.shape[1]
    out_ref[...] = w_ref[:, pl.ds(columns(info_ref, block, width), width)]


def att_grad(rows, c_ref, cin_ref, w_ref, n_ref, g_ref, base_ref, normed_ref, inv_ref, q_ref, ag_ref):
    wide = q_ref.shape[1]
    x = n_ref[...] * at_end(c_ref)[:, :1] + g_ref[rows, :]
    zero = jnp.zeros((), BF16)
    cin = cin_ref[rows, :] > 0.5
    states = []
    for i in range(wide // TILE):
        feats = slice(i * TILE, (i + 1) * TILE)
        ng2 = base_ref[rows, feats] + dot(x, w_ref[feats, :], 1, 1)
        for j in range(TILE // DH):
            at = head(i * (TILE // DH) + j)
            ng, normed = ng2[:, head(j)], normed_ref[rows, at]
            proj = jnp.mean(ng * normed, axis=-1, keepdims=True)
            ag = ((ng - normed * proj) * inv_ref[rows, at]).astype(BF16)
            ag_ref[:, at] = ag
            states.append(dot(jnp.where(cin, q_ref[rows, at], zero), ag, 0, 0))
    return states


def att_grad_first_body(rows, *refs):
    for h, state in enumerate(att_grad(rows, *refs[:-1])):
        refs[-1][h] = state


def att_grad_second_body(rows, before_ref, *refs):
    send_ref, keep_ref = refs[-2:]
    states = att_grad(rows, *refs[:-2])
    put_states([before_ref[h] + state for h, state in enumerate(states)], refs[0], keep_ref, send_ref)


def query_grad(h, rows, s1, mask, c_ref, cin_ref, k_ref, v_ref, ag_ref, own_ref, back_ref):
    ag, at = ag_ref[:, head(h)], head(h)
    inter = dot(ag, pick(c_ref, own_ref, back_ref, h), 1, 1)
    g = jnp.where(mask, dot(ag, v_ref[:s1, at], 1, 1), 0.0).astype(BF16)
    return (dot(g, k_ref[:s1, at], 1, 0) + cin_ref[rows, :] * inter).astype(BF16)


def key_value_grad(h, rows, s1, mask, q_ref, k_ref, v_ref, ag_ref):
    at = head(h)
    q, ag = q_ref[rows, at], ag_ref[:, at]
    st = jnp.where(mask, dot(k_ref[:s1, at], q, 1, 1), 0.0).astype(BF16)
    gt = jnp.where(mask, dot(v_ref[:s1, at], ag, 1, 1), 0.0).astype(BF16)
    return dot(gt, q, 1, 0), dot(st, ag, 1, 0)


def first_grads_body(rows, low_ref, low_t_ref, c_ref, cin_ref, q_ref, k_ref, v_ref, ag_ref, own_ref, back_ref, qg_ref, kg_ref, vg_ref):
    r1 = rows.stop
    mask, mask_t = visible(low_ref, 0, 0, r1, r1), visible(low_t_ref, 1, 0, r1, r1)
    for h in range(q_ref.shape[1] // DH):
        qg_ref[:, head(h)] = query_grad(h, rows, r1, mask, c_ref, cin_ref, k_ref, v_ref, ag_ref, own_ref, back_ref)
        kg, vg = key_value_grad(h, rows, r1, mask_t, q_ref, k_ref, v_ref, ag_ref)
        kg_ref[:, head(h)] = kg
        vg_ref[:, head(h)] = vg


def query_grad_body(rows, low_ref, c_ref, cin_ref, k_ref, v_ref, ag_ref, own_ref, back_ref, first_ref, qg_ref, mark_ref):
    r0, r1 = rows.start, rows.stop
    mask = visible(low_ref, 0, r0, r1, r1)
    mark_ref[...] = jnp.zeros_like(mark_ref)
    qg_ref[:r0, :] = first_ref[...]
    for h in range(k_ref.shape[1] // DH):
        qg_ref[rows, head(h)] = query_grad(h, rows, r1, mask, c_ref, cin_ref, k_ref, v_ref, ag_ref, own_ref, back_ref)


def key_value_body(rows, low_t_ref, q_ref, k_ref, v_ref, ag_ref, k_first_ref, v_first_ref, kg_ref, vg_ref):
    r0, r1 = rows.start, rows.stop
    mask = visible(low_t_ref, 1, r0, r1, r1)
    for h in range(q_ref.shape[1] // DH):
        at = head(h)
        kg, vg = key_value_grad(h, rows, r1, mask, q_ref, k_ref, v_ref, ag_ref)
        for ref, first_ref, new in ((kg_ref, k_first_ref, kg), (vg_ref, v_first_ref, vg)):
            ref[:r0, at] = first_ref[:, at] + new[:r0]
            ref[r0:, at] = new[r0:]


def last_body(c_ref, cout_ref, k_ref, v_ref, own_ref, back_ref, kp_ref, vp_ref, kg_hbm, vg_hbm, mark_ref, kg_ref, vg_ref, sem):
    mark_ref[...] = jnp.zeros_like(mark_ref)
    cout = cout_ref[...]
    copies = []
    for i in range(k_ref.shape[1] // TILE):
        for h in range(i * (TILE // DH), (i + 1) * (TILE // DH)):
            leaving = pick(c_ref, own_ref, back_ref, h)
            kg = cout * dot(v_ref[:, head(h)], leaving, 1, 1)
            vg = cout * dot(k_ref[:, head(h)], leaving, 1, 0)
            kg_ref[:, head(h)] = (kp_ref[:, head(h)] + kg).astype(BF16)
            vg_ref[:, head(h)] = (vp_ref[:, head(h)] + vg).astype(BF16)
        at = slice(i * TILE, (i + 1) * TILE)
        for j, (src, dst) in enumerate(((kg_ref, kg_hbm), (vg_ref, vg_hbm))):
            copies.append(pltpu.make_async_copy(src.at[:, at], dst.at[:, at], sem.at[j, i]))
            copies[-1].start()
    for copy in copies:
        copy.wait()


def sum_body(*refs):
    total = refs[0][...].astype(F32)
    for r in refs[1:-1]:
        total = total + r[...].astype(F32)
    refs[-1][...] = total.astype(BF16)


def at_end(c_ref):
    return c_ref[C_END:C_END + 1, :].astype(BF16)


def end_body(c_ref, a_ref, b_ref, out_ref):
    end = at_end(c_ref)
    for i in range(out_ref.shape[1] // DH):
        out_ref[:, head(i)] = a_ref[:, head(i)] * end + b_ref[:, head(i)]


def first_body(c_ref, g1_ref, p3_ref, g3_ref, *out_refs):
    r0 = 0
    for n_ref, i_ref in zip(out_refs[::2], out_refs[1::2], strict=True):
        rows = slice(r0, r0 + n_ref.shape[0])
        i_ref[...] = g1_ref[rows, :]
        end_body(c_ref, p3_ref.at[rows, :], g3_ref.at[rows, :], n_ref)
        r0 = rows.stop


def ends_body(c_ref, *refs):
    out_ref = refs[-1]
    r0 = 0
    for a_ref, b_ref in zip(refs[:-1:2], refs[1:-1:2], strict=True):
        rows = slice(r0, r0 + a_ref.shape[0])
        end_body(c_ref, a_ref, b_ref, out_ref.at[rows, :])
        r0 = rows.stop


def turn_body(rows, c_ref, n2_ref, p2_ref, i2_ref, s2_ref, n3_ref):
    s2_ref[...] = p2_ref[rows, :] + n2_ref[...]
    end_body(c_ref, p2_ref.at[rows, :], i2_ref, n3_ref)


def turn_again_body(rows, n3_ref, i3_ref, p3_ref, p1_ref, s1_ref, s3_ref):
    s3_ref[...] = p3_ref[rows, :] + n3_ref[...]
    s1_ref[...] = p1_ref[rows, :] + i3_ref[...]


def mix_body(n_dep, rows, p_ref, a_ref, b_ref, *refs):
    total = p_ref[rows, :].astype(F32) + a_ref[...].astype(F32) + b_ref[...].astype(F32)
    refs[n_dep][...] = total.astype(BF16)
    if len(refs) > n_dep + 1:
        refs[-1][...] = jnp.zeros_like(refs[-1])


def mix_half(half, p0, parts, deps, into=None):
    tok, width = p0.shape
    lot = tok // 2
    mine = pl.BlockSpec((lot, width), lambda i: (half, 0))
    whole = pl.BlockSpec(memory_space=pltpu.VMEM)
    extra = list(deps) + ([] if into is None else [into])
    first = into is None
    out = pl.pallas_call(
        functools.partial(mix_body, len(extra), slice(half * lot, (half + 1) * lot)),
        name="mixed",
        grid=(1,),
        in_specs=[whole] * 3 + [pl.BlockSpec(memory_space=pl.ANY)] * len(extra),
        out_specs=[mine] + [pl.BlockSpec((8, DH), lambda i: (0, 0))] * first,
        out_shape=[like((tok, width), BF16)] + [like((8, DH), F32)] * first,
        input_output_aliases={} if first else {2 + len(extra): 0},
        compiler_params=pltpu.CompilerParams(vmem_limit_bytes=12 * MIB),
        cost_estimate=pl.CostEstimate(flops=RATE, bytes_accessed=0, transcendentals=0),
    )(p0, *parts, *extra)
    return out if first else out[0]


def shards(q, k, v, lens, w, grad):
    tok, width = grad.shape
    feats = w.shape[0]
    heads = feats // DH
    half = heads // 2
    n = lax.axis_size("ctx")
    blk = lax.axis_index("ctx").astype(jnp.int32)
    z = lax.axis_index("head").astype(jnp.int32)
    info = jnp.concatenate([jnp.stack([blk, blk % 2, z]), lens])
    part = like((tok, width), BF16)
    wide_b, wide_f = like((tok, feats), BF16), like((tok, feats), F32)
    state = like((half, DH, DH), BF16)
    lanes = like((tok, DH), F32)
    table = like((ROWS, DH), F32)

    def project(block, name, deps=()):
        body = functools.partial(project_body, block)
        return kernel(body, name, [info], [normed, w], [part], deps)[0]

    def back_project(blocks, name, grads, base=None, deps=()):
        body = functools.partial(back_body, blocks, base is not None)
        return kernel(body, name, [info], [w, *grads] + ([] if base is None else [base]), [wide_f], deps)[0]

    neighbours = [(0, 1), (1, 0), (2, 3), (3, 2)]
    inner = [(1, 2), (2, 1)]
    g1 = lax.ppermute(grad, "head", neighbours)
    g3_inner = lax.ppermute(grad, "head", inner)
    coef, coefb, cin, cout, low, low_t = kernel(
        functools.partial(setup_body, n, tok), "setup", [info], [],
        [table, table, lanes, lanes, like((tok, DH), jnp.int32), like((8, tok), jnp.int32)],
    )
    send, keep = kernel(states_body, "local_states", [], [coef, cout, k, v], [state, state])
    got, total = pair_total(send, keep, coef)
    (inside,) = kernel(intra_body, "intra", [], [low, q, k, v], [wide_f], [total])
    base = back_project([0], "back_own", [grad], None, [inside])
    own, other = exchange(total, keep, got, coef, True, [lambda _: [inside], lambda _: [base]])
    normed_f, inv, normed = kernel(
        norm_body, "normalise", [], [coef, cin, q, own, other, inside], [wide_f, wide_f, wide_b]
    )
    lot = like((tok // 2, width), BF16)
    rows = [slice(0, tok // 2), slice(tok // 2, tok)]

    def both(arrays, kind):
        return [lax.ppermute(a, "head", kind) for a in arrays]

    def turn(h, deps):
        return kernel(functools.partial(turn_body, rows[h]), "turn", [], [coef, n2[h], p2, i2[h]], [lot, lot], deps)

    def turn_again(h, deps):
        return kernel(functools.partial(turn_again_body, rows[h]), "turn", [], [n3[h], i3[h], p3, p1], [lot, lot], deps)

    p3 = project(3, "project_3")
    g1, g3_inner, _ = lax.optimization_barrier((g1, g3_inner, p3))
    n2a, i2a, n2b, i2b = kernel(first_body, "pick", [], [coef, g1, p3, g3_inner], [lot] * 4)
    n2a, i2a = lax.ppermute(n2a, "head", neighbours), lax.ppermute(i2a, "head", inner)
    n2b, i2b = lax.ppermute(n2b, "head", neighbours), lax.ppermute(i2b, "head", inner)
    n2, i2 = [n2a, n2b], [i2a, i2b]
    p2 = project(2, "project_2", [p3])
    s2a, n3a = turn(0, [])
    i3a, n3a = lax.ppermute(s2a, "head", inner), lax.ppermute(n3a, "head", neighbours)
    p1 = project(1, "project_1", [s2a])
    p0 = project(0, "project_0", [p1])
    base = back_project([1], "back_1", [g1], base, [p0])
    s2b, n3b = turn(1, [base])
    i3b, n3b = lax.ppermute(s2b, "head", inner), lax.ppermute(n3b, "head", neighbours)
    n3, i3 = [n3a, n3b], [i3a, i3b]
    (g2,) = kernel(ends_body, "pick", [], [coef, n2a, i2a, n2b, i2b], [part], [s2b])
    base = back_project([2], "back_2", [g2], base)
    (w3,) = kernel(functools.partial(block_body, 3), "block", [info], [w], [like((feats, width), BF16)], [base])
    s1a, s3a = turn_again(0, [w3])
    n4a = lax.ppermute(s1a, "head", neighbours)
    ag_ins = [g3_inner, base, normed_f, inv, q]
    aga, states = kernel(
        functools.partial(att_grad_first_body, rows[0]), "attended_grads", [], [coef, cin, w3, n3a, *ag_ins],
        [like((tok // 2, feats), BF16), like((heads, DH, DH), F32)], [s1a],
    )
    s3a, _ = lax.optimization_barrier((s3a, aga))
    i4a = lax.ppermute(s3a, "head", inner)
    half_f = like((tok // 2, feats), F32)
    qga, kga, vga = kernel(
        functools.partial(first_grads_body, rows[0]), "first_grads", [],
        [low, low_t, coef, cin, q, k, v, aga, own, other], [like((tok // 2, feats), BF16), half_f, half_f],
    )
    ag, gsend, gkeep = kernel(
        functools.partial(att_grad_second_body, rows[1]), "attended_grads", [],
        [states, coef, cin, w3, n3b, *ag_ins], [like((tok // 2, feats), BF16), state, state], [qga],
    )
    ggot, gtotal = pair_total(gsend, gkeep, coefb)
    s1b, s3b = turn_again(1, [gsend])
    n4b, i4b = lax.ppermute(s1b, "head", neighbours), lax.ppermute(s3b, "head", inner)
    kp, vp = kernel(
        functools.partial(key_value_body, rows[1]), "key_value_grads", [],
        [low_t, q, k, v, ag, kga, vga], [wide_f, wide_f], [gtotal],
    )
    grads = []

    def beside_second(sent):
        query_grad, mark = kernel(
            functools.partial(query_grad_body, rows[1]), "query_grad", [],
            [low, coef, cin, k, v, ag, own, other, qga], [wide_b, like((8, DH), F32)], [sent],
        )
        grads.append(query_grad)
        return [mark]

    leaving, leaving_other = exchange(gtotal, gkeep, ggot, coefb, False, [lambda _: [kp], beside_second])
    (query_grad,) = grads
    mixed, mark = mix_half(0, p0, [n4a, i4a], [leaving])
    key_grad, value_grad, mark = kernel(
        last_body, "last_grads", [], [coef, cout, k, v, leaving, leaving_other, kp, vp],
        [wide_b, wide_b, like((8, DH), F32)], [mark], hbm_outs=2,
        scratch=[pltpu.VMEM((tok, feats), BF16)] * 2 + [pltpu.SemaphoreType.DMA((2, feats // TILE))],
    )
    mixed = mix_half(1, p0, [n4b, i4b], [mark], mixed)
    return mixed, query_grad, key_grad, value_grad


def solution(mesh):
    return jax.shard_map(
        shards,
        mesh=mesh,
        in_specs=(
            P("ctx", "head"),
            P("ctx", "head"),
            P("ctx", "head"),
            P(),
            P("head", None),
            P("ctx", "head"),
        ),
        out_specs=(P("ctx", "head"), P("ctx", "head"), P("ctx", "head"), P("ctx", "head")),
        check_vma=False,
    )
```
